32 devices in a mesh: freq: 4 (over z), sub: 8 (over y, x, core).
Axes of the slice: x: 2, y: 2, z: 4, core: 2. Of those that a mesh axis runs over, the one named last changes fastest.
Arguments:
- sources: float32 [8, 4, 64, 64, 256], P('freq', None, 'sub'), may hold values from -5 to 5
- slowness: float32 [64, 64, 256], P('sub'), may hold values from 0.6 to 1.6
- freq_index: int32 [8], P('freq'), may hold values from 0 to 15
- coverage: int32 [4, 8, 8], P('freq'), may hold values from 0 to 63, as said below
Outputs:
- precond_gradient: float32 [64, 64, 256], P('sub', 'freq')
- delivered: float32 [4, 8, 8, 16, 256], P('freq', 'sub')
The draws below stay inside these ranges and needn't reach their ends.
Inputs may be any that keep to these rules, and one draw needn't show every extreme that they name: `coverage`: each list names 8 distinct tiles of its depth band; a list names exactly 2 tiles of each owner it names and none of the others, so at most 2 of any one owner.
All inputs are finite; a program needn't handle non-finite values.
Results may differ from the reference program's by a relative error of at most 0.00002.
Values sent between devices are 32-bit elements; how exact they have to be, the bound alone decides.
No kernel may reach another device: no remote copies, remote signals or barrier semaphores. Data moves between devices by JAX's collectives and lax.ppermute only.
A program may use at most 128 MiB of HBM per device.

```python
import math
import jax
import jax.numpy as jnp
from jax import lax

CX = 8
NZ = 64
NY = 256
PASSES = 4
TPD = 8
CAP = 2
FREQS = 8
NX = 64
TROWS = 16
KF = 8
N_FREQ = 4
N_SUB = 8


def draw_sources(key, part):
    shape = (FREQS, 4, NX, NZ, NY)
    return jnp.clip(jax.random.normal(key, shape, jnp.float32), -5.0, 5.0)


def draw_coverage(key, part):
    total_lists = N_FREQ * N_SUB
    picked = N_SUB // 2
    list_keys = jax.random.split(jax.random.fold_in(key, 11), total_lists)

    def one_list(list_key, list_id):
        owner_key, tile_key, shuffle_key = jax.random.split(list_key, 3)
        owners_all = jnp.arange(N_SUB, dtype=jnp.int32)
        owner_score = jax.random.randint(owner_key, (N_SUB,), 0, 1 << 20) * N_SUB + owners_all
        forced = (list_id == 0) & ((owners_all == 0) | (owners_all == N_SUB - 1))
        owner_score = jnp.where(forced, -1 - owners_all, owner_score)
        owners = jnp.argsort(owner_score, stable=True)[:picked].astype(jnp.int32)
        tiles_all = jnp.arange(TPD, dtype=jnp.int32)
        tile_score = jax.random.randint(tile_key, (picked, TPD), 0, 1 << 20) * TPD + tiles_all[None, :]
        first_low = (owners[:, None] == 0) & (tiles_all[None, :] == 0)
        last_high = (owners[:, None] == N_SUB - 1) & (tiles_all[None, :] == TPD - 1)
        tile_force = (list_id == 0) & (first_low | last_high)
        tile_score = jnp.where(tile_force, -1, tile_score)
        chosen = jnp.argsort(tile_score, axis=1, stable=True)[:, :CAP].astype(jnp.int32)
        numbers = (owners[:, None] * TPD + chosen).reshape(-1)
        shuffle = jax.random.permutation(shuffle_key, KF)
        return numbers[shuffle]
    lists = jax.vmap(one_list)(list_keys, jnp.arange(total_lists, dtype=jnp.int32))
    return lists.reshape(N_FREQ, N_SUB, KF)


def touch_ends(array, stream_key, low, high):
    shape = array.shape
    place = [jax.random.randint(jax.random.fold_in(stream_key, axis), (), 0, shape[axis]) for axis in range(len(shape))]
    array = array.at[tuple(place)].set(low)
    longest = shape.index(max(shape))
    place[longest] = (place[longest] + 1) % shape[longest]
    return array.at[tuple(place)].set(high)


def steps_of(rng, dims, cuts, smallest, top_value):
    gain, own = 1.0, jax.random.fold_in(rng, 6)
    for dim, shards_of in cuts:
        draws = jnp.exp(jax.random.uniform(jax.random.fold_in(own, dim), (shards_of,), jnp.float32, smallest / len(cuts), top_value / len(cuts)))
        gain = gain * jnp.repeat(draws, dims[dim] // shards_of).reshape([-1 if axis == dim else 1 for axis in range(len(dims))])
    return gain


def setup_inputs(seed: int = 0) -> dict:
    streams_of = jax.random.split(jax.random.key(seed), 5)
    sources = draw_sources(jax.random.fold_in(streams_of[4], 71), 0)
    slowness = jnp.clip(jnp.exp(math.log(1.6) - 0.98082923 * jax.random.uniform(streams_of[1], (NX, NZ, NY), jnp.float32) ** steps_of(streams_of[1], (NX, NZ, NY), ((0, 8),), -0.2, 0.2)), 0.6, 1.6)
    freq_index = touch_ends(jax.random.randint(streams_of[2], (FREQS,), 0, 16), jax.random.fold_in(streams_of[2], 1), 0, 15).astype(jnp.int32)
    coverage = draw_coverage(jax.random.fold_in(streams_of[4], 71), 0)
    return {"sources": sources, "slowness": slowness, "freq_index": freq_index, "coverage": coverage}


def smooth_axis(values, axis):
    widths = [(0, 0)] * values.ndim
    widths[axis] = (1, 1)
    padded = jnp.pad(values, widths)
    length = values.shape[axis]
    before = lax.slice_in_dim(padded, 0, length, axis=axis)
    middle = lax.slice_in_dim(padded, 1, length + 1, axis=axis)
    after = lax.slice_in_dim(padded, 2, length + 2, axis=axis)
    return 0.25 * before + 0.5 * middle + 0.25 * after

def smooth_all(values):
    first = smooth_axis(values, values.ndim - 3)
    second = smooth_axis(first, values.ndim - 2)
    return smooth_axis(second, values.ndim - 1)

def one_frequency(forcing, weight, slowness):
    sigma_cells = 0.12 * weight * slowness
    diag_real = 0.875 - sigma_cells
    diag_imag = sigma_cells
    diag_norm = diag_real * diag_real + diag_imag * diag_imag
    force_real = forcing[0::2]
    force_imag = forcing[1::2]
    real_part = jnp.zeros(force_real.shape, jnp.float32)
    imag_part = jnp.zeros(force_real.shape, jnp.float32)
    for step in range(PASSES):
        applied_real = real_part - sigma_cells * (real_part + imag_part) - smooth_all(real_part)
        applied_imag = imag_part - sigma_cells * (imag_part - real_part) - smooth_all(imag_part)
        resid_real = force_real - applied_real
        resid_imag = force_imag - applied_imag
        real_part = real_part + (resid_real * diag_real + resid_imag * diag_imag) / diag_norm
        imag_part = imag_part + (resid_imag * diag_real - resid_real * diag_imag) / diag_norm
    grad_term = weight * (real_part[0] * real_part[1] - imag_part[0] * imag_part[1])
    illum_term = weight * (real_part[0] * real_part[0] + imag_part[0] * imag_part[0])
    return (grad_term, illum_term)

def reference(sources, slowness, freq_index, coverage):
    weights = 1.0 + freq_index.astype(jnp.float32) / 16.0
    terms = lax.map(lambda pair: one_frequency(pair[0], pair[1], slowness), (sources, weights))
    gradient = lax.optimization_barrier(jnp.sum(terms[0], axis=0))
    illum = lax.optimization_barrier(jnp.sum(terms[1], axis=0))
    precond = gradient / jnp.sqrt(illum + 1.0)
    depth = NZ // N_FREQ
    tiles = precond.reshape(N_SUB, CX, N_FREQ, depth, NY).transpose(2, 0, 1, 3, 4)
    tiles = tiles.reshape(N_FREQ, N_SUB * TPD, TROWS, NY)
    group_ids = jnp.arange(N_FREQ, dtype=jnp.int32)[:, None, None]
    delivered = tiles[group_ids, coverage]
    return (precond, delivered)
```

```python
import functools

import jax
import jax.numpy as jnp
from jax import lax
from jax.experimental import pallas as pl
from jax.experimental.pallas import tpu as pltpu
from jax.sharding import PartitionSpec as P

TPD = 8
CAP = 2
HALF = 128
VMEM_LIMIT = 48 * 1024 * 1024


def masks():
    lane = lax.broadcasted_iota(jnp.int32, (8, HALF), 1)
    row = lax.broadcasted_iota(jnp.int32, (8, HALF), 0)
    return lane == 0, lane == HALF - 1, row == 0, row == 7


def load_rows(refs, index, nk):
    return [[ref[index + (pl.ds(k, 8, stride=nk), slice(None))] for k in range(nk)] for ref in refs]


def load_plane(ref, index, nk):
    return [[ref[index + (h, pl.ds(8 * k, 8), slice(None))] for k in range(nk)] for h in range(2)]


def store_plane(ref, index, plane):
    for h, pieces in enumerate(plane):
        for k, piece in enumerate(pieces):
            ref[index + (h, pl.ds(8 * k, 8), slice(None))] = piece


def smooth(before, middle, after, marks):
    lane_first, lane_last, row_first, row_last = marks
    nk = len(middle[0])
    depth = []
    for h in range(2):
        across = [
            (before[h][k] + after[h][k]) + (middle[h][k] + middle[h][k]) for k in range(nk)
        ]
        below = jnp.where(row_last, 0.0, pltpu.roll(across[0], 7, 0))
        above = jnp.where(row_first, 0.0, pltpu.roll(across[-1], 1, 0))
        pairs = [across[k] + across[k + 1] for k in range(nk - 1)] + [across[-1] + below]
        depth.append([above + across[0] + pairs[0]] + [pairs[k - 1] + pairs[k] for k in range(1, nk)])
    out = [[], []]
    for k in range(nk):
        left, right = depth[0][k], depth[1][k]
        left_up, right_up = pltpu.roll(left, HALF - 1, 1), pltpu.roll(right, HALF - 1, 1)
        left_pair = left + jnp.where(lane_last, right_up, left_up)
        right_pair = right + jnp.where(lane_last, 0.0, right_up)
        left_down, right_down = pltpu.roll(left_pair, 1, 1), pltpu.roll(right_pair, 1, 1)
        out[0].append(left_pair + jnp.where(lane_first, left, left_down))
        out[1].append(right_pair + jnp.where(lane_first, left_down, right_down))
    return out


def turn(real, imag, coef_real, coef_imag):
    new_real = [
        [r * e + i * f for r, i, e, f in zip(*parts)] for parts in zip(real, imag, coef_real, coef_imag)
    ]
    new_imag = [
        [i * e - r * f for r, i, e, f in zip(*parts)] for parts in zip(real, imag, coef_real, coef_imag)
    ]
    return new_real, new_imag


def forced(forcing, smoothed, middle):
    return [
        [s + (v - 8.0 * m) for s, v, m in zip(*parts)] for parts in zip(forcing, smoothed, middle)
    ]


def coefficients(slow, scale, factor):
    coef_real, coef_imag = [], []
    for pieces in slow:
        for out in (coef_real, coef_imag):
            out.append([])
        for piece in pieces:
            sigma = scale * piece
            diag = 0.875 - sigma
            inverse = factor / (diag * diag + sigma * sigma)
            coef_real[-1].append(diag * inverse)
            coef_imag[-1].append(sigma * inverse)
    return coef_real, coef_imag


def relax(forcing, before, middle, after, coef, marks):
    terms = [
        forced(forcing(c), smooth(before(c), middle(c), after(c), marks), middle(c)) for c in range(2)
    ]
    return turn(terms[0], terms[1], coef(0), coef(1))


def products(forward, adjoint, weight):
    (fr, fi), (ar, ai) = forward, adjoint
    grad = [
        [weight * (a * c - b * d) for a, b, c, d in zip(*parts)] for parts in zip(fr, fi, ar, ai)
    ]
    illum = [[weight * (a * a + b * b) for a, b in zip(*parts)] for parts in zip(fr, fi)]
    return grad, illum


def accumulate(acc, side, terms, nk, first):
    for number, plane in enumerate(terms):
        for h, pieces in enumerate(plane):
            for k, piece in enumerate(pieces):
                place = (number, side, h, pl.ds(k, 8, stride=nk), slice(None))
                acc[place] = jnp.where(first, piece, acc[place] + piece)


def write_out(out, acc):
    bands, _, _, depth, _ = out.shape
    for band in range(bands):
        for number in range(2):
            for side in range(2):
                for h in range(2):
                    out[band, number, side, :, pl.ds(h * HALF, HALF)] = acc[
                        number, side, h, pl.ds(band * depth, depth), :
                    ]


def interior_kernel(params, src_l, src_r, slow_l, slow_r, two, three, out, coef, one, last, acc):
    group, pair = pl.program_id(0), pl.program_id(1)
    groups = pl.num_programs(0)
    layers, rows = src_l.shape[2], src_l.shape[3]
    nk = rows // 8
    marks = masks()
    scale, weight = params[0, group], params[1, group]

    @pl.when(pair == 0)
    def _():
        @pl.loop(0, layers)
        def _(layer):
            planes = coefficients(load_rows((slow_l, slow_r), (layer,), nk), scale, 1.0 / 64.0)
            for c in range(2):
                store_plane(coef, (c, layer), planes[c])

    def source(layer):
        return lambda c: load_rows((src_l, src_r), (0, c, layer), nk)

    def factor(layer):
        return lambda c: load_plane(coef, (c, layer), nk)

    @pl.loop(0, layers)
    def _(layer):
        force, scaled = source(layer), factor(layer)
        planes = turn(force(0), force(1), scaled(0), scaled(1))
        for c in range(2):
            store_plane(one, (layer, c), planes[c])

    @pl.loop(1, layers - 1)
    def _(layer):
        near = [lambda c, at=at: load_plane(one, (at, c), nk) for at in (layer - 1, layer, layer + 1)]
        planes = relax(source(layer), *near, factor(layer), marks)
        for c in range(2):
            store_plane(two, (0, 0, layer - 1, c), planes[c])

    @pl.loop(2, layers - 2)
    def _(layer):
        near = [
            lambda c, at=at: load_plane(two, (0, 0, at, c), nk) for at in (layer - 2, layer - 1, layer)
        ]
        planes = relax(source(layer), *near, factor(layer), marks)
        for c in range(2):
            store_plane(three, (0, 0, layer - 2, c), planes[c])

    for side in range(2):
        layer = 3 + side
        near = [
            lambda c, at=at: load_plane(three, (0, 0, at, c), nk)
            for at in (layer - 3, layer - 2, layer - 1)
        ]
        planes = relax(source(layer), *near, factor(layer), marks)
        finish(planes, side, last, acc, group, pair, weight, nk)

    @pl.when((group == groups - 1) & (pair == 1))
    def _():
        write_out(out, acc)


def finish(planes, side, last, acc, group, pair, weight, nk):
    @pl.when(pair == 0)
    def _():
        for c in range(2):
            store_plane(last, (side, c), planes[c])

    @pl.when(pair == 1)
    def _():
        forward = [load_plane(last, (side, c), nk) for c in range(2)]
        accumulate(acc, side, products(forward, planes, weight), nk, group == 0)


def stage_kernel(depth_in, keep, params, *refs):
    refs = list(refs)

    def take(count):
        taken = refs[:count]
        del refs[:count]
        return taken

    sides = []
    for _ in range(2):
        source = [take(2) for _ in range(4)]
        slow = [take(2) for _ in range(4)]
        sides.append((source, slow, take(4)))
    out = take(1)[0]
    if keep:
        new_two, new_three = take(2)
    coef, one, fresh, last, acc = take(5)
    group, pair = pl.program_id(0), pl.program_id(1)
    groups = pl.num_programs(0)
    rows = sides[0][1][3][0].shape[-2]
    nk = rows // 8
    marks = masks()
    scale, weight = params[0, group], params[1, group]

    for side, (source, slow, (two_near, two_far, three_near, three_far)) in enumerate(sides):
        inside = params[2, side]

        def pick(ref, c):
            return (c,) if len(ref.shape) == 3 else (0, c, 0)

        def force(at):
            return lambda c: load_rows(source[at], pick(source[at][0], c), nk)

        def factor(at):
            return lambda c: load_plane(coef, (side, at, c), nk)

        @pl.when(pair == 0)
        def _():
            for at in range(4):
                amount = inside / 64.0 if at < depth_in else 1.0 / 64.0
                planes = coefficients(load_rows(slow[at], (0,), nk), scale, amount)
                for c in range(2):
                    store_plane(coef, (side, at, c), planes[c])

        for at in range(3):
            planes = turn(force(at)(0), force(at)(1), factor(at)(0), factor(at)(1))
            for c in range(2):
                store_plane(one, (side, at, c), planes[c])

        def first(at):
            return lambda c: load_plane(one, (side, at, c), nk)

        def held(ref):
            return lambda c: load_plane(ref, (0, 0, 0, c), nk)

        def made(level):
            return lambda c: load_plane(fresh, (side, level, c), nk)

        two = relax(force(1), first(0), first(1), first(2), factor(1), marks)
        for c in range(2):
            store_plane(fresh, (side, 0, c), two[c])
            if keep:
                store_plane(new_two, (0, 0, side, c), two[c])
        three = relax(force(2), made(0), held(two_near), held(two_far), factor(2), marks)
        for c in range(2):
            store_plane(fresh, (side, 1, c), three[c])
            if keep:
                store_plane(new_three, (0, 0, side, c), three[c])
        four = relax(force(3), made(1), held(three_near), held(three_far), factor(3), marks)
        finish(four, side, last, acc, group, pair, weight, nk)

    @pl.when((group == groups - 1) & (pair == 1))
    def _():
        write_out(out, acc)


def precond_kernel(pick, *refs):
    chunks, (precond, outgoing) = refs[:-2], refs[-2:]
    layers = precond.shape[0]
    for step, chunk in enumerate(chunks):
        for side in range(2):
            layer = layers // 2 - 1 - step if side == 0 else layers // 2 + step
            grad = chunk[0, 0, side]
            illum = chunk[0, 1, side]
            for other in range(1, chunk.shape[0]):
                grad = grad + chunk[other, 0, side]
                illum = illum + chunk[other, 1, side]
            precond[layer] = grad / jnp.sqrt(illum + 1.0)

    @pl.loop(0, outgoing.shape[0])
    def _(slot):
        outgoing[slot] = precond[pick[slot]]


def deliver_kernel(slots, incoming, out):
    @pl.loop(0, out.shape[2])
    def _(number):
        out[0, 0, number] = incoming[slots[number]]


def smem():
    return pl.BlockSpec(memory_space=pltpu.SMEM)


def vmem():
    return pl.BlockSpec(memory_space=pltpu.VMEM)


def plane_scratch(*lead, rows):
    return pltpu.VMEM(lead + (2, rows, HALF), jnp.float32)


def compiler_params(**more):
    return pltpu.CompilerParams(vmem_limit_bytes=VMEM_LIMIT, **more)


def interior(params, sources, slowness, bands):
    groups, _, layers, rows, columns = sources.shape
    half = [
        pl.BlockSpec((1, 2, layers, rows, HALF), lambda g, p, h=h: (g, p, 0, 0, h)) for h in range(2)
    ]
    slow = [pl.BlockSpec((layers, rows, HALF), lambda g, p, h=h: (0, 0, h)) for h in range(2)]

    def state(count):
        return (
            jax.ShapeDtypeStruct((groups, 2, count, 2, 2, rows, HALF), jnp.float32),
            pl.BlockSpec((1, 1, count, 2, 2, rows, HALF), lambda g, p: (g, p, 0, 0, 0, 0, 0)),
        )

    chunk = (bands, 2, 2, rows // bands, columns)
    shapes = [state(layers - 2), state(layers - 4)]
    return pl.pallas_call(
        interior_kernel,
        grid=(groups, 2),
        in_specs=[smem()] + half + slow,
        out_specs=[s[1] for s in shapes] + [pl.BlockSpec(chunk, lambda g, p: (0,) * 5)],
        out_shape=[s[0] for s in shapes] + [jax.ShapeDtypeStruct(chunk, jnp.float32)],
        scratch_shapes=[
            plane_scratch(2, layers, rows=rows),
            plane_scratch(layers, 2, rows=rows),
            plane_scratch(2, 2, rows=rows),
            plane_scratch(2, 2, rows=rows),
        ],
        compiler_params=compiler_params(),
        cost_estimate=pl.CostEstimate(flops=400_000_000, bytes_accessed=10_000_000, transcendentals=0),
        name="interior",
    )(params, sources, sources, slowness, slowness)


def stage(depth_in, params, sources, slowness, halos, held, bands, keep):
    groups, _, layers, rows, columns = sources.shape
    operands, specs = [params], [smem()]

    def add(array, block, index):
        operands.append(array)
        specs.append(pl.BlockSpec(block, index))

    for side in range(2):
        for what in range(2):
            for at in range(4):
                layer = at - depth_in
                for h in range(2):
                    if layer < 0:
                        halo = halos[-layer - 1][side]
                        if what == 0:
                            add(halo, (2, rows, HALF), lambda g, p, h=h: (2 * g + p, 0, h))
                        else:
                            add(halo, (1, rows, HALF), lambda g, p, h=h: (4 * groups, 0, h))
                        continue
                    own = layer if side == 0 else layers - 1 - layer
                    if what == 0:
                        add(
                            sources,
                            (1, 2, 1, rows, HALF),
                            lambda g, p, h=h, own=own: (g, p, own, 0, h),
                        )
                    else:
                        add(slowness, (1, rows, HALF), lambda g, p, h=h, own=own: (own, 0, h))
        for array, places in held:
            add(
                array,
                (1, 1, 1, 2, 2, rows, HALF),
                lambda g, p, at=places[side]: (g, p, at, 0, 0, 0, 0),
            )
    chunk = (bands, 2, 2, rows // bands, columns)
    out_shape = [jax.ShapeDtypeStruct(chunk, jnp.float32)]
    out_specs = [pl.BlockSpec(chunk, lambda g, p: (0,) * 5)]
    if keep:
        for _ in range(2):
            out_shape.append(jax.ShapeDtypeStruct((groups, 2, 2, 2, 2, rows, HALF), jnp.float32))
            out_specs.append(
                pl.BlockSpec((1, 1, 2, 2, 2, rows, HALF), lambda g, p: (g, p, 0, 0, 0, 0, 0))
            )
    return pl.pallas_call(
        functools.partial(stage_kernel, depth_in, keep),
        grid=(groups, 2),
        in_specs=specs,
        out_specs=out_specs,
        out_shape=out_shape,
        scratch_shapes=[
            plane_scratch(2, 4, 2, rows=rows),
            plane_scratch(2, 3, 2, rows=rows),
            plane_scratch(2, 2, 2, rows=rows),
            plane_scratch(2, 2, rows=rows),
            plane_scratch(2, 2, rows=rows),
        ],
        compiler_params=compiler_params(),
        cost_estimate=pl.CostEstimate(flops=100_000_000, bytes_accessed=8_000_000, transcendentals=0),
        name=f"stage{depth_in}",
    )(*operands)


def route(coverage, own_index):
    lists = coverage[0]
    owner, local = lists // TPD, lists % TPD
    position = jnp.arange(lists.shape[1], dtype=jnp.int32)
    same_owner = owner[:, :, None] == owner[:, None, :]
    earlier = position[None, :] < position[:, None]
    rank = jnp.sum((same_owner & earlier[None]).astype(jnp.int32), axis=2)
    slots = jnp.arange(CAP, dtype=jnp.int32)
    hit = (owner == own_index)[:, :, None] & (rank[:, :, None] == slots[None, None, :])
    pick = jnp.sum(jnp.where(hit, local[:, :, None], 0), axis=1).reshape(-1)
    own_slots = owner * CAP + rank
    return pick, lax.dynamic_index_in_dim(own_slots, own_index, 0, keepdims=False)


def body(sources, slowness, freq_index, coverage):
    groups, _, layers, rows, columns = sources.shape
    bands, members = lax.axis_size("freq"), lax.axis_size("sub")
    own_index = lax.axis_index("sub")
    weights = 1.0 + freq_index.astype(jnp.float32) / 16.0
    inside = jnp.stack([own_index > 0, own_index < members - 1]).astype(jnp.float32)
    params = jnp.stack([0.12 * weights, 4096.0 * weights, inside])
    up = [(i, i + 1) for i in range(members - 1)]
    down = [(j, i) for i, j in up]

    def edge(layer):
        part = lax.slice_in_dim(sources, layer, layer + 1, axis=2).reshape(4 * groups, rows, columns)
        return jnp.concatenate([part, slowness[layer : layer + 1]], axis=0)

    halos = []
    for depth_in in range(1, 4):
        halos.append(
            (
                lax.ppermute(edge(layers - depth_in), "sub", up),
                lax.ppermute(edge(depth_in - 1), "sub", down),
            )
        )
    pick, slots = route(coverage, own_index)

    def spread(chunk):
        return lax.all_to_all(chunk, "freq", split_axis=0, concat_axis=0, tiled=True)

    two, three, chunk = interior(params, sources, slowness, bands)
    chunks = [spread(chunk)]
    twos = [(two, (1, layers - 4)), (two, (0, layers - 3))]
    threes = [(three, (1, layers - 6)), (three, (0, layers - 5))]
    for depth_in in range(1, 4):
        keep = depth_in < 3
        held = [twos[-1], twos[-2], threes[-1], threes[-2]]
        outs = stage(depth_in, params, sources, slowness, halos, held, bands, keep)
        chunks.append(spread(outs[0]))
        if keep:
            twos.append((outs[1], (0, 1)))
            threes.append((outs[2], (0, 1)))
    depth = rows // bands
    precond, outgoing = pl.pallas_call(
        precond_kernel,
        in_specs=[smem()] + [vmem()] * 4,
        out_specs=[vmem()] * 2,
        out_shape=[
            jax.ShapeDtypeStruct((layers, depth, columns), jnp.float32),
            jax.ShapeDtypeStruct((members * CAP, depth, columns), jnp.float32),
        ],
        compiler_params=compiler_params(),
        name="precond",
    )(pick, *chunks)
    incoming = lax.all_to_all(outgoing, "sub", split_axis=0, concat_axis=0, tiled=True)
    delivered = pl.pallas_call(
        deliver_kernel,
        in_specs=[smem(), vmem()],
        out_specs=vmem(),
        out_shape=jax.ShapeDtypeStruct((1, 1, coverage.shape[2], depth, columns), jnp.float32),
        compiler_params=compiler_params(),
        name="deliver",
    )(slots, incoming)
    return precond, delivered


def solution(mesh):
    placed = (
        P("freq", None, "sub", None, None),
        P("sub", None, None),
        P("freq"),
        P("freq", None, None),
    )
    return jax.shard_map(
        body,
        mesh=mesh,
        in_specs=placed,
        out_specs=(P("sub", "freq", None), P("freq", "sub", None, None, None)),
        check_vma=False,
    )
```

```python
import functools

import jax
import jax.numpy as jnp
from jax import lax
from jax.experimental import pallas as pl
from jax.experimental.pallas import tpu as pltpu
from jax.sharding import PartitionSpec as P

TPD = 8
CAP = 2
HALF = 128


def masks():
    lane = lax.broadcasted_iota(jnp.int32, (8, HALF), 1)
    row = lax.broadcasted_iota(jnp.int32, (8, HALF), 0)
    return lane == 0, lane == HALF - 1, row == 0, row == 7


def load_rows(refs, index, nk):
    return [[ref[index + (pl.ds(k, 8, stride=nk), slice(None))] for k in range(nk)] for ref in refs]


def load_plane(ref, index, nk):
    return [[ref[index + (h, pl.ds(8 * k, 8), slice(None))] for k in range(nk)] for h in range(2)]


def store_plane(ref, index, plane):
    for h, pieces in enumerate(plane):
        for k, piece in enumerate(pieces):
            ref[index + (h, pl.ds(8 * k, 8), slice(None))] = piece


def smooth(before, middle, after, marks):
    lane_first, lane_last, row_first, row_last = marks
    nk = len(middle[0])
    depth = []
    for h in range(2):
        across = [
            (before[h][k] + after[h][k]) + (middle[h][k] + middle[h][k]) for k in range(nk)
        ]
        below = jnp.where(row_last, 0.0, pltpu.roll(across[0], 7, 0))
        above = jnp.where(row_first, 0.0, pltpu.roll(across[-1], 1, 0))
        pairs = [across[k] + across[k + 1] for k in range(nk - 1)] + [across[-1] + below]
        depth.append([above + across[0] + pairs[0]] + [pairs[k - 1] + pairs[k] for k in range(1, nk)])
    out = [[], []]
    for k in range(nk):
        left, right = depth[0][k], depth[1][k]
        left_up, right_up = pltpu.roll(left, HALF - 1, 1), pltpu.roll(right, HALF - 1, 1)
        left_pair = left + jnp.where(lane_last, right_up, left_up)
        right_pair = right + jnp.where(lane_last, 0.0, right_up)
        left_down, right_down = pltpu.roll(left_pair, 1, 1), pltpu.roll(right_pair, 1, 1)
        out[0].append(left_pair + jnp.where(lane_first, left, left_down))
        out[1].append(right_pair + jnp.where(lane_first, left_down, right_down))
    return out


def turn(real, imag, coef_real, coef_imag):
    new_real = [
        [r * e + i * f for r, i, e, f in zip(*parts)] for parts in zip(real, imag, coef_real, coef_imag)
    ]
    new_imag = [
        [i * e - r * f for r, i, e, f in zip(*parts)] for parts in zip(real, imag, coef_real, coef_imag)
    ]
    return new_real, new_imag


def forced(forcing, smoothed, middle):
    return [
        [s + (v - 8.0 * m) for s, v, m in zip(*parts)] for parts in zip(forcing, smoothed, middle)
    ]


def coefficients(slow, scale, factor):
    coef_real, coef_imag = [], []
    for pieces in slow:
        for out in (coef_real, coef_imag):
            out.append([])
        for piece in pieces:
            sigma = scale * piece
            diag = 0.875 - sigma
            inverse = factor / (diag * diag + sigma * sigma)
            coef_real[-1].append(diag * inverse)
            coef_imag[-1].append(sigma * inverse)
    return coef_real, coef_imag


def relax(forcing, before, middle, after, coef, marks):
    terms = [
        forced(forcing(c), smooth(before(c), middle(c), after(c), marks), middle(c)) for c in range(2)
    ]
    return turn(terms[0], terms[1], coef(0), coef(1))


def products(forward, adjoint, weight):
    (fr, fi), (ar, ai) = forward, adjoint
    grad = [
        [weight * (a * c - b * d) for a, b, c, d in zip(*parts)] for parts in zip(fr, fi, ar, ai)
    ]
    illum = [[weight * (a * a + b * b) for a, b in zip(*parts)] for parts in zip(fr, fi)]
    return grad, illum


def accumulate(acc, side, terms, nk, first):
    for number, plane in enumerate(terms):
        for h, pieces in enumerate(plane):
            for k, piece in enumerate(pieces):
                place = (number, side, h, pl.ds(k, 8, stride=nk), slice(None))
                acc[place] = jnp.where(first, piece, acc[place] + piece)


def write_out(out, acc):
    bands, _, _, depth, _ = out.shape
    for band in range(bands):
        for number in range(2):
            for side in range(2):
                for h in range(2):
                    out[band, number, side, :, pl.ds(h * HALF, HALF)] = acc[
                        number, side, h, pl.ds(band * depth, depth), :
                    ]


def interior_kernel(
    params, sources, slowness, force, one, two, three, coef, out, raw, slow, last, acc, sems
):
    groups, layers, rows = sources.shape[0], sources.shape[2], sources.shape[3]
    nk = rows // 8
    marks = masks()
    copies = []
    for h in range(2):
        lanes = pl.ds(h * HALF, HALF)
        copies.append(
            pltpu.make_async_copy(slowness.at[:, :, lanes], slow.at[h], sems.at[2 * groups, h])
        )
    for item in range(2 * groups):
        for h in range(2):
            lanes = pl.ds(h * HALF, HALF)
            copies.append(
                pltpu.make_async_copy(
                    sources.at[item // 2, pl.ds(2 * (item % 2), 2), :, :, lanes],
                    raw.at[item, h],
                    sems.at[item, h],
                )
            )
    for copy in copies:
        copy.start()
    for copy in copies[:2]:
        copy.wait()

    @pl.loop(0, groups)
    def _(group):
        scale = params[0, group]

        @pl.loop(0, layers)
        def _(layer):
            pieces = load_rows((slow.at[0], slow.at[1]), (layer,), nk)
            planes = coefficients(pieces, scale, 1.0 / 64.0)
            for c in range(2):
                store_plane(coef, (group, layer, c), planes[c])

    @pl.loop(0, 2 * groups)
    def _(item):
        group, pair = item // 2, item % 2
        for h in range(2):
            lanes = pl.ds(h * HALF, HALF)
            pltpu.make_async_copy(
                sources.at[group, pl.ds(2 * pair, 2), :, :, lanes], raw.at[item, h], sems.at[item, h]
            ).wait()

        def factor(layer):
            return lambda c: load_plane(coef, (group, layer, c), nk)

        def held(ref, at):
            return lambda c: load_plane(ref, (group, pair, at, c), nk)

        @pl.loop(0, layers)
        def _(layer):
            planes = []
            for c in range(2):
                planes.append(load_rows((raw.at[item, 0], raw.at[item, 1]), (c, layer), nk))
                store_plane(force, (group, pair, layer, c), planes[c])
            planes = turn(planes[0], planes[1], factor(layer)(0), factor(layer)(1))
            for c in range(2):
                store_plane(one, (group, pair, layer, c), planes[c])

        def step(layer, ref):
            at = (layer, 0 if ref is one else 1 if ref is two else 2)
            near = [held(ref, at[0] + shift - at[1]) for shift in (-1, 0, 1)]
            return relax(held(force, layer), *near, factor(layer), marks)

        @pl.loop(1, layers - 1)
        def _(layer):
            planes = step(layer, one)
            for c in range(2):
                store_plane(two, (group, pair, layer - 1, c), planes[c])

        @pl.loop(2, layers - 2)
        def _(layer):
            planes = step(layer, two)
            for c in range(2):
                store_plane(three, (group, pair, layer - 2, c), planes[c])

        @pl.loop(0, 2)
        def _(side):
            finish(step(layers // 2 - 1 + side, three), side, last, acc, group, pair, params[1, group], nk)

    write_out(out, acc)


def finish(planes, side, last, acc, group, pair, weight, nk):
    @pl.when(pair == 0)
    def _():
        for c in range(2):
            store_plane(last, (side, c), planes[c])

    @pl.when(pair == 1)
    def _():
        forward = [load_plane(last, (side, c), nk) for c in range(2)]
        accumulate(acc, side, products(forward, planes, weight), nk, group == 0)


def stage_kernel(depth_in, counts, params, before, after, *refs):
    refs = list(refs)

    def take(count):
        taken = refs[:count]
        del refs[:count]
        return taken

    force, one, two, three, coef = take(5)
    earlier = [take(5) for _ in range(counts)]
    out = take(1)[0]
    new = take(5)
    raw, last, acc, sems = take(4)
    fresh = earlier + [new]
    groups, layers = force.shape[0], force.shape[2]
    rows = before.shape[1]
    nk = rows // 8
    marks = masks()
    copies = []
    for side, halo in enumerate((before, after)):
        for h in range(2):
            copies.append(
                pltpu.make_async_copy(
                    halo.at[:, :, pl.ds(h * HALF, HALF)], raw.at[side, h], sems.at[side, h]
                )
            )
    for copy in copies:
        copy.start()
    for copy in copies:
        copy.wait()

    @pl.loop(0, 2 * groups)
    def _(item):
        group, pair = item // 2, item % 2

        @pl.loop(0, 2)
        def _(side):
            halves = (raw.at[side, 0], raw.at[side, 1])

            @pl.when(pair == 0)
            def _():
                pieces = load_rows(halves, (4 * groups,), nk)
                planes = coefficients(pieces, params[0, group], params[2, side] / 64.0)
                for c in range(2):
                    store_plane(new[4], (group, side, c), planes[c])

            def own(layer, skip=0):
                return jnp.where(side == 0, layer, layers - 1 - layer) - skip

            def getter(number, whole, skip, turned):
                def at(layer):
                    if layer >= skip:
                        return lambda c: load_plane(whole, (group, pair, own(layer, skip), c), nk)
                    return lambda c: load_plane(
                        fresh[skip - layer - 1][number], (group, pair, side, c), nk
                    )

                return at

            forces = getter(0, force, 0, False)
            firsts = getter(1, one, 0, False)
            seconds = getter(2, two, 1, False)
            thirds = getter(3, three, 2, False)

            def factor(layer):
                if layer >= 0:
                    return lambda c: load_plane(coef, (group, own(layer), c), nk)
                return lambda c: load_plane(fresh[-layer - 1][4], (group, side, c), nk)

            j = depth_in
            planes = [load_rows(halves, (2 * item + c,), nk) for c in range(2)]
            for c in range(2):
                store_plane(new[0], (group, pair, side, c), planes[c])
            planes = turn(planes[0], planes[1], factor(-j)(0), factor(-j)(1))
            for c in range(2):
                store_plane(new[1], (group, pair, side, c), planes[c])
            planes = relax(forces(1 - j), *[firsts(-j + n) for n in range(3)], factor(1 - j), marks)
            for c in range(2):
                store_plane(new[2], (group, pair, side, c), planes[c])
            planes = relax(
                forces(2 - j), *[seconds(1 - j + n) for n in range(3)], factor(2 - j), marks
            )
            for c in range(2):
                store_plane(new[3], (group, pair, side, c), planes[c])
            planes = relax(
                forces(3 - j), *[thirds(2 - j + n) for n in range(3)], factor(3 - j), marks
            )
            finish(planes, side, last, acc, group, pair, params[1, group], nk)

    write_out(out, acc)


def pack_kernel(sources, slowness, *refs):
    outs, sems = refs[:-1], refs[-1]
    groups, _, layers = sources.shape[:3]
    copies = []
    for number, out in enumerate(outs):
        depth_in = number // 2 + 1
        layer = layers - depth_in if number % 2 == 0 else depth_in - 1
        for group in range(groups):
            copies.append(
                pltpu.make_async_copy(
                    sources.at[group, :, layer], out.at[pl.ds(4 * group, 4)], sems.at[number, group]
                )
            )
        copies.append(
            pltpu.make_async_copy(slowness.at[layer], out.at[4 * groups], sems.at[number, groups])
        )
    for copy in copies:
        copy.start()
    for copy in copies:
        copy.wait()


def precond_kernel(pick, *refs):
    chunks, (precond, outgoing) = refs[:-2], refs[-2:]
    layers = precond.shape[0]
    for step, chunk in enumerate(chunks):
        for side in range(2):
            layer = layers // 2 - 1 - step if side == 0 else layers // 2 + step
            grad = chunk[0, 0, side]
            illum = chunk[0, 1, side]
            for other in range(1, chunk.shape[0]):
                grad = grad + chunk[other, 0, side]
                illum = illum + chunk[other, 1, side]
            precond[layer] = grad / jnp.sqrt(illum + 1.0)

    @pl.loop(0, outgoing.shape[0])
    def _(slot):
        outgoing[slot] = precond[pick[slot]]


def deliver_kernel(slots, incoming, out):
    @pl.loop(0, out.shape[2])
    def _(number):
        out[0, 0, number] = incoming[slots[number]]


def smem():
    return pl.BlockSpec(memory_space=pltpu.SMEM)


def vmem():
    return pl.BlockSpec(memory_space=pltpu.VMEM)


def plane_scratch(*lead, rows, halves=(2,)):
    return pltpu.VMEM(lead + halves + (rows, HALF), jnp.float32)


def compiler_params(mebibytes):
    return pltpu.CompilerParams(vmem_limit_bytes=mebibytes * 1024 * 1024)


def resident(*shape):
    return pltpu.VMEM(shape, jnp.float32)


def anywhere():
    return pl.BlockSpec(memory_space=pl.ANY)


def kept(arrays):
    return [pltpu.with_memory_space_constraint(a, pltpu.VMEM) for a in arrays]


def pack(sources, slowness):
    groups, _, _, rows, columns = sources.shape
    return pl.pallas_call(
        pack_kernel,
        in_specs=[anywhere()] * 2,
        out_specs=[anywhere()] * 6,
        out_shape=[pltpu.HBM((4 * groups + 1, rows, columns), jnp.float32)] * 6,
        scratch_shapes=[pltpu.SemaphoreType.DMA((6, groups + 1))],
        compiler_params=compiler_params(2),
        name="pack",
    )(sources, slowness)


def interior(params, sources, slowness, bands):
    groups, _, layers, rows, columns = sources.shape

    def state(count):
        return resident(groups, 2, count, 2, 2, rows, HALF)

    chunk = pltpu.HBM((bands, 2, 2, rows // bands, columns), jnp.float32)
    return pl.pallas_call(
        interior_kernel,
        in_specs=[smem()] + [anywhere()] * 2,
        out_specs=[vmem()] * 6,
        out_shape=[state(layers), state(layers), state(layers - 2), state(layers - 4)]
        + [resident(groups, layers, 2, 2, rows, HALF), chunk],
        scratch_shapes=[
            plane_scratch(2 * groups, 2, 2, layers, rows=rows, halves=()),
            plane_scratch(2, layers, rows=rows, halves=()),
            plane_scratch(2, 2, rows=rows),
            plane_scratch(2, 2, rows=rows),
            pltpu.SemaphoreType.DMA((2 * groups + 1, 2)),
        ],
        compiler_params=compiler_params(8),
        cost_estimate=pl.CostEstimate(flops=400_000_000, bytes_accessed=10_000_000, transcendentals=0),
        name="interior",
    )(params, sources, slowness)


def stage(depth_in, params, halo, state, earlier, bands, columns):
    groups, _, layers, _, _, rows, _ = state[0].shape
    fresh = [resident(groups, 2, 2, 2, 2, rows, HALF)] * 4
    fresh.append(resident(groups, 2, 2, 2, rows, HALF))
    last = depth_in == 3
    out_shape = [pltpu.HBM((bands, 2, 2, rows // bands, columns), jnp.float32)]
    held = kept(list(state) + [array for arrays in earlier for array in arrays])
    return pl.pallas_call(
        functools.partial(stage_kernel, depth_in, len(earlier)),
        in_specs=[smem()] + [anywhere()] * 2 + [vmem()] * len(held),
        out_specs=[vmem()] * (1 if last else 6),
        out_shape=out_shape + ([] if last else fresh),
        scratch_shapes=(fresh if last else [])
        + [
            plane_scratch(2, 2, 4 * groups + 1, rows=rows, halves=()),
            plane_scratch(2, 2, rows=rows),
            plane_scratch(2, 2, rows=rows),
            pltpu.SemaphoreType.DMA((2, 2)),
        ],
        compiler_params=compiler_params(12 if last else 8),
        cost_estimate=pl.CostEstimate(flops=100_000_000, bytes_accessed=8_000_000, transcendentals=0),
        name=f"stage{depth_in}",
    )(params, *halo, *held)


def route(coverage, own_index):
    lists = coverage[0]
    owner, local = lists // TPD, lists % TPD
    position = jnp.arange(lists.shape[1], dtype=jnp.int32)
    same_owner = owner[:, :, None] == owner[:, None, :]
    earlier = position[None, :] < position[:, None]
    rank = jnp.sum((same_owner & earlier[None]).astype(jnp.int32), axis=2)
    slots = jnp.arange(CAP, dtype=jnp.int32)
    hit = (owner == own_index)[:, :, None] & (rank[:, :, None] == slots[None, None, :])
    pick = jnp.sum(jnp.where(hit, local[:, :, None], 0), axis=1).reshape(-1)
    own_slots = owner * CAP + rank
    return pick, lax.dynamic_index_in_dim(own_slots, own_index, 0, keepdims=False)


def body(sources, slowness, freq_index, coverage):
    groups, _, layers, rows, columns = sources.shape
    bands, members = lax.axis_size("freq"), lax.axis_size("sub")
    own_index = lax.axis_index("sub")
    weights = 1.0 + freq_index.astype(jnp.float32) / 16.0
    inside = jnp.stack([own_index > 0, own_index < members - 1]).astype(jnp.float32)
    params = jnp.stack([0.12 * weights, 4096.0 * weights, inside])
    up = [(i, i + 1) for i in range(members - 1)]
    down = [(j, i) for i, j in up]

    packed = pack(sources, slowness)
    halos = []
    for number in range(0, 6, 2):
        halos.append(
            (lax.ppermute(packed[number], "sub", up), lax.ppermute(packed[number + 1], "sub", down))
        )
    pick, slots = route(coverage, own_index)

    def spread(chunk):
        return lax.all_to_all(chunk, "freq", split_axis=0, concat_axis=0, tiled=True)

    *state, chunk = interior(params, sources, slowness, bands)
    chunks = [spread(chunk)]
    earlier = []
    for depth_in in range(1, 4):
        halo = halos[depth_in - 1]
        if depth_in > 1:
            chunks[-2], halo = lax.optimization_barrier((chunks[-2], halo))
        chunk, *fresh = stage(depth_in, params, halo, state, earlier, bands, columns)
        chunk, chunks[-1] = lax.optimization_barrier((chunk, chunks[-1]))
        chunks.append(spread(chunk))
        earlier.append(fresh)
    depth = rows // bands
    precond, outgoing = pl.pallas_call(
        precond_kernel,
        in_specs=[smem()] + [vmem()] * 4,
        out_specs=[vmem()] * 2,
        out_shape=[
            jax.ShapeDtypeStruct((layers, depth, columns), jnp.float32),
            jax.ShapeDtypeStruct((members * CAP, depth, columns), jnp.float32),
        ],
        compiler_params=compiler_params(12),
        name="precond",
    )(pick, *chunks)
    incoming = lax.all_to_all(outgoing, "sub", split_axis=0, concat_axis=0, tiled=True)
    delivered = pl.pallas_call(
        deliver_kernel,
        in_specs=[smem(), vmem()],
        out_specs=vmem(),
        out_shape=jax.ShapeDtypeStruct((1, 1, coverage.shape[2], depth, columns), jnp.float32),
        compiler_params=compiler_params(12),
        name="deliver",
    )(slots, incoming)
    return precond, delivered


def solution(mesh):
    placed = (
        P("freq", None, "sub", None, None),
        P("sub", None, None),
        P("freq"),
        P("freq", None, None),
    )
    return jax.shard_map(
        body,
        mesh=mesh,
        in_specs=placed,
        out_specs=(P("sub", "freq", None), P("freq", "sub", None, None, None)),
        check_vma=False,
    )
```

```python
import functools

import jax
import jax.numpy as jnp
from jax import lax
from jax.experimental import pallas as pl
from jax.experimental.pallas import tpu as pltpu
from jax.sharding import PartitionSpec as P

TPD = 8
CAP = 2
HALF = 128


def masks():
    lane = lax.broadcasted_iota(jnp.int32, (8, HALF), 1)
    row = lax.broadcasted_iota(jnp.int32, (8, HALF), 0)
    return lane == 0, lane == HALF - 1, row == 0, row == 7


def load_rows(refs, index, nk):
    return [[ref[index + (pl.ds(k, 8, stride=nk), slice(None))] for k in range(nk)] for ref in refs]


def load_plane(ref, index, nk):
    return [[ref[index + (h, pl.ds(8 * k, 8), slice(None))] for k in range(nk)] for h in range(2)]


def store_plane(ref, index, plane):
    for h, pieces in enumerate(plane):
        for k, piece in enumerate(pieces):
            ref[index + (h, pl.ds(8 * k, 8), slice(None))] = piece


def smooth(before, middle, after, marks):
    lane_first, lane_last, row_first, row_last = marks
    nk = len(middle[0])
    depth = []
    for h in range(2):
        across = [
            (before[h][k] + after[h][k]) + (middle[h][k] + middle[h][k]) for k in range(nk)
        ]
        below = jnp.where(row_last, 0.0, pltpu.roll(across[0], 7, 0))
        above = jnp.where(row_first, 0.0, pltpu.roll(across[-1], 1, 0))
        pairs = [across[k] + across[k + 1] for k in range(nk - 1)] + [across[-1] + below]
        depth.append([above + across[0] + pairs[0]] + [pairs[k - 1] + pairs[k] for k in range(1, nk)])
    out = [[], []]
    for k in range(nk):
        left, right = depth[0][k], depth[1][k]
        left_up, right_up = pltpu.roll(left, HALF - 1, 1), pltpu.roll(right, HALF - 1, 1)
        left_down, right_down = pltpu.roll(left, 1, 1), pltpu.roll(right, 1, 1)
        left_sides = jnp.where(lane_last, right_up, left_up) + jnp.where(lane_first, 0.0, left_down)
        right_sides = jnp.where(lane_last, 0.0, right_up) + jnp.where(lane_first, left_down, right_down)
        out[0].append(left_sides + (left + left))
        out[1].append(right_sides + (right + right))
    return out


def turn(real, imag, coef_real, coef_imag):
    new_real = [
        [r * e + i * f for r, i, e, f in zip(*parts)] for parts in zip(real, imag, coef_real, coef_imag)
    ]
    new_imag = [
        [i * e - r * f for r, i, e, f in zip(*parts)] for parts in zip(real, imag, coef_real, coef_imag)
    ]
    return new_real, new_imag


def forced(forcing, smoothed, middle):
    return [
        [s + (v - 8.0 * m) for s, v, m in zip(*parts)] for parts in zip(forcing, smoothed, middle)
    ]


def coefficients(slow, scale, factor):
    coef_real, coef_imag = [], []
    for pieces in slow:
        for out in (coef_real, coef_imag):
            out.append([])
        for piece in pieces:
            sigma = scale * piece
            diag = 0.875 - sigma
            inverse = factor / (diag * diag + sigma * sigma)
            coef_real[-1].append(diag * inverse)
            coef_imag[-1].append(sigma * inverse)
    return coef_real, coef_imag


def relax(forcing, before, middle, after, coef, marks):
    terms = [
        forced(forcing(c), smooth(before(c), middle(c), after(c), marks), middle(c)) for c in range(2)
    ]
    return turn(terms[0], terms[1], coef(0), coef(1))


def products(forward, adjoint, weight):
    (fr, fi), (ar, ai) = forward, adjoint
    grad = [
        [weight * (a * c - b * d) for a, b, c, d in zip(*parts)] for parts in zip(fr, fi, ar, ai)
    ]
    illum = [[weight * (a * a + b * b) for a, b in zip(*parts)] for parts in zip(fr, fi)]
    return grad, illum


def accumulate(acc, side, terms, nk, first):
    for number, plane in enumerate(terms):
        for h, pieces in enumerate(plane):
            for k, piece in enumerate(pieces):
                place = (number, side, h, pl.ds(k, 8, stride=nk), slice(None))
                acc[place] = jnp.where(first, piece, acc[place] + piece)


def write_out(out, acc):
    bands, _, _, depth, _ = out.shape
    for band in range(bands):
        for number in range(2):
            for side in range(2):
                for h in range(2):
                    out[band, number, side, :, pl.ds(h * HALF, HALF)] = acc[
                        number, side, h, pl.ds(band * depth, depth), :
                    ]


def interior_kernel(params, src_l, src_r, slow_l, slow_r, two, three, out, coef, one, last, acc):
    group = pl.program_id(0)
    groups = pl.num_programs(0)
    layers, rows = src_l.shape[2], src_l.shape[3]
    nk = rows // 8
    marks = masks()
    scale, weight = params[0, group], params[1, group]

    def source(pair, layer):
        return lambda c: load_rows((src_l, src_r), (0, 2 * pair + c, layer), nk)

    def factor(layer):
        return lambda c: load_plane(coef, (c, layer), nk)

    @pl.loop(0, layers)
    def _(layer):
        scaled = coefficients(load_rows((slow_l, slow_r), (layer,), nk), scale, 1.0 / 64.0)
        for c in range(2):
            store_plane(coef, (c, layer), scaled[c])
        for pair in range(2):
            force = source(pair, layer)
            planes = turn(force(0), force(1), scaled[0], scaled[1])
            for c in range(2):
                store_plane(one, (pair, layer, c), planes[c])

    def step(pair, layer, ref, lead, skip):
        near = [
            lambda c, at=layer + shift - skip: load_plane(ref, lead + (pair, at, c), nk)
            for shift in (-1, 0, 1)
        ]
        return relax(source(pair, layer), *near, factor(layer), marks)

    @pl.loop(0, (layers - 2) // 2)
    def _(turn_at):
        for offset in range(2):
            layer = 1 + 2 * turn_at + offset
            for pair in range(2):
                planes = step(pair, layer, one, (), 0)
                for c in range(2):
                    store_plane(two, (0, pair, layer - 1, c), planes[c])

    @pl.loop(0, (layers - 4) // 2)
    def _(turn_at):
        for offset in range(2):
            layer = 2 + 2 * turn_at + offset
            for pair in range(2):
                planes = step(pair, layer, two, (0,), 1)
                for c in range(2):
                    store_plane(three, (0, pair, layer - 2, c), planes[c])

    for side in range(2):
        for pair in range(2):
            planes = step(pair, layers // 2 - 1 + side, three, (0,), 2)
            for c in range(2):
                store_plane(last, (side, pair, c), planes[c])
    finish(last, acc, group, weight, nk)

    @pl.when(group == groups - 1)
    def _():
        write_out(out, acc)


def finish(last, acc, group, weight, nk):
    for side in range(2):
        fields = [[load_plane(last, (side, pair, c), nk) for c in range(2)] for pair in range(2)]
        accumulate(acc, side, products(fields[0], fields[1], weight), nk, group == 0)


def stage_kernel(depth_in, keep, params, *refs):
    refs = list(refs)

    def take(count):
        taken = refs[:count]
        del refs[:count]
        return taken

    sides = []
    for _ in range(2):
        source = [take(2) for _ in range(4)]
        slow = [take(2) for _ in range(4)]
        sides.append((source, slow, take(4)))
    out = take(1)[0]
    if keep:
        new_two, new_three = take(2)
    coef, one, fresh, last, acc = take(5)
    group = pl.program_id(0)
    groups = pl.num_programs(0)
    rows = sides[0][1][3][0].shape[-2]
    nk = rows // 8
    marks = masks()
    scale, weight = params[0, group], params[1, group]
    chains = [(side, pair) for side in range(2) for pair in range(2)]

    def force(side, pair, at):
        refs_at = sides[side][0][at]
        if len(refs_at[0].shape) == 3:
            return lambda c: load_rows(refs_at, (2 * pair + c,), nk)
        return lambda c: load_rows(refs_at, (0, 2 * pair + c, 0), nk)

    def factor(side, at):
        return lambda c: load_plane(coef, (side, at, c), nk)

    def first(side, pair, at):
        return lambda c: load_plane(one, (side, pair, at, c), nk)

    def held(side, pair, number):
        return lambda c: load_plane(sides[side][2][number], (0, pair, 0, c), nk)

    def made(side, pair, level):
        return lambda c: load_plane(fresh, (level, side, pair, c), nk)

    for side in range(2):
        for at in range(4):
            amount = params[2, side] / 64.0 if at < depth_in else 1.0 / 64.0
            scaled = coefficients(load_rows(sides[side][1][at], (0,), nk), scale, amount)
            for c in range(2):
                store_plane(coef, (side, at, c), scaled[c])
            if at == 3:
                continue
            for pair in range(2):
                forces = force(side, pair, at)
                planes = turn(forces(0), forces(1), scaled[0], scaled[1])
                for c in range(2):
                    store_plane(one, (side, pair, at, c), planes[c])
    for side, pair in chains:
        near = [first(side, pair, at) for at in range(3)]
        planes = relax(force(side, pair, 1), *near, factor(side, 1), marks)
        for c in range(2):
            store_plane(fresh, (0, side, pair, c), planes[c])
            if keep:
                store_plane(new_two, (0, pair, side, c), planes[c])
    for side, pair in chains:
        near = [made(side, pair, 0), held(side, pair, 0), held(side, pair, 1)]
        planes = relax(force(side, pair, 2), *near, factor(side, 2), marks)
        for c in range(2):
            store_plane(fresh, (1, side, pair, c), planes[c])
            if keep:
                store_plane(new_three, (0, pair, side, c), planes[c])
    for side, pair in chains:
        near = [made(side, pair, 1), held(side, pair, 2), held(side, pair, 3)]
        planes = relax(force(side, pair, 3), *near, factor(side, 3), marks)
        for c in range(2):
            store_plane(last, (side, pair, c), planes[c])
    finish(last, acc, group, weight, nk)

    @pl.when(group == groups - 1)
    def _():
        write_out(out, acc)


def pack_kernel(sources, slowness, *refs):
    outs, sems = refs[:-1], refs[-1]
    groups, _, layers = sources.shape[:3]
    copies = []
    for number, out in enumerate(outs):
        depth_in = number // 2 + 1
        layer = layers - depth_in if number % 2 == 0 else depth_in - 1
        for group in range(groups):
            copies.append(
                pltpu.make_async_copy(
                    sources.at[group, :, layer], out.at[pl.ds(4 * group, 4)], sems.at[number, group]
                )
            )
        copies.append(
            pltpu.make_async_copy(slowness.at[layer], out.at[4 * groups], sems.at[number, groups])
        )
    for copy in copies:
        copy.start()
    for copy in copies:
        copy.wait()


def precond_kernel(pick, *refs):
    chunks, (precond, outgoing) = refs[:-2], refs[-2:]
    layers = precond.shape[0]
    for step, chunk in enumerate(chunks):
        for side in range(2):
            layer = layers // 2 - 1 - step if side == 0 else layers // 2 + step
            grad = chunk[0, 0, side]
            illum = chunk[0, 1, side]
            for other in range(1, chunk.shape[0]):
                grad = grad + chunk[other, 0, side]
                illum = illum + chunk[other, 1, side]
            precond[layer] = grad / jnp.sqrt(illum + 1.0)

    @pl.loop(0, outgoing.shape[0])
    def _(slot):
        outgoing[slot] = precond[pick[slot]]


def deliver_kernel(slots, incoming, out):
    @pl.loop(0, out.shape[2])
    def _(number):
        out[0, 0, number] = incoming[slots[number]]


def smem():
    return pl.BlockSpec(memory_space=pltpu.SMEM)


def vmem():
    return pl.BlockSpec(memory_space=pltpu.VMEM)


def plane_scratch(*lead, rows):
    return pltpu.VMEM(lead + (2, rows, HALF), jnp.float32)


def compiler_params(mebibytes):
    return pltpu.CompilerParams(vmem_limit_bytes=mebibytes * 1024 * 1024)


def light():
    return pl.CostEstimate(flops=1000, bytes_accessed=1000, transcendentals=0)


def in_hbm(array):
    return pltpu.with_memory_space_constraint(array, pltpu.HBM)


def hbm(*shape):
    return pltpu.HBM(shape, jnp.float32)


def pack(sources, slowness):
    groups, _, _, rows, columns = sources.shape
    anywhere = pl.BlockSpec(memory_space=pl.ANY)
    return pl.pallas_call(
        pack_kernel,
        in_specs=[anywhere] * 2,
        out_specs=[anywhere] * 6,
        out_shape=[hbm(4 * groups + 1, rows, columns)] * 6,
        scratch_shapes=[pltpu.SemaphoreType.DMA((6, groups + 1))],
        compiler_params=compiler_params(2),
        name="pack",
    )(in_hbm(sources), in_hbm(slowness))


def interior(params, sources, slowness, bands):
    groups, _, layers, rows, columns = sources.shape
    half = [
        pl.BlockSpec((1, 4, layers, rows, HALF), lambda g, h=h: (g, 0, 0, 0, h)) for h in range(2)
    ]
    slow = [pl.BlockSpec((layers, rows, HALF), lambda g, h=h: (0, 0, h)) for h in range(2)]

    def state(count):
        return (
            hbm(groups, 2, count, 2, 2, rows, HALF),
            pl.BlockSpec((1, 2, count, 2, 2, rows, HALF), lambda g: (g, 0, 0, 0, 0, 0, 0)),
        )

    chunk = (bands, 2, 2, rows // bands, columns)
    shapes = [state(layers - 2), state(layers - 4)]
    sources, slowness = in_hbm(sources), in_hbm(slowness)
    return pl.pallas_call(
        interior_kernel,
        grid=(groups,),
        in_specs=[smem()] + half + slow,
        out_specs=[s[1] for s in shapes] + [pl.BlockSpec(chunk, lambda g: (0,) * 5)],
        out_shape=[s[0] for s in shapes] + [hbm(*chunk)],
        scratch_shapes=[
            plane_scratch(2, layers, rows=rows),
            plane_scratch(2, layers, 2, rows=rows),
            plane_scratch(2, 2, 2, rows=rows),
            plane_scratch(2, 2, rows=rows),
        ],
        compiler_params=compiler_params(32),
        cost_estimate=light(),
        name="interior",
    )(params, sources, sources, slowness, slowness)


def stage(depth_in, params, sources, slowness, halos, held, bands, keep):
    groups, _, layers, rows, columns = sources.shape
    operands, specs = [params], [smem()]

    def add(array, block, index):
        operands.append(array)
        specs.append(pl.BlockSpec(block, index))

    sources, slowness = in_hbm(sources), in_hbm(slowness)
    for side in range(2):
        for what in range(2):
            for at in range(4):
                layer = at - depth_in
                for h in range(2):
                    if layer < 0:
                        halo = halos[-layer - 1][side]
                        if what == 0:
                            add(halo, (4, rows, HALF), lambda g, h=h: (g, 0, h))
                        else:
                            add(halo, (1, rows, HALF), lambda g, h=h: (4 * groups, 0, h))
                        continue
                    own = layer if side == 0 else layers - 1 - layer
                    if what == 0:
                        add(
                            sources,
                            (1, 4, 1, rows, HALF),
                            lambda g, h=h, own=own: (g, 0, own, 0, h),
                        )
                    else:
                        add(slowness, (1, rows, HALF), lambda g, h=h, own=own: (own, 0, h))
        for array, places in held:
            add(
                in_hbm(array),
                (1, 2, 1, 2, 2, rows, HALF),
                lambda g, at=places[side]: (g, 0, at, 0, 0, 0, 0),
            )
    chunk = (bands, 2, 2, rows // bands, columns)
    out_shape = [hbm(*chunk)]
    out_specs = [pl.BlockSpec(chunk, lambda g: (0,) * 5)]
    if keep:
        for _ in range(2):
            out_shape.append(hbm(groups, 2, 2, 2, 2, rows, HALF))
            out_specs.append(
                pl.BlockSpec((1, 2, 2, 2, 2, rows, HALF), lambda g: (g, 0, 0, 0, 0, 0, 0))
            )
    return pl.pallas_call(
        functools.partial(stage_kernel, depth_in, keep),
        grid=(groups,),
        in_specs=specs,
        out_specs=out_specs,
        out_shape=out_shape,
        scratch_shapes=[
            plane_scratch(2, 4, 2, rows=rows),
            plane_scratch(2, 2, 3, 2, rows=rows),
            plane_scratch(2, 2, 2, 2, rows=rows),
            plane_scratch(2, 2, 2, rows=rows),
            plane_scratch(2, 2, rows=rows),
        ],
        compiler_params=compiler_params(32),
        cost_estimate=light(),
        name=f"stage{depth_in}",
    )(*operands)


def route(coverage, own_index):
    lists = coverage[0]
    owner, local = lists // TPD, lists % TPD
    position = jnp.arange(lists.shape[1], dtype=jnp.int32)
    same_owner = owner[:, :, None] == owner[:, None, :]
    earlier = position[None, :] < position[:, None]
    rank = jnp.sum((same_owner & earlier[None]).astype(jnp.int32), axis=2)
    slots = jnp.arange(CAP, dtype=jnp.int32)
    hit = (owner == own_index)[:, :, None] & (rank[:, :, None] == slots[None, None, :])
    pick = jnp.sum(jnp.where(hit, local[:, :, None], 0), axis=1).reshape(-1)
    own_slots = owner * CAP + rank
    return pick, lax.dynamic_index_in_dim(own_slots, own_index, 0, keepdims=False)


def body(sources, slowness, freq_index, coverage):
    groups, _, layers, rows, columns = sources.shape
    bands, members = lax.axis_size("freq"), lax.axis_size("sub")
    own_index = lax.axis_index("sub")
    weights = 1.0 + freq_index.astype(jnp.float32) / 16.0
    inside = jnp.stack([own_index > 0, own_index < members - 1]).astype(jnp.float32)
    params = jnp.stack([0.12 * weights, 4096.0 * weights, inside])
    up = [(i, i + 1) for i in range(members - 1)]
    down = [(j, i) for i, j in up]

    packed = pack(sources, slowness)
    halos = []
    for number in range(0, 6, 2):
        halos.append(
            (lax.ppermute(packed[number], "sub", up), lax.ppermute(packed[number + 1], "sub", down))
        )
    pick, slots = route(coverage, own_index)

    def spread(chunk):
        return lax.all_to_all(chunk, "freq", split_axis=0, concat_axis=0, tiled=True)

    two, three, chunk = interior(params, sources, slowness, bands)
    chunks = [spread(chunk)]
    twos = [(two, (1, layers - 4)), (two, (0, layers - 3))]
    threes = [(three, (1, layers - 6)), (three, (0, layers - 5))]
    for depth_in in range(1, 4):
        keep = depth_in < 3
        held = [twos[-1], twos[-2], threes[-1], threes[-2]]
        near = halos[: depth_in]
        if depth_in > 1:
            chunks[-2], near[-1] = lax.optimization_barrier((chunks[-2], near[-1]))
        outs = stage(depth_in, params, sources, slowness, near, held, bands, keep)
        chunk, chunks[-1] = lax.optimization_barrier((outs[0], chunks[-1]))
        chunks.append(spread(chunk))
        if keep:
            twos.append((outs[1], (0, 1)))
            threes.append((outs[2], (0, 1)))
    depth = rows // bands
    precond, outgoing = pl.pallas_call(
        precond_kernel,
        in_specs=[smem()] + [vmem()] * 4,
        out_specs=[vmem()] * 2,
        out_shape=[
            jax.ShapeDtypeStruct((layers, depth, columns), jnp.float32),
            jax.ShapeDtypeStruct((members * CAP, depth, columns), jnp.float32),
        ],
        compiler_params=compiler_params(12),
        name="precond",
    )(pick, *chunks)
    incoming = lax.all_to_all(outgoing, "sub", split_axis=0, concat_axis=0, tiled=True)
    delivered = pl.pallas_call(
        deliver_kernel,
        in_specs=[smem(), vmem()],
        out_specs=vmem(),
        out_shape=jax.ShapeDtypeStruct((1, 1, coverage.shape[2], depth, columns), jnp.float32),
        compiler_params=compiler_params(12),
        name="deliver",
    )(slots, incoming)
    return precond, delivered


def solution(mesh):
    placed = (
        P("freq", None, "sub", None, None),
        P("sub", None, None),
        P("freq"),
        P("freq", None, None),
    )
    return jax.shard_map(
        body,
        mesh=mesh,
        in_specs=placed,
        out_specs=(P("sub", "freq", None), P("freq", "sub", None, None, None)),
        check_vma=False,
    )
```

```python
import functools

import jax
import jax.numpy as jnp
from jax import lax
from jax.experimental import pallas as pl
from jax.experimental.pallas import tpu as pltpu
from jax.sharding import PartitionSpec as P

TPD = 8
CAP = 2
HALF = 128


def masks():
    lane = lax.broadcasted_iota(jnp.int32, (8, HALF), 1)
    row = lax.broadcasted_iota(jnp.int32, (8, HALF), 0)
    return lane == 0, lane == HALF - 1, row == 0, row == 7


def turn(real, imag, coef_real, coef_imag):
    return real * coef_real + imag * coef_imag, imag * coef_real - real * coef_imag


def coefficients(store, slow, scale, factor, nk):
    for k in range(nk):
        for h in range(2):
            sigma = scale * slow(h, k)
            diag = 0.875 - sigma
            inverse = factor / (diag * diag + sigma * sigma)
            store(0, h, k, diag * inverse)
            store(1, h, k, sigma * inverse)


def relax(store, force, near, coef, marks, nk):
    lane_first, lane_last, row_first, row_last = marks

    def across(c, h, k):
        before, middle, after = [layer(c, h, k) for layer in near]
        return (before + after) + (middle + middle)

    both = [(c, h) for c in range(2) for h in range(2)]
    top = {at: across(*at, 0) for at in both}
    bottom = {at: across(*at, nk - 1) for at in both}
    here = top
    pair = {at: jnp.where(row_first, 0.0, pltpu.roll(bottom[at], 1, 0)) + top[at] for at in both}
    for k in range(nk):
        if k < nk - 2:
            following = {at: across(*at, k + 1) for at in both}
        elif k == nk - 2:
            following = bottom
        else:
            following = {at: jnp.where(row_last, 0.0, pltpu.roll(top[at], 7, 0)) for at in both}
        terms = []
        for c in range(2):
            depth = []
            for h in range(2):
                later = here[c, h] + following[c, h]
                depth.append(pair[c, h] + later)
                pair[c, h] = later
            left, right = depth
            left_up, right_up = pltpu.roll(left, HALF - 1, 1), pltpu.roll(right, HALF - 1, 1)
            left_down, right_down = pltpu.roll(left, 1, 1), pltpu.roll(right, 1, 1)
            left_sides = jnp.where(lane_last, right_up, left_up) + jnp.where(lane_first, 0.0, left_down)
            right_sides = jnp.where(lane_last, 0.0, right_up) + jnp.where(
                lane_first, left_down, right_down
            )
            for h, (middle, ends) in enumerate(((left, left_sides), (right, right_sides))):
                total = ends + (middle + middle)
                terms.append(force(c, h, k) + (total - 8.0 * near[1](c, h, k)))
        here = following
        for h in range(2):
            planes = turn(terms[h], terms[2 + h], coef(0, h, k), coef(1, h, k))
            for c in range(2):
                store(c, h, k, planes[c])


def piece_of(ref, lead):
    return lambda c, h, k: ref[lead + (c, h, pl.ds(8 * k, 8), slice(None))]


def row_piece(refs, lead, offset, tail, nk):
    return lambda c, h, k: refs[h][
        lead + (offset + c,) + tail + (pl.ds(k, 8, stride=nk), slice(None))
    ]


def store_to(*places):
    def store(c, h, k, piece):
        for ref, lead in places:
            ref[lead + (c, h, pl.ds(8 * k, 8), slice(None))] = piece

    return store


def start_layer(store, force, coef, nk):
    for k in range(nk):
        for h in range(2):
            planes = turn(force(0, h, k), force(1, h, k), coef(0, h, k), coef(1, h, k))
            for c in range(2):
                store(c, h, k, planes[c])


def products(last, acc, place, weight, first, nk):
    for side in range(2):
        forward, adjoint = [piece_of(last, (side, pair)) for pair in range(2)]
        for h in range(2):
            for k in range(nk):
                fr, fi = forward(0, h, k), forward(1, h, k)
                ar, ai = adjoint(0, h, k), adjoint(1, h, k)
                terms = (weight * (fr * ar - fi * ai), weight * (fr * fr + fi * fi))
                for number, term in enumerate(terms):
                    at = (place, number, side, h, pl.ds(k, 8, stride=nk), slice(None))
                    acc[at] = jnp.where(first, term, acc[at] + term)


def write_out(out, acc, offset):
    bands, _, _, _, depth, _ = out.shape
    for band in range(bands):
        for place in range(acc.shape[0]):
            for number in range(2):
                for side in range(2):
                    for h in range(2):
                        out[band, offset + place, number, side, :, pl.ds(h * HALF, HALF)] = acc[
                            place, number, side, h, pl.ds(band * depth, depth), :
                        ]


def interior_kernel(params, src_l, src_r, slow_l, slow_r, two, three, out, coef, one, force, last, acc):
    group = pl.program_id(0)
    groups = pl.num_programs(0)
    layers, rows = src_l.shape[2], src_l.shape[3]
    nk = rows // 8
    marks = masks()
    scale, weight = params[0, group], params[1, group]
    sources, slows = (src_l, src_r), (slow_l, slow_r)

    @pl.loop(0, layers)
    def _(layer):
        coefficients(
            store_to((coef, (layer,))),
            lambda h, k: slows[h][layer, pl.ds(k, 8, stride=nk), :],
            scale,
            1.0 / 64.0,
            nk,
        )
        for pair in range(2):
            rows_of = row_piece(sources, (0,), 2 * pair, (layer,), nk)
            keep = store_to((force, (pair, layer)))
            for c in range(2):
                for h in range(2):
                    for k in range(nk):
                        keep(c, h, k, rows_of(c, h, k))
            start_layer(store_to((one, (pair, layer))), rows_of, piece_of(coef, (layer,)), nk)

    def step(target, pair, layer, ref, lead, skip):
        near = [piece_of(ref, lead + (pair, layer + shift - skip)) for shift in (-1, 0, 1)]
        relax(
            store_to(target),
            piece_of(force, (pair, layer)),
            near,
            piece_of(coef, (layer,)),
            marks,
            nk,
        )

    @pl.loop(0, (layers - 2) // 2)
    def _(turn_at):
        for offset in range(2):
            layer = 1 + 2 * turn_at + offset
            for pair in range(2):
                step((two, (0, pair, layer - 1)), pair, layer, one, (), 0)

    @pl.loop(0, (layers - 4) // 2)
    def _(turn_at):
        for offset in range(2):
            layer = 2 + 2 * turn_at + offset
            for pair in range(2):
                step((three, (0, pair, layer - 2)), pair, layer, two, (0,), 1)

    for side in range(2):
        for pair in range(2):
            step((last, (side, pair)), pair, layers // 2 - 1 + side, three, (0,), 2)
    products(last, acc, 0, weight, group == 0, nk)

    @pl.when(group == groups - 1)
    def _():
        write_out(out, acc, 0)


def stage_kernel(depths, keep, params, *refs):
    refs = list(refs)

    def take(count):
        taken = refs[:count]
        del refs[:count]
        return taken

    reach = range(-depths[-1], 4 - depths[0])
    sides = []
    for _ in range(2):
        source = {at: take(2) for at in reach}
        slow = {at: take(2) for at in reach}
        sides.append((source, slow, take(4)))
    inner = take(1)[0] if keep else None
    out = take(1)[0]
    if keep:
        new_two, new_three = take(2)
    coef, one, fresh, last, acc = take(5)
    group = pl.program_id(0)
    groups = pl.num_programs(0)
    rows = sides[0][1][reach[-1]][0].shape[-2]
    nk = rows // 8
    marks = masks()
    scale, weight = params[0, group], params[1, group]
    chains = [(side, pair) for side in range(2) for pair in range(2)]

    def force(side, pair, at):
        refs_at = sides[side][0][at]
        if len(refs_at[0].shape) == 3:
            return row_piece(refs_at, (), 2 * pair, (), nk)
        return row_piece(refs_at, (0,), 2 * pair, (0,), nk)

    def place(at):
        return at - reach[0]

    def factor(side, at):
        return piece_of(coef, (side, place(at)))

    for side in range(2):
        for at in reach:
            slows = sides[side][1][at]
            coefficients(
                store_to((coef, (side, place(at)))),
                lambda h, k, slows=slows: slows[h][0, pl.ds(k, 8, stride=nk), :],
                scale,
                params[2, side] / 64.0 if at < 0 else 1.0 / 64.0,
                nk,
            )
            if at < reach[-1]:
                for pair in range(2):
                    start_layer(
                        store_to((one, (side, pair, place(at)))),
                        force(side, pair, at),
                        factor(side, at),
                        nk,
                    )
    twos, threes = {}, {}
    for side, pair in chains:
        near_two, far_two, near_three, far_three = [
            piece_of(ref, (0, pair, 0)) for ref in sides[side][2]
        ]
        twos[side, pair, 2 - depths[0]] = near_two
        twos[side, pair, 3 - depths[0]] = far_two
        threes[side, pair, 3 - depths[0]] = near_three
        threes[side, pair, 4 - depths[0]] = far_three
    for number, j in enumerate(depths):
        for side, pair in chains:
            at = 1 - j
            target = [(fresh, (0, number, side, pair))]
            if keep:
                target.append((new_two, (0, pair, side)))
            near = [piece_of(one, (side, pair, place(at + shift))) for shift in (-1, 0, 1)]
            relax(store_to(*target), force(side, pair, at), near, factor(side, at), marks, nk)
            twos[side, pair, at] = piece_of(*target[0])
        for side, pair in chains:
            at = 2 - j
            target = [(fresh, (1, number, side, pair))]
            if keep:
                target.append((new_three, (0, pair, side)))
            near = [twos[side, pair, at + shift] for shift in (-1, 0, 1)]
            relax(store_to(*target), force(side, pair, at), near, factor(side, at), marks, nk)
            threes[side, pair, at] = piece_of(*target[0])
        for side, pair in chains:
            at = 3 - j
            near = [threes[side, pair, at + shift] for shift in (-1, 0, 1)]
            relax(
                store_to((last, (side, pair))),
                force(side, pair, at),
                near,
                factor(side, at),
                marks,
                nk,
            )
        products(last, acc, number, weight, group == 0, nk)

    @pl.when(group == groups - 1)
    def _():
        if keep:
            out[:, 0] = inner[:, 0]
        write_out(out, acc, 1 if keep else 0)


def pack_kernel(sources, slowness, *refs):
    count = (len(refs) - 2) // 2
    outs, held, sems, out_sems = refs[:count], refs[count : 2 * count], refs[-2], refs[-1]
    groups, _, layers = sources.shape[:3]
    loads, stores = [], []
    first = 1
    for number in range(0, count, 2):
        deep = held[number].shape[0]
        for side in range(2):
            place = number + side
            start = layers - first - deep + 1 if side == 0 else first - 1
            mine = []
            for at in range(deep):
                depth_at = deep - 1 - at if side == 0 else at
                own = start + at
                for group in range(groups):
                    mine.append(
                        pltpu.make_async_copy(
                            sources.at[group, :, own],
                            held[place].at[depth_at, pl.ds(4 * group, 4)],
                            sems.at[place, len(mine)],
                        )
                    )
                mine.append(
                    pltpu.make_async_copy(
                        slowness.at[own],
                        held[place].at[depth_at, 4 * groups],
                        sems.at[place, len(mine)],
                    )
                )
            loads.append(mine)
            stores.append(pltpu.make_async_copy(held[place], outs[place], out_sems.at[place]))
        first += deep
    for mine in loads:
        for copy in mine:
            copy.start()
    for mine, store in zip(loads, stores):
        for copy in mine:
            copy.wait()
        store.start()
    for store in stores:
        store.wait()


def precond_kernel(pick, *refs):
    chunks, (precond, outgoing) = refs[:-2], refs[-2:]
    layers = precond.shape[0]
    step = 0
    for chunk in chunks:
        for place in range(chunk.shape[1]):
            for side in range(2):
                layer = layers // 2 - 1 - step if side == 0 else layers // 2 + step
                grad = chunk[0, place, 0, side]
                illum = chunk[0, place, 1, side]
                for other in range(1, chunk.shape[0]):
                    grad = grad + chunk[other, place, 0, side]
                    illum = illum + chunk[other, place, 1, side]
                precond[layer] = grad / jnp.sqrt(illum + 1.0)
            step += 1

    @pl.loop(0, outgoing.shape[0])
    def _(slot):
        outgoing[slot] = precond[pick[slot]]


def deliver_kernel(slots, incoming, out):
    @pl.loop(0, out.shape[2])
    def _(number):
        out[0, 0, number] = incoming[slots[number]]


def smem():
    return pl.BlockSpec(memory_space=pltpu.SMEM)


def vmem():
    return pl.BlockSpec(memory_space=pltpu.VMEM)


def plane_scratch(*lead, rows):
    return pltpu.VMEM(lead + (2, rows, HALF), jnp.float32)


def compiler_params(mebibytes):
    return pltpu.CompilerParams(vmem_limit_bytes=mebibytes * 1024 * 1024)


def light():
    return pl.CostEstimate(flops=1000, bytes_accessed=1000, transcendentals=0)


def in_hbm(array):
    return pltpu.with_memory_space_constraint(array, pltpu.HBM)


def hbm(*shape):
    return pltpu.HBM(shape, jnp.float32)


def pack(sources, slowness, depths):
    groups, _, _, rows, columns = sources.shape
    anywhere = pl.BlockSpec(memory_space=pl.ANY)
    shapes = [(len(part), 4 * groups + 1, rows, columns) for part in depths for _ in range(2)]
    return pl.pallas_call(
        pack_kernel,
        in_specs=[anywhere] * 2,
        out_specs=[anywhere] * len(shapes),
        out_shape=[hbm(*shape) for shape in shapes],
        scratch_shapes=[pltpu.VMEM(shape, jnp.float32) for shape in shapes]
        + [
            pltpu.SemaphoreType.DMA((len(shapes), max(map(len, depths)) * (groups + 1))),
            pltpu.SemaphoreType.DMA((len(shapes),)),
        ],
        compiler_params=compiler_params(8),
        cost_estimate=light(),
        name="pack",
    )(in_hbm(sources), in_hbm(slowness))


def interior(params, sources, slowness, bands):
    groups, _, layers, rows, columns = sources.shape
    half = [
        pl.BlockSpec((1, 4, layers, rows, HALF), lambda g, h=h: (g, 0, 0, 0, h)) for h in range(2)
    ]
    slow = [pl.BlockSpec((layers, rows, HALF), lambda g, h=h: (0, 0, h)) for h in range(2)]

    def state(count):
        return (
            hbm(groups, 2, count, 2, 2, rows, HALF),
            pl.BlockSpec((1, 2, count, 2, 2, rows, HALF), lambda g: (g, 0, 0, 0, 0, 0, 0)),
        )

    chunk = (bands, 1, 2, 2, rows // bands, columns)
    shapes = [state(layers - 2), state(layers - 4)]
    sources, slowness = in_hbm(sources), in_hbm(slowness)
    return pl.pallas_call(
        interior_kernel,
        grid=(groups,),
        in_specs=[smem()] + half + slow,
        out_specs=[s[1] for s in shapes] + [pl.BlockSpec(chunk, lambda g: (0,) * 6)],
        out_shape=[s[0] for s in shapes] + [hbm(*chunk)],
        scratch_shapes=[
            plane_scratch(layers, 2, rows=rows),
            plane_scratch(2, layers, 2, rows=rows),
            plane_scratch(2, layers, 2, rows=rows),
            plane_scratch(2, 2, 2, rows=rows),
            plane_scratch(1, 2, 2, rows=rows),
        ],
        compiler_params=compiler_params(32),
        cost_estimate=light(),
        name="interior",
    )(params, sources, sources, slowness, slowness)


def stage(depths, params, sources, slowness, halos, held, inner, bands):
    groups, _, layers, rows, columns = sources.shape
    operands, specs = [params], [smem()]

    def add(array, block, index):
        operands.append(array)
        specs.append(pl.BlockSpec(block, index))

    sources, slowness = in_hbm(sources), in_hbm(slowness)
    reach = range(-depths[-1], 4 - depths[0])
    for side in range(2):
        for what in range(2):
            for layer in reach:
                for h in range(2):
                    if layer < 0:
                        halo, at = halos[-layer][side]
                        if what == 0:
                            add(halo, (pl.squeezed, 4, rows, HALF), lambda g, h=h, at=at: (at, g, 0, h))
                        else:
                            add(
                                halo,
                                (pl.squeezed, 1, rows, HALF),
                                lambda g, h=h, at=at: (at, 4 * groups, 0, h),
                            )
                        continue
                    own = layer if side == 0 else layers - 1 - layer
                    if what == 0:
                        add(
                            sources,
                            (1, 4, 1, rows, HALF),
                            lambda g, h=h, own=own: (g, 0, own, 0, h),
                        )
                    else:
                        add(slowness, (1, rows, HALF), lambda g, h=h, own=own: (own, 0, h))
        for array, places in held:
            add(
                in_hbm(array),
                (1, 2, 1, 2, 2, rows, HALF),
                lambda g, at=places[side]: (g, 0, at, 0, 0, 0, 0),
            )
    keep = inner is not None
    if keep:
        add(in_hbm(inner), inner.shape, lambda g: (0,) * 6)
    count = len(depths)
    chunk = (bands, count + (1 if keep else 0), 2, 2, rows // bands, columns)
    out_shape = [hbm(*chunk)]
    out_specs = [pl.BlockSpec(chunk, lambda g: (0,) * 6)]
    if keep:
        for _ in range(2):
            out_shape.append(hbm(groups, 2, 2, 2, 2, rows, HALF))
            out_specs.append(
                pl.BlockSpec((1, 2, 2, 2, 2, rows, HALF), lambda g: (g, 0, 0, 0, 0, 0, 0))
            )
    return pl.pallas_call(
        functools.partial(stage_kernel, depths, keep),
        grid=(groups,),
        in_specs=specs,
        out_specs=out_specs,
        out_shape=out_shape,
        scratch_shapes=[
            plane_scratch(2, len(reach), 2, rows=rows),
            plane_scratch(2, 2, len(reach) - 1, 2, rows=rows),
            plane_scratch(2, count, 2, 2, 2, rows=rows),
            plane_scratch(2, 2, 2, rows=rows),
            plane_scratch(count, 2, 2, rows=rows),
        ],
        compiler_params=compiler_params(32),
        cost_estimate=light(),
        name="stage" + "".join(str(j) for j in depths),
    )(*operands)


def route(coverage, own_index):
    lists = coverage[0]
    owner, local = lists // TPD, lists % TPD
    position = jnp.arange(lists.shape[1], dtype=jnp.int32)
    same_owner = owner[:, :, None] == owner[:, None, :]
    earlier = position[None, :] < position[:, None]
    rank = jnp.sum((same_owner & earlier[None]).astype(jnp.int32), axis=2)
    slots = jnp.arange(CAP, dtype=jnp.int32)
    hit = (owner == own_index)[:, :, None] & (rank[:, :, None] == slots[None, None, :])
    pick = jnp.sum(jnp.where(hit, local[:, :, None], 0), axis=1).reshape(-1)
    own_slots = owner * CAP + rank
    return pick, lax.dynamic_index_in_dim(own_slots, own_index, 0, keepdims=False)


def body(sources, slowness, freq_index, coverage):
    groups, _, layers, rows, columns = sources.shape
    bands, members = lax.axis_size("freq"), lax.axis_size("sub")
    own_index = lax.axis_index("sub")
    weights = 1.0 + freq_index.astype(jnp.float32) / 16.0
    inside = jnp.stack([own_index > 0, own_index < members - 1]).astype(jnp.float32)
    params = jnp.stack([0.12 * weights, 4096.0 * weights, inside])
    up = [(i, i + 1) for i in range(members - 1)]
    down = [(j, i) for i, j in up]

    parts = ((1,), (2, 3))
    packed = pack(sources, slowness, parts)
    halos = {}
    for number, depths in enumerate(parts):
        sent = (
            lax.ppermute(packed[2 * number], "sub", up),
            lax.ppermute(packed[2 * number + 1], "sub", down),
        )
        for at, depth_in in enumerate(depths):
            halos[depth_in] = [(array, at) for array in sent]
    pick, slots = route(coverage, own_index)

    def spread(chunk):
        return lax.all_to_all(chunk, "freq", split_axis=0, concat_axis=0, tiled=True)

    two, three, inner = interior(params, sources, slowness, bands)
    held = [
        (two, (0, layers - 3)),
        (two, (1, layers - 4)),
        (three, (0, layers - 5)),
        (three, (1, layers - 6)),
    ]
    chunk, new_two, new_three = stage(
        parts[0], params, sources, slowness, halos, held, inner, bands
    )
    chunks = [spread(chunk)]
    held = [(new_two, (0, 1)), held[0], (new_three, (0, 1)), held[2]]
    (chunk,) = stage(parts[1], params, sources, slowness, halos, held, None, bands)
    chunks[0], chunk = lax.optimization_barrier((chunks[0], chunk))
    chunks.append(spread(chunk))
    depth = rows // bands
    precond, outgoing = pl.pallas_call(
        precond_kernel,
        in_specs=[smem()] + [vmem()] * len(chunks),
        out_specs=[vmem()] * 2,
        out_shape=[
            jax.ShapeDtypeStruct((layers, depth, columns), jnp.float32),
            jax.ShapeDtypeStruct((members * CAP, depth, columns), jnp.float32),
        ],
        compiler_params=compiler_params(12),
        name="precond",
    )(pick, *chunks)
    incoming = lax.all_to_all(outgoing, "sub", split_axis=0, concat_axis=0, tiled=True)
    delivered = pl.pallas_call(
        deliver_kernel,
        in_specs=[smem(), vmem()],
        out_specs=vmem(),
        out_shape=jax.ShapeDtypeStruct((1, 1, coverage.shape[2], depth, columns), jnp.float32),
        compiler_params=compiler_params(12),
        name="deliver",
    )(slots, incoming)
    return precond, delivered


def solution(mesh):
    placed = (
        P("freq", None, "sub", None, None),
        P("sub", None, None),
        P("freq"),
        P("freq", None, None),
    )
    return jax.shard_map(
        body,
        mesh=mesh,
        in_specs=placed,
        out_specs=(P("sub", "freq", None), P("freq", "sub", None, None, None)),
        check_vma=False,
    )
```

```python
import jax
import jax.numpy as jnp
from jax import lax
from jax.experimental import pallas as pl
from jax.experimental.pallas import tpu as pltpu
from jax.sharding import PartitionSpec as P

TPD = 8
CAP = 2
HALF = 128


def masks():
    lane = lax.broadcasted_iota(jnp.int32, (8, HALF), 1)
    row = lax.broadcasted_iota(jnp.int32, (8, HALF), 0)
    return lane == 0, lane == HALF - 1, row == 0, row == 7


def turn(real, imag, coef_real, coef_imag):
    return real * coef_real + imag * coef_imag, imag * coef_real - real * coef_imag


def coefficients(store, slow, scale, factor, nk):
    for k in range(nk):
        for h in range(2):
            sigma = scale * slow(h, k)
            diag = 0.875 - sigma
            inverse = factor / (diag * diag + sigma * sigma)
            store(0, h, k, diag * inverse)
            store(1, h, k, sigma * inverse)


def relax(store, force, near, coef, marks, nk):
    lane_first, lane_last, row_first, row_last = marks

    def across(c, h, k):
        before, middle, after = [None if layer is None else layer(c, h, k) for layer in near]
        ends = after if before is None else before + after
        return ends if middle is None else ends + (middle + middle)

    both = [(c, h) for c in range(2) for h in range(2)]
    top = {at: across(*at, 0) for at in both}
    bottom = {at: across(*at, nk - 1) for at in both}
    here = top
    pair = {at: jnp.where(row_first, 0.0, pltpu.roll(bottom[at], 1, 0)) + top[at] for at in both}
    for k in range(nk):
        if k < nk - 2:
            following = {at: across(*at, k + 1) for at in both}
        elif k == nk - 2:
            following = bottom
        else:
            following = {at: jnp.where(row_last, 0.0, pltpu.roll(top[at], 7, 0)) for at in both}
        terms = []
        for c in range(2):
            depth = []
            for h in range(2):
                later = here[c, h] + following[c, h]
                depth.append(pair[c, h] + later)
                pair[c, h] = later
            left, right = depth
            left_up, right_up = pltpu.roll(left, HALF - 1, 1), pltpu.roll(right, HALF - 1, 1)
            left_down, right_down = pltpu.roll(left, 1, 1), pltpu.roll(right, 1, 1)
            left_sides = jnp.where(lane_last, right_up, left_up) + jnp.where(lane_first, 0.0, left_down)
            right_sides = jnp.where(lane_last, 0.0, right_up) + jnp.where(
                lane_first, left_down, right_down
            )
            for h, (middle, ends) in enumerate(((left, left_sides), (right, right_sides))):
                total = ends + (middle + middle)
                if near[1] is not None:
                    total = total - 8.0 * near[1](c, h, k)
                terms.append(total if force is None else force(c, h, k) + total)
        here = following
        for h in range(2):
            planes = turn(terms[h], terms[2 + h], coef(0, h, k), coef(1, h, k))
            for c in range(2):
                store(c, h, k, planes[c])


def piece_of(ref, lead):
    return lambda c, h, k: ref[lead + (c, h, pl.ds(8 * k, 8), slice(None))]


def row_piece(refs, lead, offset, tail, nk):
    return lambda c, h, k: refs[h][
        lead + (offset + c,) + tail + (pl.ds(k, 8, stride=nk), slice(None))
    ]


def store_to(*places):
    def store(c, h, k, piece):
        for ref, lead in places:
            ref[lead + (c, h, pl.ds(8 * k, 8), slice(None))] = piece

    return store


def start_layer(store, force, coef, nk):
    for k in range(nk):
        for h in range(2):
            planes = turn(force(0, h, k), force(1, h, k), coef(0, h, k), coef(1, h, k))
            for c in range(2):
                store(c, h, k, planes[c])


def products(last, acc, place, weight, first, nk):
    for side in range(2):
        forward, adjoint = [piece_of(last, (side, pair)) for pair in range(2)]
        for h in range(2):
            for k in range(nk):
                fr, fi = forward(0, h, k), forward(1, h, k)
                ar, ai = adjoint(0, h, k), adjoint(1, h, k)
                terms = (weight * (fr * ar - fi * ai), weight * (fr * fr + fi * fi))
                for number, term in enumerate(terms):
                    at = (place, number, side, h, pl.ds(k, 8, stride=nk), slice(None))
                    acc[at] = jnp.where(first, term, acc[at] + term)


def write_out(out, acc, offset):
    bands, _, _, _, depth, _ = out.shape
    for band in range(bands):
        for place in range(acc.shape[0]):
            for number in range(2):
                for side in range(2):
                    for h in range(2):
                        out[band, offset + place, number, side, :, pl.ds(h * HALF, HALF)] = acc[
                            place, number, side, h, pl.ds(band * depth, depth), :
                        ]


def first_kernel(params, sources, slowness, up, down, raw, slow, coef, sems):
    groups, _, layers, rows = sources.shape[:4]
    nk = rows // 8
    copies = []
    for side in range(2):
        own = side * (layers - 1)
        for h in range(2):
            lanes = pl.ds(h * HALF, HALF)
            for number, (ref, held) in enumerate(
                ((sources.at[:, :, own, :, lanes], raw), (slowness.at[own, :, lanes], slow))
            ):
                copies.append(
                    pltpu.make_async_copy(ref, held.at[side, h], sems.at[side, h, number])
                )
    for copy in copies:
        copy.start()
    for copy in copies:
        copy.wait()
    for side, out in enumerate((down, up)):
        halves = (raw.at[side, 0], raw.at[side, 1])

        def sigma(h, k):
            return slow[side, h, pl.ds(k, 8, stride=nk), :]

        for h in range(2):
            for k in range(nk):
                out[4 * groups, h, pl.ds(8 * k, 8), :] = sigma(h, k)
        for group in range(groups):
            coefficients(store_to((coef, (side, group))), sigma, params[0, group], 1.0 / 64.0, nk)
            for pair in range(2):
                at = 4 * group + 2 * pair
                start_layer(
                    store_from(out, (), at),
                    row_piece(halves, (group,), 2 * pair, (), nk),
                    piece_of(coef, (side, group)),
                    nk,
                )


def store_from(ref, lead, offset):
    def store(c, h, k, piece):
        ref[lead + (offset + c, h, pl.ds(8 * k, 8), slice(None))] = piece

    return store


def sent_piece(ref, lead, offset):
    return lambda c, h, k: ref[lead + (offset + c, h, pl.ds(8 * k, 8), slice(None))]


def edge_kernel(params, *refs):
    sides = []
    for side in range(2):
        part = refs[12 * side : 12 * side + 12]
        sides.append(([part[2 * at : 2 * at + 2] for at in range(3)], [part[6 + 2 * at : 8 + 2 * at] for at in range(3)]))
    up, down, second, coef, one, two = refs[24:]
    group = pl.program_id(0)
    rows = sides[0][1][0][0].shape[-2]
    nk = rows // 8
    marks = masks()
    chains = [(side, pair) for side in range(2) for pair in range(2)]
    outs = (down, up)

    def force(side, pair, at):
        return row_piece(sides[side][0][at], (0,), 2 * pair, (0,), nk)

    for side in range(2):
        for at in range(3):
            slows = sides[side][1][at]
            coefficients(
                store_to((coef, (side, at))),
                lambda h, k, slows=slows: slows[h][0, pl.ds(k, 8, stride=nk), :],
                params[0, group],
                1.0 / 64.0,
                nk,
            )
            for pair in range(2):
                start_layer(
                    store_to((one, (side, pair, at))),
                    force(side, pair, at),
                    piece_of(coef, (side, at)),
                    nk,
                )
    for at in range(2):
        for side, pair in chains:
            near = [piece_of(one, (side, pair, n)) if n >= 0 else None for n in (at - 1, at, at + 1)]
            target = (two, (side, pair)) if at == 0 else (second, (0, pair, side))
            relax(
                store_to(target), force(side, pair, at), near, piece_of(coef, (side, at)), marks, nk
            )
    for side, pair in chains:
        middle = piece_of(two, (side, pair))
        for c in range(2):
            for h in range(2):
                for k in range(nk):
                    store_from(outs[side], (0, 0), 2 * pair)(c, h, k, middle(c, h, k))
        near = [None, middle, piece_of(second, (0, pair, side))]
        relax(
            store_from(outs[side], (1, 0), 2 * pair),
            force(side, pair, 0),
            near,
            piece_of(coef, (side, 0)),
            marks,
            nk,
        )


def inner_kernel(
    params, src_l, src_r, slow_l, slow_r, near_b, near_a, far_b, far_a, second,
    out, two_edge, three_edge, three_next, change_two, change_three,
    coef, beyond, one, force, two, three, last, acc,
):
    group = pl.program_id(0)
    groups = pl.num_programs(0)
    layers, rows = src_l.shape[2], src_l.shape[3]
    nk = rows // 8
    marks = masks()
    scale, weight = params[0, group], params[1, group]
    sources, slows = (src_l, src_r), (slow_l, slow_r)
    halos, halo_slows = (near_b, near_a), (far_b, far_a)
    chains = [(side, pair) for side in range(2) for pair in range(2)]

    @pl.loop(0, layers)
    def _(layer):
        coefficients(
            store_to((coef, (layer,))),
            lambda h, k: slows[h][layer, pl.ds(k, 8, stride=nk), :],
            scale,
            1.0 / 64.0,
            nk,
        )
        for pair in range(2):
            rows_of = row_piece(sources, (0,), 2 * pair, (layer,), nk)
            keep = store_to((force, (pair, layer)))
            for c in range(2):
                for h in range(2):
                    for k in range(nk):
                        keep(c, h, k, rows_of(c, h, k))
            start_layer(store_to((one, (pair, layer))), rows_of, piece_of(coef, (layer,)), nk)

    for side in range(2):
        coefficients(
            store_to((beyond, (side,))),
            lambda h, k: halo_slows[side][0, h, pl.ds(8 * k, 8), :],
            scale,
            params[2, side] / 64.0,
            nk,
        )
    for side, pair in chains:
        given = piece_of(second, (0, pair, side))
        keep = store_to((two, (pair, 1 if side == 0 else layers - 2)))
        for c in range(2):
            for h in range(2):
                for k in range(nk):
                    keep(c, h, k, given(c, h, k))

    def step(targets, pair, layer, near):
        relax(
            store_to(*targets),
            piece_of(force, (pair, layer)),
            near,
            piece_of(coef, (layer,)),
            marks,
            nk,
        )

    def around(ref, pair, layer, skip):
        return [piece_of(ref, (pair, layer + shift - skip)) for shift in (-1, 0, 1)]

    for side, pair in chains:
        layer = side * (layers - 1)
        near = [
            sent_piece(halos[side], (), 2 * pair),
            piece_of(one, (pair, layer)),
            piece_of(one, (pair, layer + 1 - 2 * side)),
        ]
        step(((two, (pair, layer)), (two_edge, (0, pair, side))), pair, layer, near)
    for side, pair in chains:
        near = [None, None, piece_of(one, (pair, side * (layers - 1)))]
        relax(
            store_to((change_two, (0, pair, side))), None, near, piece_of(beyond, (side,)), marks, nk
        )

    @pl.loop(0, (layers - 4) // 2)
    def _(turn_at):
        for offset in range(2):
            layer = 2 + 2 * turn_at + offset
            for pair in range(2):
                step(((two, (pair, layer)),), pair, layer, around(one, pair, layer, 0))

    for side, pair in chains:
        near = [
            None,
            piece_of(change_two, (0, pair, side)),
            piece_of(two, (pair, side * (layers - 1))),
        ]
        relax(
            store_to((change_three, (0, pair, side))),
            None,
            near,
            piece_of(beyond, (side,)),
            marks,
            nk,
        )

    @pl.loop(0, (layers - 2) // 2)
    def _(turn_at):
        for offset in range(2):
            layer = 1 + 2 * turn_at + offset
            for pair in range(2):
                step(((three, (pair, layer - 1)),), pair, layer, around(two, pair, layer, 0))

    for side, pair in chains:
        for at, kept in ((1, three_edge), (2, three_next)):
            layer = at if side == 0 else layers - 1 - at
            given = piece_of(three, (pair, layer - 1))
            keep = store_to((kept, (0, pair, side)))
            for c in range(2):
                for h in range(2):
                    for k in range(nk):
                        keep(c, h, k, given(c, h, k))

    @pl.loop(0, 2)
    def _(place):
        for side, pair in chains:
            layer = layers // 2 - 1 + side + (2 * side - 1) * place
            step(((last, (side, pair)),), pair, layer, around(three, pair, layer, 1))
        products(last, acc, place, weight, group == 0, nk)

    @pl.when(group == groups - 1)
    def _():
        write_out(out, acc, 0)


def outer_kernel(params, *refs):
    sides = []
    for side in range(2):
        part = refs[9 * side : 9 * side + 9]
        sides.append(([part[0:2], part[2:4]], [part[4:6], part[6:8]], part[8]))
    two_edge, second, three_edge, three_next, change_two, change_three = refs[18:24]
    out, coef, fresh, last, acc = refs[24:]
    group = pl.program_id(0)
    groups = pl.num_programs(0)
    rows = sides[0][1][0][0].shape[-2]
    nk = rows // 8
    marks = masks()
    weight = params[1, group]
    chains = [(side, pair) for side in range(2) for pair in range(2)]

    for side in range(2):
        for at in range(2):
            slows = sides[side][1][at]
            coefficients(
                store_to((coef, (side, at))),
                lambda h, k, slows=slows: slows[h][0, pl.ds(k, 8, stride=nk), :],
                params[0, group],
                1.0 / 64.0,
                nk,
            )

    def beyond(side, pair, number, change):
        sent = sent_piece(sides[side][2], (number, 0), 2 * pair)
        add = piece_of(change, (0, pair, side))
        return lambda c, h, k: sent(c, h, k) + add(c, h, k)

    def step(target, side, pair, at, near):
        relax(
            store_to(target),
            row_piece(sides[side][0][at], (0,), 2 * pair, (0,), nk),
            near,
            piece_of(coef, (side, at)),
            marks,
            nk,
        )

    for side, pair in chains:
        near = [
            beyond(side, pair, 0, change_two),
            piece_of(two_edge, (0, pair, side)),
            piece_of(second, (0, pair, side)),
        ]
        step((fresh, (side, pair)), side, pair, 0, near)
    for side, pair in chains:
        near = [piece_of(fresh, (side, pair))] + [
            piece_of(ref, (0, pair, side)) for ref in (three_edge, three_next)
        ]
        step((last, (0, side, pair)), side, pair, 1, near)
    for side, pair in chains:
        near = [
            beyond(side, pair, 1, change_three),
            piece_of(fresh, (side, pair)),
            piece_of(three_edge, (0, pair, side)),
        ]
        step((last, (1, side, pair)), side, pair, 0, near)
    for place in range(2):
        products(last.at[place], acc, place, weight, group == 0, nk)

    @pl.when(group == groups - 1)
    def _():
        write_out(out, acc, 0)


def precond_kernel(pick, *refs):
    chunks, (precond, outgoing) = refs[:-2], refs[-2:]
    layers = precond.shape[0]
    step = 0
    for chunk in chunks:
        for place in range(chunk.shape[1]):
            for side in range(2):
                layer = layers // 2 - 1 - step if side == 0 else layers // 2 + step
                grad = chunk[0, place, 0, side]
                illum = chunk[0, place, 1, side]
                for other in range(1, chunk.shape[0]):
                    grad = grad + chunk[other, place, 0, side]
                    illum = illum + chunk[other, place, 1, side]
                precond[layer] = grad / jnp.sqrt(illum + 1.0)
            step += 1

    @pl.loop(0, outgoing.shape[0])
    def _(slot):
        outgoing[slot] = precond[pick[slot]]


def deliver_kernel(slots, incoming, out):
    @pl.loop(0, out.shape[2])
    def _(number):
        out[0, 0, number] = incoming[slots[number]]


def smem():
    return pl.BlockSpec(memory_space=pltpu.SMEM)


def vmem():
    return pl.BlockSpec(memory_space=pltpu.VMEM)


def plane_scratch(*lead, rows):
    return pltpu.VMEM(lead + (2, rows, HALF), jnp.float32)


def compiler_params(mebibytes):
    return pltpu.CompilerParams(vmem_limit_bytes=mebibytes * 1024 * 1024)


def light():
    return pl.CostEstimate(flops=1000, bytes_accessed=1000, transcendentals=0)


def in_hbm(array):
    return pltpu.with_memory_space_constraint(array, pltpu.HBM)


def hbm(*shape):
    return pltpu.HBM(shape, jnp.float32)


def state(groups, rows):
    return (
        hbm(groups, 2, 2, 2, 2, rows, HALF),
        pl.BlockSpec((1, 2, 2, 2, 2, rows, HALF), lambda g: (g, 0, 0, 0, 0, 0, 0)),
    )


def sent(groups, rows):
    return (
        hbm(2, groups, 4, 2, rows, HALF),
        pl.BlockSpec((2, 1, 4, 2, rows, HALF), lambda g: (0, g, 0, 0, 0, 0)),
    )


def sums(bands, rows, columns):
    shape = (bands, 2, 2, 2, rows // bands, columns)
    return hbm(*shape), pl.BlockSpec(shape, lambda g: (0,) * 6)


def split(pairs):
    return dict(out_shape=[p[0] for p in pairs], out_specs=[p[1] for p in pairs])


def layer_specs(sources, own):
    rows = sources.shape[3]
    return (
        [pl.BlockSpec((1, 4, 1, rows, HALF), lambda g, h=h: (g, 0, own, 0, h)) for h in range(2)],
        [pl.BlockSpec((1, rows, HALF), lambda g, h=h: (own, 0, h)) for h in range(2)],
    )


def first_edges(params, sources, slowness):
    groups, _, _, rows, _ = sources.shape
    anywhere = pl.BlockSpec(memory_space=pl.ANY)
    return pl.pallas_call(
        first_kernel,
        in_specs=[smem(), anywhere, anywhere],
        out_specs=[vmem()] * 2,
        out_shape=[hbm(4 * groups + 1, 2, rows, HALF)] * 2,
        scratch_shapes=[
            pltpu.VMEM((2, 2, groups, 4, rows, HALF), jnp.float32),
            plane_scratch(2, rows=rows),
            plane_scratch(2, groups, 2, rows=rows),
            pltpu.SemaphoreType.DMA((2, 2, 2)),
        ],
        compiler_params=compiler_params(8),
        cost_estimate=light(),
        name="first",
    )(params, in_hbm(sources), in_hbm(slowness))


def later_edges(params, sources, slowness):
    groups, _, layers, rows, _ = sources.shape
    sources, slowness = in_hbm(sources), in_hbm(slowness)
    operands, specs = [params], [smem()]
    for side in range(2):
        parts = [layer_specs(sources, at if side == 0 else layers - 1 - at) for at in range(3)]
        for what, array in enumerate((sources, slowness)):
            for part in parts:
                operands += [array] * 2
                specs += part[what]
    return pl.pallas_call(
        edge_kernel,
        grid=(groups,),
        in_specs=specs,
        **split([sent(groups, rows)] * 2 + [state(groups, rows)]),
        scratch_shapes=[
            plane_scratch(2, 3, 2, rows=rows),
            plane_scratch(2, 2, 3, 2, rows=rows),
            plane_scratch(2, 2, 2, rows=rows),
        ],
        compiler_params=compiler_params(32),
        cost_estimate=light(),
        name="edges",
    )(*operands)


def inner(params, sources, slowness, halo, second, bands):
    groups, _, layers, rows, columns = sources.shape
    half = [
        pl.BlockSpec((1, 4, layers, rows, HALF), lambda g, h=h: (g, 0, 0, 0, h)) for h in range(2)
    ]
    slow = [pl.BlockSpec((layers, rows, HALF), lambda g, h=h: (0, 0, h)) for h in range(2)]
    near = pl.BlockSpec((4, 2, rows, HALF), lambda g: (g, 0, 0, 0))
    far = pl.BlockSpec((1, 2, rows, HALF), lambda g: (4 * groups, 0, 0, 0))
    sources, slowness = in_hbm(sources), in_hbm(slowness)
    return pl.pallas_call(
        inner_kernel,
        grid=(groups,),
        in_specs=[smem()] + half + slow + [near] * 2 + [far] * 2 + [state(groups, rows)[1]],
        **split([sums(bands, rows, columns)] + [state(groups, rows)] * 5),
        scratch_shapes=[
            plane_scratch(layers, 2, rows=rows),
            plane_scratch(2, 2, rows=rows),
            plane_scratch(2, layers, 2, rows=rows),
            plane_scratch(2, layers, 2, rows=rows),
            plane_scratch(2, layers, 2, rows=rows),
            plane_scratch(2, layers - 2, 2, rows=rows),
            plane_scratch(2, 2, 2, rows=rows),
            plane_scratch(2, 2, 2, rows=rows),
        ],
        compiler_params=compiler_params(40),
        cost_estimate=light(),
        name="inner",
    )(params, sources, sources, slowness, slowness, *halo, *halo, in_hbm(second))


def outer(params, sources, slowness, halo, held, bands):
    groups, _, layers, rows, columns = sources.shape
    sources, slowness = in_hbm(sources), in_hbm(slowness)
    operands, specs = [params], [smem()]
    for side in range(2):
        parts = [layer_specs(sources, at if side == 0 else layers - 1 - at) for at in range(2)]
        for what, array in enumerate((sources, slowness)):
            for part in parts:
                operands += [array] * 2
                specs += part[what]
        operands.append(halo[side])
        specs.append(sent(groups, rows)[1])
    for array in held:
        operands.append(in_hbm(array))
        specs.append(state(groups, rows)[1])
    return pl.pallas_call(
        outer_kernel,
        grid=(groups,),
        in_specs=specs,
        **split([sums(bands, rows, columns)]),
        scratch_shapes=[
            plane_scratch(2, 2, 2, rows=rows),
            plane_scratch(2, 2, 2, rows=rows),
            plane_scratch(2, 2, 2, 2, rows=rows),
            plane_scratch(2, 2, 2, rows=rows),
        ],
        compiler_params=compiler_params(32),
        cost_estimate=light(),
        name="outer",
    )(*operands)[0]


def route(coverage, own_index):
    lists = coverage[0]
    owner, local = lists // TPD, lists % TPD
    position = jnp.arange(lists.shape[1], dtype=jnp.int32)
    same_owner = owner[:, :, None] == owner[:, None, :]
    earlier = position[None, :] < position[:, None]
    rank = jnp.sum((same_owner & earlier[None]).astype(jnp.int32), axis=2)
    slots = jnp.arange(CAP, dtype=jnp.int32)
    hit = (owner == own_index)[:, :, None] & (rank[:, :, None] == slots[None, None, :])
    pick = jnp.sum(jnp.where(hit, local[:, :, None], 0), axis=1).reshape(-1)
    own_slots = owner * CAP + rank
    return pick, lax.dynamic_index_in_dim(own_slots, own_index, 0, keepdims=False)


def body(sources, slowness, freq_index, coverage):
    groups, _, layers, rows, columns = sources.shape
    bands, members = lax.axis_size("freq"), lax.axis_size("sub")
    own_index = lax.axis_index("sub")
    weights = 1.0 + freq_index.astype(jnp.float32) / 16.0
    inside = jnp.stack([own_index > 0, own_index < members - 1]).astype(jnp.float32)
    params = jnp.stack([0.12 * weights, 4096.0 * weights, inside])
    up = [(i, i + 1) for i in range(members - 1)]
    down = [(j, i) for i, j in up]

    def exchange(toward_up, toward_down):
        return lax.ppermute(toward_up, "sub", up), lax.ppermute(toward_down, "sub", down)

    near = exchange(*first_edges(params, sources, slowness))
    *edges, second = later_edges(params, sources, slowness)
    far = exchange(*edges)
    pick, slots = route(coverage, own_index)

    def spread(chunk):
        return lax.all_to_all(chunk, "freq", split_axis=0, concat_axis=0, tiled=True)

    chunk, two_edge, *held = inner(params, sources, slowness, near, second, bands)
    chunks = [spread(chunk)]
    chunk = outer(params, sources, slowness, far, [two_edge, second] + held, bands)
    chunks[0], chunk = lax.optimization_barrier((chunks[0], chunk))
    chunks.append(spread(chunk))
    depth = rows // bands
    precond, outgoing = pl.pallas_call(
        precond_kernel,
        in_specs=[smem()] + [vmem()] * len(chunks),
        out_specs=[vmem()] * 2,
        out_shape=[
            jax.ShapeDtypeStruct((layers, depth, columns), jnp.float32),
            jax.ShapeDtypeStruct((members * CAP, depth, columns), jnp.float32),
        ],
        compiler_params=compiler_params(12),
        name="precond",
    )(pick, *chunks)
    incoming = lax.all_to_all(outgoing, "sub", split_axis=0, concat_axis=0, tiled=True)
    delivered = pl.pallas_call(
        deliver_kernel,
        in_specs=[smem(), vmem()],
        out_specs=vmem(),
        out_shape=jax.ShapeDtypeStruct((1, 1, coverage.shape[2], depth, columns), jnp.float32),
        compiler_params=compiler_params(12),
        name="deliver",
    )(slots, incoming)
    return precond, delivered


def solution(mesh):
    placed = (
        P("freq", None, "sub", None, None),
        P("sub", None, None),
        P("freq"),
        P("freq", None, None),
    )
    return jax.shard_map(
        body,
        mesh=mesh,
        in_specs=placed,
        out_specs=(P("sub", "freq", None), P("freq", "sub", None, None, None)),
        check_vma=False,
    )
```

```python
import functools

import jax
import jax.numpy as jnp
from jax import lax
from jax.experimental import pallas as pl
from jax.experimental.pallas import tpu as pltpu
from jax.sharding import PartitionSpec as P

TPD = 8
CAP = 2
HALF = 128


def masks():
    lane = lax.broadcasted_iota(jnp.int32, (8, HALF), 1)
    row = lax.broadcasted_iota(jnp.int32, (8, HALF), 0)
    return lane == 0, lane == HALF - 1, row == 0, row == 7


def turn(real, imag, coef_real, coef_imag):
    return real * coef_real + imag * coef_imag, imag * coef_real - real * coef_imag


def coefficients(store, slow, scale, factor, nk):
    for k in range(nk):
        for h in range(2):
            sigma = scale * slow(h, k)
            diag = 0.875 - sigma
            inverse = factor / (diag * diag + sigma * sigma)
            store(0, h, k, diag * inverse)
            store(1, h, k, sigma * inverse)


def relax(store, force, near, coef, marks, nk, base=None):
    lane_first, lane_last, row_first, row_last = marks

    def across(c, h, k):
        before, middle, after = [None if layer is None else layer(c, h, k) for layer in near]
        parts = [part for part in (before, after) if part is not None]
        if middle is not None:
            parts.append(middle + middle)
        return functools.reduce(lambda total, part: total + part, parts)

    both = [(c, h) for c in range(2) for h in range(2)]
    top = {at: across(*at, 0) for at in both}
    bottom = {at: across(*at, nk - 1) for at in both}
    here = top
    pair = {at: jnp.where(row_first, 0.0, pltpu.roll(bottom[at], 1, 0)) + top[at] for at in both}
    for k in range(nk):
        if k < nk - 2:
            following = {at: across(*at, k + 1) for at in both}
        elif k == nk - 2:
            following = bottom
        else:
            following = {at: jnp.where(row_last, 0.0, pltpu.roll(top[at], 7, 0)) for at in both}
        terms = []
        for c in range(2):
            depth = []
            for h in range(2):
                later = here[c, h] + following[c, h]
                depth.append(pair[c, h] + later)
                pair[c, h] = later
            left, right = depth
            left_up, right_up = pltpu.roll(left, HALF - 1, 1), pltpu.roll(right, HALF - 1, 1)
            left_down, right_down = pltpu.roll(left, 1, 1), pltpu.roll(right, 1, 1)
            left_sides = jnp.where(lane_last, right_up, left_up) + jnp.where(lane_first, 0.0, left_down)
            right_sides = jnp.where(lane_last, 0.0, right_up) + jnp.where(
                lane_first, left_down, right_down
            )
            for h, (middle, ends) in enumerate(((left, left_sides), (right, right_sides))):
                total = ends + (middle + middle)
                if near[1] is not None:
                    total = total - 8.0 * near[1](c, h, k)
                terms.append(total if force is None else force(c, h, k) + total)
        here = following
        for h in range(2):
            planes = turn(terms[h], terms[2 + h], coef(0, h, k), coef(1, h, k))
            for c in range(2):
                store(c, h, k, planes[c] if base is None else base(c, h, k) + planes[c])


def piece_of(ref, lead):
    return lambda c, h, k: ref[lead + (c, h, pl.ds(8 * k, 8), slice(None))]


def row_piece(refs, lead, offset, tail, nk):
    return lambda c, h, k: refs[h][
        lead + (offset + c,) + tail + (pl.ds(k, 8, stride=nk), slice(None))
    ]


def store_to(*places):
    def store(c, h, k, piece):
        for ref, lead in places:
            ref[lead + (c, h, pl.ds(8 * k, 8), slice(None))] = piece

    return store


def start_layer(store, force, coef, nk):
    for k in range(nk):
        for h in range(2):
            planes = turn(force(0, h, k), force(1, h, k), coef(0, h, k), coef(1, h, k))
            for c in range(2):
                store(c, h, k, planes[c])


def products(last, acc, place, weight, first, nk):
    for side in range(2):
        forward, adjoint = [piece_of(last, (side, pair)) for pair in range(2)]
        for h in range(2):
            for k in range(nk):
                fr, fi = forward(0, h, k), forward(1, h, k)
                ar, ai = adjoint(0, h, k), adjoint(1, h, k)
                terms = (weight * (fr * ar - fi * ai), weight * (fr * fr + fi * fi))
                for number, term in enumerate(terms):
                    at = (place, number, side, h, pl.ds(k, 8, stride=nk), slice(None))
                    acc[at] = jnp.where(first, term, acc[at] + term)


def write_out(out, acc, offset):
    bands, _, _, _, depth, _ = out.shape
    for band in range(bands):
        for place in range(acc.shape[0]):
            for number in range(2):
                for side in range(2):
                    for h in range(2):
                        out[band, offset + place, number, side, :, pl.ds(h * HALF, HALF)] = acc[
                            place, number, side, h, pl.ds(band * depth, depth), :
                        ]


def scale_of(freq, group):
    weight = 1.0 + freq[group].astype(jnp.float32) / 16.0
    return weight, 0.12 * weight


def parity():
    return lax.axis_index("sub") % 2


def paired(side):
    index = lax.axis_index("sub")
    there = index > 0 if side == 0 else index < lax.axis_size("sub") - 1
    return jnp.where(there, 1.0 / 64.0, 0.0)


def first_kernel(freq, sources, slowness, out, raw, slow, coef, sems):
    groups, _, layers, rows = sources.shape[:4]
    nk = rows // 8
    own = parity() * (layers - 1)
    copies = []
    for h in range(2):
        lanes = pl.ds(h * HALF, HALF)
        pairs = ((slowness.at[own, :, lanes], slow), (sources.at[:, :, own, :, lanes], raw))
        for number, (ref, held) in enumerate(pairs):
            copies.append(pltpu.make_async_copy(ref, held.at[h], sems.at[h, number]))
    for copy in copies:
        copy.start()
    for copy in copies:
        copy.wait()

    def sigma(h, k):
        return slow[h, pl.ds(k, 8, stride=nk), :]

    for h in range(2):
        for k in range(nk):
            out[4 * groups, h, pl.ds(8 * k, 8), :] = sigma(h, k)
    for group in range(groups):
        coefficients(store_to((coef, (group,))), sigma, scale_of(freq, group)[1], 1.0 / 64.0, nk)
        for pair in range(2):
            start_layer(
                store_from(out, (), 4 * group + 2 * pair),
                row_piece((raw.at[0], raw.at[1]), (group,), 2 * pair, (), nk),
                piece_of(coef, (group,)),
                nk,
            )


def store_from(ref, lead, offset):
    def store(c, h, k, piece):
        ref[lead + (offset + c, h, pl.ds(8 * k, 8), slice(None))] = piece

    return store


def sent_piece(ref, lead, offset):
    return lambda c, h, k: ref[lead + (offset + c, h, pl.ds(8 * k, 8), slice(None))]


def edge_kernel(freq, *refs):
    sides = []
    for side in range(2):
        part = refs[12 * side : 12 * side + 12]
        sides.append([[part[at + 2 * n : at + 2 * n + 2] for n in range(3)] for at in (0, 6)])
    near_all, far, second, coef, one, slow, fields = refs[24:]
    group = pl.program_id(0)
    rows = sides[0][1][0][0].shape[-2]
    nk = rows // 8
    marks = masks()
    scale = scale_of(freq, group)[1]
    chains = [(side, pair) for side in range(2) for pair in range(2)]

    def force(side, pair, at):
        return row_piece(sides[side][0][at], (0,), 2 * pair, (0,), nk)

    for side in range(2):
        for at in range(3):
            slows = sides[side][1][at]
            coefficients(
                store_to((coef, (side, at))),
                lambda h, k, slows=slows: slows[h][0, pl.ds(k, 8, stride=nk), :],
                scale,
                1.0 / 64.0,
                nk,
            )
            for pair in range(2):
                targets = [(one, (side, pair, at))]
                if at == 0:
                    targets.append((fields, (side, 0, pair)))
                start_layer(
                    store_to(*targets), force(side, pair, at), piece_of(coef, (side, at)), nk
                )
        for h in range(2):
            for k in range(nk):
                slow[side, h, pl.ds(8 * k, 8), :] = sides[side][1][0][h][0, pl.ds(k, 8, stride=nk), :]
    for at in range(2):
        for side, pair in chains:
            near = [piece_of(one, (side, pair, n)) if n >= 0 else None for n in (at - 1, at, at + 1)]
            target = (fields, (side, 1, pair)) if at == 0 else (second, (0, pair, side))
            relax(
                store_to(target), force(side, pair, at), near, piece_of(coef, (side, at)), marks, nk
            )
    for side, pair in chains:
        near = [None, piece_of(fields, (side, 1, pair)), piece_of(second, (0, pair, side))]
        relax(
            store_to((fields, (side, 2, pair))),
            force(side, pair, 0),
            near,
            piece_of(coef, (side, 0)),
            marks,
            nk,
        )
    to_chip, to_core = parity(), 1 - parity()
    near_all[0, 12] = slow[to_core]
    for level in range(3):
        for pair in range(2):
            for c in range(2):
                near_all[0, 4 * level + 2 * pair + c] = fields[to_core, level, pair, c]
                if level:
                    far[level - 1, 0, 2 * pair + c] = fields[to_chip, level, pair, c]


def inner_kernel(
    freq, src_l, src_r, slow_l, slow_r, core_field, core_slow, chip_field, chip_slow, second,
    out, base_three, base_next, base_four, factors,
    coef, beyond, one, force, two, three, halo, halo_slow, change, last, acc,
):
    group = pl.program_id(0)
    groups = pl.num_programs(0)
    layers, rows = src_l.shape[2], src_l.shape[3]
    nk = rows // 8
    marks = masks()
    weight, scale = scale_of(freq, group)
    weight = weight * 4096.0
    sources, slows = (src_l, src_r), (slow_l, slow_r)
    chains = [(side, pair) for side in range(2) for pair in range(2)]
    to_chip, to_core = parity(), 1 - parity()
    halo[to_core] = core_field[0]
    halo[to_chip] = chip_field[...]
    halo_slow[to_core] = core_slow[0, 0]
    halo_slow[to_chip] = chip_slow[0]

    @pl.loop(0, layers)
    def _(layer):
        coefficients(
            store_to((coef, (layer,))),
            lambda h, k: slows[h][layer, pl.ds(k, 8, stride=nk), :],
            scale,
            1.0 / 64.0,
            nk,
        )
        for pair in range(2):
            rows_of = row_piece(sources, (0,), 2 * pair, (layer,), nk)
            keep = store_to((force, (pair, layer)))
            for c in range(2):
                for h in range(2):
                    for k in range(nk):
                        keep(c, h, k, rows_of(c, h, k))
            start_layer(store_to((one, (pair, layer))), rows_of, piece_of(coef, (layer,)), nk)

    for side in range(2):
        coefficients(
            store_to((beyond, (side,))),
            lambda h, k, side=side: halo_slow[side, h, pl.ds(8 * k, 8), :],
            scale,
            paired(side),
            nk,
        )
    for side, pair in chains:
        given = piece_of(second, (0, pair, side))
        keep = store_to((two, (pair, 1 if side == 0 else layers - 2)))
        for c in range(2):
            for h in range(2):
                for k in range(nk):
                    keep(c, h, k, given(c, h, k))

    def step(targets, pair, layer, near):
        relax(
            store_to(*targets),
            piece_of(force, (pair, layer)),
            near,
            piece_of(coef, (layer,)),
            marks,
            nk,
        )

    def around(ref, pair, layer, skip):
        return [piece_of(ref, (pair, layer + shift - skip)) for shift in (-1, 0, 1)]

    for side, pair in chains:
        layer = side * (layers - 1)
        near = [
            sent_piece(halo, (side,), 2 * pair),
            piece_of(one, (pair, layer)),
            piece_of(one, (pair, layer + 1 - 2 * side)),
        ]
        step(((two, (pair, layer)),), pair, layer, near)
    for side, pair in chains:
        near = [None, None, piece_of(one, (pair, side * (layers - 1)))]
        relax(
            store_to((change, (0, side, pair))), None, near, piece_of(beyond, (side,)), marks, nk
        )

    @pl.loop(0, (layers - 4) // 2)
    def _(turn_at):
        for offset in range(2):
            layer = 2 + 2 * turn_at + offset
            for pair in range(2):
                step(((two, (pair, layer)),), pair, layer, around(one, pair, layer, 0))

    for side, pair in chains:
        near = [
            None,
            piece_of(change, (0, side, pair)),
            piece_of(two, (pair, side * (layers - 1))),
        ]
        relax(
            store_to((change, (1, side, pair))),
            None,
            near,
            piece_of(beyond, (side,)),
            marks,
            nk,
        )

    @pl.loop(0, (layers - 2) // 2)
    def _(turn_at):
        for offset in range(2):
            layer = 1 + 2 * turn_at + offset
            for pair in range(2):
                step(((three, (pair, layer - 1)),), pair, layer, around(two, pair, layer, 0))

    def layer_at(side, at):
        return at if side == 0 else layers - 1 - at

    for side in range(2):
        for at in range(2):
            given = piece_of(coef, (layer_at(side, at),))
            keep = store_to((factors, (0, side, at)))
            for c in range(2):
                for h in range(2):
                    for k in range(nk):
                        keep(c, h, k, given(c, h, k))
    for side, pair in chains:
        twos = [piece_of(two, (pair, layer_at(side, at))) for at in range(2)]
        threes = [piece_of(three, (pair, layer_at(side, at) - 1)) for at in (1, 2)]
        changes = [piece_of(change, (number, side, pair)) for number in range(2)]
        for target, at, near in (
            (base_three, 0, [changes[0], *twos]),
            (base_next, 1, [None, *threes]),
            (base_four, 0, [changes[1], None, threes[0]]),
        ):
            step(((target, (0, pair, side)),), pair, layer_at(side, at), near)

    @pl.loop(0, 2)
    def _(place):
        for side, pair in chains:
            layer = layers // 2 - 1 + side + (2 * side - 1) * place
            step(((last, (side, pair)),), pair, layer, around(three, pair, layer, 1))
        products(last, acc, place, weight, group == 0, nk)

    @pl.when(group == groups - 1)
    def _():
        write_out(out, acc, 0)


def outer_kernel(freq, core_two, core_three, chip, base_three, base_next, base_four, factors, out, sent_fields, fresh, last, acc):
    group = pl.program_id(0)
    groups = pl.num_programs(0)
    rows = base_three.shape[-2]
    nk = rows // 8
    marks = masks()
    weight = scale_of(freq, group)[0] * 4096.0
    chains = [(side, pair) for side in range(2) for pair in range(2)]
    to_chip, to_core = parity(), 1 - parity()
    for number, ref in enumerate((core_two, core_three)):
        sent_fields[to_core, number] = ref[0]
        sent_fields[to_chip, number] = chip[number, 0]

    def step(target, base, side, pair, at, near):
        relax(
            store_to(target),
            None,
            near,
            piece_of(factors, (0, side, at)),
            marks,
            nk,
            base=piece_of(base, (0, pair, side)),
        )

    for side, pair in chains:
        near = [sent_piece(sent_fields, (side, 0), 2 * pair), None, None]
        step((fresh, (side, pair)), base_three, side, pair, 0, near)
    for side, pair in chains:
        near = [piece_of(fresh, (side, pair)), None, None]
        step((last, (0, side, pair)), base_next, side, pair, 1, near)
    for side, pair in chains:
        near = [sent_piece(sent_fields, (side, 1), 2 * pair), piece_of(fresh, (side, pair)), None]
        step((last, (1, side, pair)), base_four, side, pair, 0, near)
    for place in range(2):
        products(last.at[place], acc, place, weight, group == 0, nk)

    @pl.when(group == groups - 1)
    def _():
        write_out(out, acc, 0)


def precond_kernel(pick, *refs):
    chunks, (precond, outgoing) = refs[:-2], refs[-2:]
    layers = precond.shape[0]
    step = 0
    for chunk in chunks:
        for place in range(chunk.shape[1]):
            for side in range(2):
                layer = layers // 2 - 1 - step if side == 0 else layers // 2 + step
                grad = chunk[0, place, 0, side]
                illum = chunk[0, place, 1, side]
                for other in range(1, chunk.shape[0]):
                    grad = grad + chunk[other, place, 0, side]
                    illum = illum + chunk[other, place, 1, side]
                precond[layer] = grad / jnp.sqrt(illum + 1.0)
            step += 1

    @pl.loop(0, outgoing.shape[0])
    def _(slot):
        outgoing[slot] = precond[pick[slot]]


def deliver_kernel(slots, incoming, out):
    @pl.loop(0, out.shape[2])
    def _(number):
        out[0, 0, number] = incoming[slots[number]]


def smem():
    return pl.BlockSpec(memory_space=pltpu.SMEM)


def vmem():
    return pl.BlockSpec(memory_space=pltpu.VMEM)


def plane_scratch(*lead, rows):
    return pltpu.VMEM(lead + (2, rows, HALF), jnp.float32)


def compiler_params(mebibytes):
    return pltpu.CompilerParams(vmem_limit_bytes=mebibytes * 1024 * 1024)


def light():
    return pl.CostEstimate(flops=1000, bytes_accessed=1000, transcendentals=0)


def in_hbm(array):
    return pltpu.with_memory_space_constraint(array, pltpu.HBM)


def hbm(*shape):
    return pltpu.HBM(shape, jnp.float32)


def state(groups, rows):
    return (
        hbm(groups, 2, 2, 2, 2, rows, HALF),
        pl.BlockSpec((1, 2, 2, 2, 2, rows, HALF), lambda g: (g, 0, 0, 0, 0, 0, 0)),
    )


def sent(groups, rows):
    return (
        hbm(2, groups, 4, 2, rows, HALF),
        pl.BlockSpec((2, 1, 4, 2, rows, HALF), lambda g: (0, g, 0, 0, 0, 0)),
    )


def sums(bands, rows, columns):
    shape = (bands, 2, 2, 2, rows // bands, columns)
    return hbm(*shape), pl.BlockSpec(shape, lambda g: (0,) * 6)


def split(pairs):
    return dict(out_shape=[p[0] for p in pairs], out_specs=[p[1] for p in pairs])


def layer_specs(sources, own):
    rows = sources.shape[3]
    return (
        [pl.BlockSpec((1, 4, 1, rows, HALF), lambda g, h=h: (g, 0, own, 0, h)) for h in range(2)],
        [pl.BlockSpec((1, rows, HALF), lambda g, h=h: (own, 0, h)) for h in range(2)],
    )


def first_edges(freq, sources, slowness):
    groups, _, _, rows, _ = sources.shape
    anywhere = pl.BlockSpec(memory_space=pl.ANY)
    return pl.pallas_call(
        first_kernel,
        in_specs=[smem(), anywhere, anywhere],
        out_specs=vmem(),
        out_shape=hbm(4 * groups + 1, 2, rows, HALF),
        scratch_shapes=[
            pltpu.VMEM((2, groups, 4, rows, HALF), jnp.float32),
            plane_scratch(rows=rows),
            plane_scratch(groups, 2, rows=rows),
            pltpu.SemaphoreType.DMA((2, 2)),
        ],
        compiler_params=compiler_params(8),
        cost_estimate=light(),
        name="first",
    )(freq, in_hbm(sources), in_hbm(slowness))


def later_edges(freq, sources, slowness):
    groups, _, layers, rows, _ = sources.shape
    sources, slowness = in_hbm(sources), in_hbm(slowness)
    operands, specs = [freq], [smem()]
    for side in range(2):
        parts = [layer_specs(sources, at if side == 0 else layers - 1 - at) for at in range(3)]
        for what, array in enumerate((sources, slowness)):
            for part in parts:
                operands += [array] * 2
                specs += part[what]
    everything = (
        hbm(groups, 13, 2, rows, HALF),
        pl.BlockSpec((1, 13, 2, rows, HALF), lambda g: (g, 0, 0, 0, 0)),
    )
    return pl.pallas_call(
        edge_kernel,
        grid=(groups,),
        in_specs=specs,
        **split([everything, sent(groups, rows), state(groups, rows)]),
        scratch_shapes=[
            plane_scratch(2, 3, 2, rows=rows),
            plane_scratch(2, 2, 3, 2, rows=rows),
            plane_scratch(2, rows=rows),
            plane_scratch(2, 3, 2, 2, rows=rows),
        ],
        compiler_params=compiler_params(32),
        cost_estimate=light(),
        name="edges",
    )(*operands)


def core_spec(rows, count, place):
    return pl.BlockSpec((1, count, 2, rows, HALF), lambda g: (g, place, 0, 0, 0))


def inner(freq, sources, slowness, from_core, from_chip, second, bands):
    groups, _, layers, rows, columns = sources.shape
    half = [
        pl.BlockSpec((1, 4, layers, rows, HALF), lambda g, h=h: (g, 0, 0, 0, h)) for h in range(2)
    ]
    slow = [pl.BlockSpec((layers, rows, HALF), lambda g, h=h: (0, 0, h)) for h in range(2)]
    chip = [
        pl.BlockSpec((4, 2, rows, HALF), lambda g: (g, 0, 0, 0)),
        pl.BlockSpec((1, 2, rows, HALF), lambda g: (4 * groups, 0, 0, 0)),
    ]
    core = [core_spec(rows, 4, 0), core_spec(rows, 1, 12)]
    sources, slowness = in_hbm(sources), in_hbm(slowness)
    return pl.pallas_call(
        inner_kernel,
        grid=(groups,),
        in_specs=[smem()] + half + slow + core + chip + [state(groups, rows)[1]],
        **split([sums(bands, rows, columns)] + [state(groups, rows)] * 4),
        scratch_shapes=[
            plane_scratch(layers, 2, rows=rows),
            plane_scratch(2, 2, rows=rows),
            plane_scratch(2, layers, 2, rows=rows),
            plane_scratch(2, layers, 2, rows=rows),
            plane_scratch(2, layers, 2, rows=rows),
            plane_scratch(2, layers - 2, 2, rows=rows),
            plane_scratch(2, 4, rows=rows),
            plane_scratch(2, rows=rows),
            plane_scratch(2, 2, 2, 2, rows=rows),
            plane_scratch(2, 2, 2, rows=rows),
            plane_scratch(2, 2, 2, rows=rows),
        ],
        compiler_params=compiler_params(40),
        cost_estimate=light(),
        name="inner",
    )(
        freq, sources, sources, slowness, slowness,
        from_core, from_core, from_chip, from_chip, in_hbm(second),
    )


def outer(freq, from_core, from_chip, held, bands, rows, columns):
    groups = from_core.shape[0]
    return pl.pallas_call(
        outer_kernel,
        grid=(groups,),
        in_specs=[smem(), core_spec(rows, 4, 1), core_spec(rows, 4, 2), sent(groups, rows)[1]]
        + [state(groups, rows)[1]] * 4,
        **split([sums(bands, rows, columns)]),
        scratch_shapes=[
            plane_scratch(2, 2, 4, rows=rows),
            plane_scratch(2, 2, 2, rows=rows),
            plane_scratch(2, 2, 2, 2, rows=rows),
            plane_scratch(2, 2, 2, rows=rows),
        ],
        compiler_params=compiler_params(32),
        cost_estimate=light(),
        name="outer",
    )(freq, from_core, from_core, from_chip, *[in_hbm(array) for array in held])[0]


def route(coverage, own_index):
    lists = coverage[0]
    owner, local = lists // TPD, lists % TPD
    position = jnp.arange(lists.shape[1], dtype=jnp.int32)
    same_owner = owner[:, :, None] == owner[:, None, :]
    earlier = position[None, :] < position[:, None]
    rank = jnp.sum((same_owner & earlier[None]).astype(jnp.int32), axis=2)
    slots = jnp.arange(CAP, dtype=jnp.int32)
    hit = (owner == own_index)[:, :, None] & (rank[:, :, None] == slots[None, None, :])
    pick = jnp.sum(jnp.where(hit, local[:, :, None], 0), axis=1).reshape(-1)
    own_slots = owner * CAP + rank
    return pick, lax.dynamic_index_in_dim(own_slots, own_index, 0, keepdims=False)


def body(sources, slowness, freq_index, coverage):
    groups, _, layers, rows, columns = sources.shape
    bands, members = lax.axis_size("freq"), lax.axis_size("sub")
    own_index = lax.axis_index("sub")
    cores = [(i, i ^ 1) for i in range(members)]
    chips = [(i, i + step) for i in range(members) for step in (2 * (i % 2) - 1,) if 0 <= i + step < members]
    near_chip = lax.ppermute(first_edges(freq_index, sources, slowness), "sub", chips)
    everything, far, second = later_edges(freq_index, sources, slowness)
    far_chip = lax.ppermute(far, "sub", chips)
    core = lax.ppermute(everything, "sub", cores)
    pick, slots = route(coverage, own_index)

    def spread(chunk):
        return lax.all_to_all(chunk, "freq", split_axis=0, concat_axis=0, tiled=True)

    chunk, *held = inner(freq_index, sources, slowness, core, near_chip, second, bands)
    chunks = [spread(chunk)]
    chunk = outer(freq_index, core, far_chip, held, bands, rows, columns)
    chunks[0], chunk = lax.optimization_barrier((chunks[0], chunk))
    chunks.append(spread(chunk))
    depth = rows // bands
    precond, outgoing = pl.pallas_call(
        precond_kernel,
        in_specs=[smem()] + [vmem()] * len(chunks),
        out_specs=[vmem()] * 2,
        out_shape=[
            jax.ShapeDtypeStruct((layers, depth, columns), jnp.float32),
            jax.ShapeDtypeStruct((members * CAP, depth, columns), jnp.float32),
        ],
        compiler_params=compiler_params(12),
        name="precond",
    )(pick, *chunks)
    incoming = lax.all_to_all(outgoing, "sub", split_axis=0, concat_axis=0, tiled=True)
    delivered = pl.pallas_call(
        deliver_kernel,
        in_specs=[smem(), vmem()],
        out_specs=vmem(),
        out_shape=jax.ShapeDtypeStruct((1, 1, coverage.shape[2], depth, columns), jnp.float32),
        compiler_params=compiler_params(12),
        name="deliver",
    )(slots, incoming)
    return precond, delivered


def solution(mesh):
    placed = (
        P("freq", None, "sub", None, None),
        P("sub", None, None),
        P("freq"),
        P("freq", None, None),
    )
    return jax.shard_map(
        body,
        mesh=mesh,
        in_specs=placed,
        out_specs=(P("sub", "freq", None), P("freq", "sub", None, None, None)),
        check_vma=False,
    )
```

```python
import functools

import jax
import jax.numpy as jnp
from jax import lax
from jax.experimental import pallas as pl
from jax.experimental.pallas import tpu as pltpu
from jax.sharding import PartitionSpec as P

TPD = 8
CAP = 2
HALF = 128


def masks():
    lane = lax.broadcasted_iota(jnp.int32, (8, HALF), 1)
    row = lax.broadcasted_iota(jnp.int32, (8, HALF), 0)
    return lane == 0, lane == HALF - 1, row == 0, row == 7


def turn(real, imag, coef_real, coef_imag):
    return real * coef_real + imag * coef_imag, imag * coef_real - real * coef_imag


def coefficients(store, slow, scale, factor, nk):
    for k in range(nk):
        for h in range(2):
            sigma = scale * slow(h, k)
            diag = 0.875 - sigma
            inverse = factor / (diag * diag + sigma * sigma)
            store(0, h, k, diag * inverse)
            store(1, h, k, sigma * inverse)


def relax(store, force, near, coef, marks, nk, base=None):
    lane_first, lane_last, row_first, row_last = marks

    def across(c, h, k):
        before, middle, after = [None if layer is None else layer(c, h, k) for layer in near]
        parts = [part for part in (before, after) if part is not None]
        if middle is not None:
            parts.append(middle + middle)
        return functools.reduce(lambda total, part: total + part, parts)

    both = [(c, h) for c in range(2) for h in range(2)]
    top = {at: across(*at, 0) for at in both}
    bottom = {at: across(*at, nk - 1) for at in both}
    here = top
    pair = {at: jnp.where(row_first, 0.0, pltpu.roll(bottom[at], 1, 0)) + top[at] for at in both}
    for k in range(nk):
        if k < nk - 2:
            following = {at: across(*at, k + 1) for at in both}
        elif k == nk - 2:
            following = bottom
        else:
            following = {at: jnp.where(row_last, 0.0, pltpu.roll(top[at], 7, 0)) for at in both}
        terms = []
        for c in range(2):
            depth = []
            for h in range(2):
                later = here[c, h] + following[c, h]
                depth.append(pair[c, h] + later)
                pair[c, h] = later
            left, right = depth
            left_up, right_up = pltpu.roll(left, HALF - 1, 1), pltpu.roll(right, HALF - 1, 1)
            left_down, right_down = pltpu.roll(left, 1, 1), pltpu.roll(right, 1, 1)
            left_sides = jnp.where(lane_last, right_up, left_up) + jnp.where(lane_first, 0.0, left_down)
            right_sides = jnp.where(lane_last, 0.0, right_up) + jnp.where(
                lane_first, left_down, right_down
            )
            for h, (middle, ends) in enumerate(((left, left_sides), (right, right_sides))):
                total = ends + (middle + middle)
                if near[1] is not None:
                    total = total - 8.0 * near[1](c, h, k)
                terms.append(total if force is None else force(c, h, k) + total)
        here = following
        for h in range(2):
            planes = turn(terms[h], terms[2 + h], coef(0, h, k), coef(1, h, k))
            for c in range(2):
                store(c, h, k, planes[c] if base is None else base(c, h, k) + planes[c])


def piece_of(ref, lead):
    return lambda c, h, k: ref[lead + (c, h, pl.ds(8 * k, 8), slice(None))]


def row_piece(refs, lead, offset, tail, nk):
    return lambda c, h, k: refs[h][
        lead + (offset + c,) + tail + (pl.ds(k, 8, stride=nk), slice(None))
    ]


def store_to(*places):
    def store(c, h, k, piece):
        for ref, lead in places:
            ref[lead + (c, h, pl.ds(8 * k, 8), slice(None))] = piece

    return store


def start_layer(store, force, coef, nk):
    for k in range(nk):
        for h in range(2):
            planes = turn(force(0, h, k), force(1, h, k), coef(0, h, k), coef(1, h, k))
            for c in range(2):
                store(c, h, k, planes[c])


def products(last, acc, place, weight, first, nk):
    for side in range(2):
        forward, adjoint = [piece_of(last, (side, pair)) for pair in range(2)]
        for h in range(2):
            for k in range(nk):
                fr, fi = forward(0, h, k), forward(1, h, k)
                ar, ai = adjoint(0, h, k), adjoint(1, h, k)
                terms = (weight * (fr * ar - fi * ai), weight * (fr * fr + fi * fi))
                for number, term in enumerate(terms):
                    at = (place, number, side, h, pl.ds(k, 8, stride=nk), slice(None))
                    acc[at] = jnp.where(first, term, acc[at] + term)


def write_out(out, acc, offset):
    bands, _, _, _, depth, _ = out.shape
    for band in range(bands):
        for place in range(acc.shape[0]):
            for number in range(2):
                for side in range(2):
                    for h in range(2):
                        out[band, offset + place, number, side, :, pl.ds(h * HALF, HALF)] = acc[
                            place, number, side, h, pl.ds(band * depth, depth), :
                        ]


def scale_of(freq, group):
    weight = 1.0 + freq[group].astype(jnp.float32) / 16.0
    return weight, 0.12 * weight


def parity():
    return lax.axis_index("sub") % 2


def paired(side):
    index = lax.axis_index("sub")
    there = index > 0 if side == 0 else index < lax.axis_size("sub") - 1
    return jnp.where(there, 1.0 / 64.0, 0.0)


def first_kernel(freq, sources, slowness, to_chip, to_core, raw, slow, coef, sems):
    groups, _, layers, rows = sources.shape[:4]
    nk = rows // 8
    places = (parity() * (layers - 1), (1 - parity()) * (layers - 1))
    copies = []
    for side, own in enumerate(places):
        for h in range(2):
            lanes = pl.ds(h * HALF, HALF)
            pairs = ((slowness.at[own, :, lanes], slow), (sources.at[:, :, own, :, lanes], raw))
            for number, (ref, held) in enumerate(pairs):
                copies.append(
                    pltpu.make_async_copy(ref, held.at[side, h], sems.at[side, h, number])
                )
    for copy in copies:
        copy.start()
    for side, out in enumerate((to_chip, to_core)):
        for copy in copies[4 * side : 4 * side + 4]:
            copy.wait()

        def sigma(h, k):
            return slow[side, h, pl.ds(k, 8, stride=nk), :]

        for h in range(2):
            for k in range(nk):
                out[4 * groups, h, pl.ds(8 * k, 8), :] = sigma(h, k)
        for group in range(groups):
            scale = scale_of(freq, group)[1]
            coefficients(store_to((coef, (side, group))), sigma, scale, 1.0 / 64.0, nk)
            for pair in range(2):
                start_layer(
                    store_from(out, (), 4 * group + 2 * pair),
                    row_piece((raw.at[side, 0], raw.at[side, 1]), (group,), 2 * pair, (), nk),
                    piece_of(coef, (side, group)),
                    nk,
                )


def store_from(ref, lead, offset):
    def store(c, h, k, piece):
        ref[lead + (offset + c, h, pl.ds(8 * k, 8), slice(None))] = piece

    return store


def sent_piece(ref, lead, offset):
    return lambda c, h, k: ref[lead + (offset + c, h, pl.ds(8 * k, 8), slice(None))]


def edge_kernel(freq, *refs):
    sides = []
    for side in range(2):
        part = refs[12 * side : 12 * side + 12]
        sides.append([[part[at + 2 * n : at + 2 * n + 2] for n in range(3)] for at in (0, 6)])
    far_chip, far_core, second, coef, one, fields = refs[24:]
    group = pl.program_id(0)
    rows = sides[0][1][0][0].shape[-2]
    nk = rows // 8
    marks = masks()
    scale = scale_of(freq, group)[1]
    chains = [(side, pair) for side in range(2) for pair in range(2)]

    def force(side, pair, at):
        return row_piece(sides[side][0][at], (0,), 2 * pair, (0,), nk)

    for side in range(2):
        for at in range(3):
            slows = sides[side][1][at]
            coefficients(
                store_to((coef, (side, at))),
                lambda h, k, slows=slows: slows[h][0, pl.ds(k, 8, stride=nk), :],
                scale,
                1.0 / 64.0,
                nk,
            )
            for pair in range(2):
                start_layer(
                    store_to((one, (side, pair, at))),
                    force(side, pair, at),
                    piece_of(coef, (side, at)),
                    nk,
                )
    for at in range(2):
        for side, pair in chains:
            near = [piece_of(one, (side, pair, n)) if n >= 0 else None for n in (at - 1, at, at + 1)]
            target = (fields, (side, 0, pair)) if at == 0 else (second, (0, pair, side))
            relax(
                store_to(target), force(side, pair, at), near, piece_of(coef, (side, at)), marks, nk
            )
    for side, pair in chains:
        near = [None, piece_of(fields, (side, 0, pair)), piece_of(second, (0, pair, side))]
        relax(
            store_to((fields, (side, 1, pair))),
            force(side, pair, 0),
            near,
            piece_of(coef, (side, 0)),
            marks,
            nk,
        )
    for out, side in ((far_chip, parity()), (far_core, 1 - parity())):
        for level in range(2):
            for pair in range(2):
                for c in range(2):
                    out[level, 0, 2 * pair + c] = fields[side, level, pair, c]


def inner_kernel(
    freq, src_l, src_r, slow_l, slow_r, core_field, core_slow, chip_field, chip_slow, second,
    out, base_three, base_next, base_four, factors,
    coef, beyond, one, force, two, three, halo, halo_slow, change, last, acc,
):
    group = pl.program_id(0)
    groups = pl.num_programs(0)
    layers, rows = src_l.shape[2], src_l.shape[3]
    nk = rows // 8
    marks = masks()
    weight, scale = scale_of(freq, group)
    weight = weight * 4096.0
    sources, slows = (src_l, src_r), (slow_l, slow_r)
    chains = [(side, pair) for side in range(2) for pair in range(2)]
    to_chip, to_core = parity(), 1 - parity()
    halo[to_core] = core_field[...]
    halo[to_chip] = chip_field[...]
    halo_slow[to_core] = core_slow[0]
    halo_slow[to_chip] = chip_slow[0]

    @pl.loop(0, layers)
    def _(layer):
        coefficients(
            store_to((coef, (layer,))),
            lambda h, k: slows[h][layer, pl.ds(k, 8, stride=nk), :],
            scale,
            1.0 / 64.0,
            nk,
        )
        for pair in range(2):
            rows_of = row_piece(sources, (0,), 2 * pair, (layer,), nk)
            keep = store_to((force, (pair, layer)))
            for c in range(2):
                for h in range(2):
                    for k in range(nk):
                        keep(c, h, k, rows_of(c, h, k))
            start_layer(store_to((one, (pair, layer))), rows_of, piece_of(coef, (layer,)), nk)

    for side in range(2):
        coefficients(
            store_to((beyond, (side,))),
            lambda h, k, side=side: halo_slow[side, h, pl.ds(8 * k, 8), :],
            scale,
            paired(side),
            nk,
        )
    for side, pair in chains:
        given = piece_of(second, (0, pair, side))
        keep = store_to((two, (pair, 1 if side == 0 else layers - 2)))
        for c in range(2):
            for h in range(2):
                for k in range(nk):
                    keep(c, h, k, given(c, h, k))

    def step(targets, pair, layer, near):
        relax(
            store_to(*targets),
            piece_of(force, (pair, layer)),
            near,
            piece_of(coef, (layer,)),
            marks,
            nk,
        )

    def around(ref, pair, layer, skip):
        return [piece_of(ref, (pair, layer + shift - skip)) for shift in (-1, 0, 1)]

    for side, pair in chains:
        layer = side * (layers - 1)
        near = [
            sent_piece(halo, (side,), 2 * pair),
            piece_of(one, (pair, layer)),
            piece_of(one, (pair, layer + 1 - 2 * side)),
        ]
        step(((two, (pair, layer)),), pair, layer, near)
    for side, pair in chains:
        near = [None, None, piece_of(one, (pair, side * (layers - 1)))]
        relax(
            store_to((change, (0, side, pair))), None, near, piece_of(beyond, (side,)), marks, nk
        )

    @pl.loop(0, (layers - 4) // 2)
    def _(turn_at):
        for offset in range(2):
            layer = 2 + 2 * turn_at + offset
            for pair in range(2):
                step(((two, (pair, layer)),), pair, layer, around(one, pair, layer, 0))

    for side, pair in chains:
        near = [
            None,
            piece_of(change, (0, side, pair)),
            piece_of(two, (pair, side * (layers - 1))),
        ]
        relax(
            store_to((change, (1, side, pair))),
            None,
            near,
            piece_of(beyond, (side,)),
            marks,
            nk,
        )

    @pl.loop(0, (layers - 2) // 2)
    def _(turn_at):
        for offset in range(2):
            layer = 1 + 2 * turn_at + offset
            for pair in range(2):
                step(((three, (pair, layer - 1)),), pair, layer, around(two, pair, layer, 0))

    def layer_at(side, at):
        return at if side == 0 else layers - 1 - at

    for side in range(2):
        for at in range(2):
            given = piece_of(coef, (layer_at(side, at),))
            keep = store_to((factors, (0, side, at)))
            for c in range(2):
                for h in range(2):
                    for k in range(nk):
                        keep(c, h, k, given(c, h, k))
    for side, pair in chains:
        twos = [piece_of(two, (pair, layer_at(side, at))) for at in range(2)]
        threes = [piece_of(three, (pair, layer_at(side, at) - 1)) for at in (1, 2)]
        changes = [piece_of(change, (number, side, pair)) for number in range(2)]
        for target, at, near in (
            (base_three, 0, [changes[0], *twos]),
            (base_next, 1, [None, *threes]),
            (base_four, 0, [changes[1], None, threes[0]]),
        ):
            step(((target, (0, pair, side)),), pair, layer_at(side, at), near)

    @pl.loop(0, 2)
    def _(place):
        for side, pair in chains:
            layer = layers // 2 - 1 + side + (2 * side - 1) * place
            step(((last, (side, pair)),), pair, layer, around(three, pair, layer, 1))
        products(last, acc, place, weight, group == 0, nk)

    @pl.when(group == groups - 1)
    def _():
        write_out(out, acc, 0)


def outer_kernel(freq, core, chip, base_three, base_next, base_four, factors, out, sent_fields, fresh, last, acc):
    group = pl.program_id(0)
    groups = pl.num_programs(0)
    rows = base_three.shape[-2]
    nk = rows // 8
    marks = masks()
    weight = scale_of(freq, group)[0] * 4096.0
    chains = [(side, pair) for side in range(2) for pair in range(2)]
    to_chip, to_core = parity(), 1 - parity()
    for number in range(2):
        sent_fields[to_core, number] = core[number, 0]
        sent_fields[to_chip, number] = chip[number, 0]

    def step(target, base, side, pair, at, near):
        relax(
            store_to(target),
            None,
            near,
            piece_of(factors, (0, side, at)),
            marks,
            nk,
            base=piece_of(base, (0, pair, side)),
        )

    for side, pair in chains:
        near = [sent_piece(sent_fields, (side, 0), 2 * pair), None, None]
        step((fresh, (side, pair)), base_three, side, pair, 0, near)
    for side, pair in chains:
        near = [piece_of(fresh, (side, pair)), None, None]
        step((last, (0, side, pair)), base_next, side, pair, 1, near)
    for side, pair in chains:
        near = [sent_piece(sent_fields, (side, 1), 2 * pair), piece_of(fresh, (side, pair)), None]
        step((last, (1, side, pair)), base_four, side, pair, 0, near)
    for place in range(2):
        products(last.at[place], acc, place, weight, group == 0, nk)

    @pl.when(group == groups - 1)
    def _():
        write_out(out, acc, 0)


def precond_kernel(pick, *refs):
    chunks, (precond, outgoing) = refs[:-2], refs[-2:]
    layers = precond.shape[0]
    step = 0
    for chunk in chunks:
        for place in range(chunk.shape[1]):
            for side in range(2):
                layer = layers // 2 - 1 - step if side == 0 else layers // 2 + step
                grad = chunk[0, place, 0, side]
                illum = chunk[0, place, 1, side]
                for other in range(1, chunk.shape[0]):
                    grad = grad + chunk[other, place, 0, side]
                    illum = illum + chunk[other, place, 1, side]
                precond[layer] = grad / jnp.sqrt(illum + 1.0)
            step += 1

    @pl.loop(0, outgoing.shape[0])
    def _(slot):
        outgoing[slot] = precond[pick[slot]]


def deliver_kernel(slots, incoming, out):
    @pl.loop(0, out.shape[2])
    def _(number):
        out[0, 0, number] = incoming[slots[number]]


def smem():
    return pl.BlockSpec(memory_space=pltpu.SMEM)


def vmem():
    return pl.BlockSpec(memory_space=pltpu.VMEM)


def plane_scratch(*lead, rows):
    return pltpu.VMEM(lead + (2, rows, HALF), jnp.float32)


def compiler_params(mebibytes):
    return pltpu.CompilerParams(vmem_limit_bytes=mebibytes * 1024 * 1024)


def light():
    return pl.CostEstimate(flops=1000, bytes_accessed=1000, transcendentals=0)


def in_hbm(array):
    return pltpu.with_memory_space_constraint(array, pltpu.HBM)


def hbm(*shape):
    return pltpu.HBM(shape, jnp.float32)


def state(groups, rows):
    return (
        hbm(groups, 2, 2, 2, 2, rows, HALF),
        pl.BlockSpec((1, 2, 2, 2, 2, rows, HALF), lambda g: (g, 0, 0, 0, 0, 0, 0)),
    )


def sent(groups, rows):
    return (
        hbm(2, groups, 4, 2, rows, HALF),
        pl.BlockSpec((2, 1, 4, 2, rows, HALF), lambda g: (0, g, 0, 0, 0, 0)),
    )


def sums(bands, rows, columns):
    shape = (bands, 2, 2, 2, rows // bands, columns)
    return hbm(*shape), pl.BlockSpec(shape, lambda g: (0,) * 6)


def split(pairs):
    return dict(out_shape=[p[0] for p in pairs], out_specs=[p[1] for p in pairs])


def layer_specs(sources, own):
    rows = sources.shape[3]
    return (
        [pl.BlockSpec((1, 4, 1, rows, HALF), lambda g, h=h: (g, 0, own, 0, h)) for h in range(2)],
        [pl.BlockSpec((1, rows, HALF), lambda g, h=h: (own, 0, h)) for h in range(2)],
    )


def first_edges(freq, sources, slowness):
    groups, _, _, rows, _ = sources.shape
    anywhere = pl.BlockSpec(memory_space=pl.ANY)
    return pl.pallas_call(
        first_kernel,
        in_specs=[smem(), anywhere, anywhere],
        out_specs=[vmem()] * 2,
        out_shape=[hbm(4 * groups + 1, 2, rows, HALF)] * 2,
        scratch_shapes=[
            pltpu.VMEM((2, 2, groups, 4, rows, HALF), jnp.float32),
            plane_scratch(2, rows=rows),
            plane_scratch(2, groups, 2, rows=rows),
            pltpu.SemaphoreType.DMA((2, 2, 2)),
        ],
        compiler_params=compiler_params(8),
        cost_estimate=light(),
        name="first",
    )(freq, in_hbm(sources), in_hbm(slowness))


def later_edges(freq, sources, slowness):
    groups, _, layers, rows, _ = sources.shape
    sources, slowness = in_hbm(sources), in_hbm(slowness)
    operands, specs = [freq], [smem()]
    for side in range(2):
        parts = [layer_specs(sources, at if side == 0 else layers - 1 - at) for at in range(3)]
        for what, array in enumerate((sources, slowness)):
            for part in parts:
                operands += [array] * 2
                specs += part[what]
    return pl.pallas_call(
        edge_kernel,
        grid=(groups,),
        in_specs=specs,
        **split([sent(groups, rows)] * 2 + [state(groups, rows)]),
        scratch_shapes=[
            plane_scratch(2, 3, 2, rows=rows),
            plane_scratch(2, 2, 3, 2, rows=rows),
            plane_scratch(2, 2, 2, 2, rows=rows),
        ],
        compiler_params=compiler_params(32),
        cost_estimate=light(),
        name="edges",
    )(*operands)


def inner(freq, sources, slowness, from_core, from_chip, second, bands):
    groups, _, layers, rows, columns = sources.shape
    half = [
        pl.BlockSpec((1, 4, layers, rows, HALF), lambda g, h=h: (g, 0, 0, 0, h)) for h in range(2)
    ]
    slow = [pl.BlockSpec((layers, rows, HALF), lambda g, h=h: (0, 0, h)) for h in range(2)]
    near = [
        pl.BlockSpec((4, 2, rows, HALF), lambda g: (g, 0, 0, 0)),
        pl.BlockSpec((1, 2, rows, HALF), lambda g: (4 * groups, 0, 0, 0)),
    ]
    sources, slowness = in_hbm(sources), in_hbm(slowness)
    return pl.pallas_call(
        inner_kernel,
        grid=(groups,),
        in_specs=[smem()] + half + slow + near * 2 + [state(groups, rows)[1]],
        **split([sums(bands, rows, columns)] + [state(groups, rows)] * 4),
        scratch_shapes=[
            plane_scratch(layers, 2, rows=rows),
            plane_scratch(2, 2, rows=rows),
            plane_scratch(2, layers, 2, rows=rows),
            plane_scratch(2, layers, 2, rows=rows),
            plane_scratch(2, layers, 2, rows=rows),
            plane_scratch(2, layers - 2, 2, rows=rows),
            plane_scratch(2, 4, rows=rows),
            plane_scratch(2, rows=rows),
            plane_scratch(2, 2, 2, 2, rows=rows),
            plane_scratch(2, 2, 2, rows=rows),
            plane_scratch(2, 2, 2, rows=rows),
        ],
        compiler_params=compiler_params(40),
        cost_estimate=light(),
        name="inner",
    )(
        freq, sources, sources, slowness, slowness,
        from_core, from_core, from_chip, from_chip, in_hbm(second),
    )


def outer(freq, from_core, from_chip, held, bands, rows, columns):
    groups = from_core.shape[1]
    return pl.pallas_call(
        outer_kernel,
        grid=(groups,),
        in_specs=[smem()] + [sent(groups, rows)[1]] * 2 + [state(groups, rows)[1]] * 4,
        **split([sums(bands, rows, columns)]),
        scratch_shapes=[
            plane_scratch(2, 2, 4, rows=rows),
            plane_scratch(2, 2, 2, rows=rows),
            plane_scratch(2, 2, 2, 2, rows=rows),
            plane_scratch(2, 2, 2, rows=rows),
        ],
        compiler_params=compiler_params(32),
        cost_estimate=light(),
        name="outer",
    )(freq, from_core, from_chip, *[in_hbm(array) for array in held])[0]


def route(coverage, own_index):
    lists = coverage[0]
    owner, local = lists // TPD, lists % TPD
    position = jnp.arange(lists.shape[1], dtype=jnp.int32)
    same_owner = owner[:, :, None] == owner[:, None, :]
    earlier = position[None, :] < position[:, None]
    rank = jnp.sum((same_owner & earlier[None]).astype(jnp.int32), axis=2)
    slots = jnp.arange(CAP, dtype=jnp.int32)
    hit = (owner == own_index)[:, :, None] & (rank[:, :, None] == slots[None, None, :])
    pick = jnp.sum(jnp.where(hit, local[:, :, None], 0), axis=1).reshape(-1)
    own_slots = owner * CAP + rank
    return pick, lax.dynamic_index_in_dim(own_slots, own_index, 0, keepdims=False)


def body(sources, slowness, freq_index, coverage):
    groups, _, layers, rows, columns = sources.shape
    bands, members = lax.axis_size("freq"), lax.axis_size("sub")
    own_index = lax.axis_index("sub")
    cores = [(i, i ^ 1) for i in range(members)]
    chips = [(i, i + step) for i in range(members) for step in (2 * (i % 2) - 1,) if 0 <= i + step < members]
    def exchange(to_chip, to_core):
        return lax.ppermute(to_chip, "sub", chips), lax.ppermute(to_core, "sub", cores)

    near_chip, near_core = exchange(*first_edges(freq_index, sources, slowness))
    *edges, second = later_edges(freq_index, sources, slowness)
    far_chip, far_core = exchange(*edges)
    pick, slots = route(coverage, own_index)

    def spread(chunk):
        return lax.all_to_all(chunk, "freq", split_axis=0, concat_axis=0, tiled=True)

    chunk, *held = inner(freq_index, sources, slowness, near_core, near_chip, second, bands)
    chunks = [spread(chunk)]
    chunk = outer(freq_index, far_core, far_chip, held, bands, rows, columns)
    chunks[0], chunk = lax.optimization_barrier((chunks[0], chunk))
    chunks.append(spread(chunk))
    depth = rows // bands
    precond, outgoing = pl.pallas_call(
        precond_kernel,
        in_specs=[smem()] + [vmem()] * len(chunks),
        out_specs=[vmem()] * 2,
        out_shape=[
            jax.ShapeDtypeStruct((layers, depth, columns), jnp.float32),
            jax.ShapeDtypeStruct((members * CAP, depth, columns), jnp.float32),
        ],
        compiler_params=compiler_params(12),
        name="precond",
    )(pick, *chunks)
    incoming = lax.all_to_all(outgoing, "sub", split_axis=0, concat_axis=0, tiled=True)
    delivered = pl.pallas_call(
        deliver_kernel,
        in_specs=[smem(), vmem()],
        out_specs=vmem(),
        out_shape=jax.ShapeDtypeStruct((1, 1, coverage.shape[2], depth, columns), jnp.float32),
        compiler_params=compiler_params(12),
        name="deliver",
    )(slots, incoming)
    return precond, delivered


def solution(mesh):
    placed = (
        P("freq", None, "sub", None, None),
        P("sub", None, None),
        P("freq"),
        P("freq", None, None),
    )
    return jax.shard_map(
        body,
        mesh=mesh,
        in_specs=placed,
        out_specs=(P("sub", "freq", None), P("freq", "sub", None, None, None)),
        check_vma=False,
    )
```

```python
import functools

import jax
import jax.numpy as jnp
from jax import lax
from jax.experimental import pallas as pl
from jax.experimental.pallas import tpu as pltpu
from jax.sharding import PartitionSpec as P

TPD = 8
CAP = 2
HALF = 128


def masks():
    lane = lax.broadcasted_iota(jnp.int32, (8, HALF), 1)
    row = lax.broadcasted_iota(jnp.int32, (8, HALF), 0)
    return lane == 0, lane == HALF - 1, row == 0, row == 7


def turn(real, imag, coef_real, coef_imag):
    return real * coef_real + imag * coef_imag, imag * coef_real - real * coef_imag


def coefficients(store, slow, scale, factor, nk):
    for k in range(nk):
        for h in range(2):
            sigma = scale * slow(h, k)
            diag = 0.875 - sigma
            inverse = factor / (diag * diag + sigma * sigma)
            store(0, h, k, diag * inverse)
            store(1, h, k, sigma * inverse)


def relax(store, force, near, coef, marks, nk, base=None):
    lane_first, lane_last, row_first, row_last = marks

    def across(c, h, k):
        before, middle, after = [None if layer is None else layer(c, h, k) for layer in near]
        parts = [part for part in (before, after) if part is not None]
        if middle is not None:
            parts.append(middle + middle)
        return functools.reduce(lambda total, part: total + part, parts)

    both = [(c, h) for c in range(2) for h in range(2)]
    top = {at: across(*at, 0) for at in both}
    bottom = {at: across(*at, nk - 1) for at in both}
    here = top
    pair = {at: jnp.where(row_first, 0.0, pltpu.roll(bottom[at], 1, 0)) + top[at] for at in both}
    for k in range(nk):
        if k < nk - 2:
            following = {at: across(*at, k + 1) for at in both}
        elif k == nk - 2:
            following = bottom
        else:
            following = {at: jnp.where(row_last, 0.0, pltpu.roll(top[at], 7, 0)) for at in both}
        terms = []
        for c in range(2):
            depth = []
            for h in range(2):
                later = here[c, h] + following[c, h]
                depth.append(pair[c, h] + later)
                pair[c, h] = later
            left, right = depth
            left_up, right_up = pltpu.roll(left, HALF - 1, 1), pltpu.roll(right, HALF - 1, 1)
            left_down, right_down = pltpu.roll(left, 1, 1), pltpu.roll(right, 1, 1)
            left_sides = jnp.where(lane_last, right_up, left_up) + jnp.where(lane_first, 0.0, left_down)
            right_sides = jnp.where(lane_last, 0.0, right_up) + jnp.where(
                lane_first, left_down, right_down
            )
            for h, (middle, ends) in enumerate(((left, left_sides), (right, right_sides))):
                total = ends + (middle + middle)
                if near[1] is not None:
                    total = total - 8.0 * near[1](c, h, k)
                terms.append(total if force is None else force(c, h, k) + total)
        here = following
        for h in range(2):
            planes = turn(terms[h], terms[2 + h], coef(0, h, k), coef(1, h, k))
            for c in range(2):
                store(c, h, k, planes[c] if base is None else base(c, h, k) + planes[c])


def piece_of(ref, lead):
    return lambda c, h, k: ref[lead + (c, h, pl.ds(8 * k, 8), slice(None))]


def row_piece(refs, lead, offset, tail, nk):
    return lambda c, h, k: refs[h][
        lead + (offset + c,) + tail + (pl.ds(k, 8, stride=nk), slice(None))
    ]


def store_to(*places):
    def store(c, h, k, piece):
        for ref, lead in places:
            ref[lead + (c, h, pl.ds(8 * k, 8), slice(None))] = piece

    return store


def start_layer(store, force, coef, nk):
    for k in range(nk):
        for h in range(2):
            planes = turn(force(0, h, k), force(1, h, k), coef(0, h, k), coef(1, h, k))
            for c in range(2):
                store(c, h, k, planes[c])


def products(last, acc, place, weight, first, nk):
    for side in range(2):
        forward, adjoint = [piece_of(last, (side, pair)) for pair in range(2)]
        for h in range(2):
            for k in range(nk):
                fr, fi = forward(0, h, k), forward(1, h, k)
                ar, ai = adjoint(0, h, k), adjoint(1, h, k)
                terms = (weight * (fr * ar - fi * ai), weight * (fr * fr + fi * fi))
                for number, term in enumerate(terms):
                    at = (place, number, side, h, pl.ds(k, 8, stride=nk), slice(None))
                    acc[at] = jnp.where(first, term, acc[at] + term)


def write_out(out, acc, offset):
    bands, _, _, _, depth, _ = out.shape
    for band in range(bands):
        for place in range(acc.shape[0]):
            for number in range(2):
                for side in range(2):
                    for h in range(2):
                        out[band, offset + place, number, side, :, pl.ds(h * HALF, HALF)] = acc[
                            place, number, side, h, pl.ds(band * depth, depth), :
                        ]


def scale_of(freq, group):
    weight = 1.0 + freq[group].astype(jnp.float32) / 16.0
    return weight, 0.12 * weight


def parity():
    return lax.axis_index("sub") % 2


def paired(side):
    index = lax.axis_index("sub")
    there = index > 0 if side == 0 else index < lax.axis_size("sub") - 1
    return jnp.where(there, 1.0 / 64.0, 0.0)


def first_kernel(freq, sources, slowness, to_chip, to_core, raw, slow, coef, sems):
    groups, _, layers, rows = sources.shape[:4]
    nk = rows // 8
    places = (parity() * (layers - 1), (1 - parity()) * (layers - 1))
    copies = []
    for side, own in enumerate(places):
        for h in range(2):
            lanes = pl.ds(h * HALF, HALF)
            pairs = ((slowness.at[own, :, lanes], slow), (sources.at[:, :, own, :, lanes], raw))
            for number, (ref, held) in enumerate(pairs):
                copies.append(
                    pltpu.make_async_copy(ref, held.at[side, h], sems.at[side, h, number])
                )
    for copy in copies:
        copy.start()
    for side, out in enumerate((to_chip, to_core)):
        for copy in copies[4 * side : 4 * side + 4]:
            copy.wait()

        def sigma(h, k):
            return slow[side, h, pl.ds(k, 8, stride=nk), :]

        for h in range(2):
            for k in range(nk):
                out[4 * groups, h, pl.ds(8 * k, 8), :] = sigma(h, k)
        for group in range(groups):
            scale = scale_of(freq, group)[1]
            coefficients(store_to((coef, (side, group))), sigma, scale, 1.0 / 64.0, nk)
            for pair in range(2):
                start_layer(
                    store_from(out, (), 4 * group + 2 * pair),
                    row_piece((raw.at[side, 0], raw.at[side, 1]), (group,), 2 * pair, (), nk),
                    piece_of(coef, (side, group)),
                    nk,
                )


def store_from(ref, lead, offset):
    def store(c, h, k, piece):
        ref[lead + (offset + c, h, pl.ds(8 * k, 8), slice(None))] = piece

    return store


def sent_piece(ref, lead, offset):
    return lambda c, h, k: ref[lead + (offset + c, h, pl.ds(8 * k, 8), slice(None))]


def edge_kernel(freq, *refs):
    sides = []
    for side in range(2):
        part = refs[12 * side : 12 * side + 12]
        sides.append([[part[at + 2 * n : at + 2 * n + 2] for n in range(3)] for at in (0, 6)])
    far_chip, far_core, second, coef, one, fields = refs[24:]
    group = pl.program_id(0)
    rows = sides[0][1][0][0].shape[-2]
    nk = rows // 8
    marks = masks()
    scale = scale_of(freq, group)[1]
    chains = [(side, pair) for side in range(2) for pair in range(2)]

    def force(side, pair, at):
        return row_piece(sides[side][0][at], (0,), 2 * pair, (0,), nk)

    for side in range(2):
        for at in range(3):
            slows = sides[side][1][at]
            coefficients(
                store_to((coef, (side, at))),
                lambda h, k, slows=slows: slows[h][0, pl.ds(k, 8, stride=nk), :],
                scale,
                1.0 / 64.0,
                nk,
            )
            for pair in range(2):
                start_layer(
                    store_to((one, (side, pair, at))),
                    force(side, pair, at),
                    piece_of(coef, (side, at)),
                    nk,
                )
    for at in range(2):
        for side, pair in chains:
            near = [piece_of(one, (side, pair, n)) if n >= 0 else None for n in (at - 1, at, at + 1)]
            target = (fields, (side, 0, pair)) if at == 0 else (second, (0, pair, side))
            relax(
                store_to(target), force(side, pair, at), near, piece_of(coef, (side, at)), marks, nk
            )
    for side, pair in chains:
        near = [None, piece_of(fields, (side, 0, pair)), piece_of(second, (0, pair, side))]
        relax(
            store_to((fields, (side, 1, pair))),
            force(side, pair, 0),
            near,
            piece_of(coef, (side, 0)),
            marks,
            nk,
        )
    for out, side in ((far_chip, parity()), (far_core, 1 - parity())):
        for level in range(2):
            for pair in range(2):
                for c in range(2):
                    out[level, 0, 2 * pair + c] = fields[side, level, pair, c]


def inner_kernel(
    freq, src_l, src_r, slow_l, slow_r, second,
    out, two_next, three_near, three_far, coef, one, force, two, three, last, acc,
):
    group = pl.program_id(0)
    groups = pl.num_programs(0)
    layers, rows = src_l.shape[2], src_l.shape[3]
    nk = rows // 8
    marks = masks()
    weight, scale = scale_of(freq, group)
    weight = weight * 4096.0
    sources, slows = (src_l, src_r), (slow_l, slow_r)
    chains = [(side, pair) for side in range(2) for pair in range(2)]

    @pl.loop(0, layers - 2)
    def _(place):
        layer = place + 1
        coefficients(
            store_to((coef, (layer,))),
            lambda h, k: slows[h][layer, pl.ds(k, 8, stride=nk), :],
            scale,
            1.0 / 64.0,
            nk,
        )
        for pair in range(2):
            rows_of = row_piece(sources, (0,), 2 * pair, (layer,), nk)
            keep = store_to((force, (pair, layer)))
            for c in range(2):
                for h in range(2):
                    for k in range(nk):
                        keep(c, h, k, rows_of(c, h, k))
            start_layer(store_to((one, (pair, layer))), rows_of, piece_of(coef, (layer,)), nk)

    def copy_plane(keep, given):
        for c in range(2):
            for h in range(2):
                for k in range(nk):
                    keep(c, h, k, given(c, h, k))

    def layer_at(side, at):
        return at if side == 0 else layers - 1 - at

    def step(target, pair, layer, ref, skip):
        near = [piece_of(ref, (pair, layer + shift - skip)) for shift in (-1, 0, 1)]
        relax(
            store_to(target),
            piece_of(force, (pair, layer)),
            near,
            piece_of(coef, (layer,)),
            marks,
            nk,
        )

    for side, pair in chains:
        copy_plane(
            store_to((two, (pair, layer_at(side, 1)))), piece_of(second, (0, pair, side))
        )

    @pl.loop(0, (layers - 4) // 2)
    def _(turn_at):
        for offset in range(2):
            for pair in range(2):
                layer = 2 + 2 * turn_at + offset
                step((two, (pair, layer)), pair, layer, one, 0)

    @pl.loop(0, (layers - 4) // 2)
    def _(turn_at):
        for offset in range(2):
            for pair in range(2):
                layer = 2 + 2 * turn_at + offset
                step((three, (pair, layer - 2)), pair, layer, two, 0)

    for side, pair in chains:
        step((last, (side, pair)), pair, layers // 2 - 1 + side, three, 2)
        for keep, ref, at in (
            (two_next, two, layer_at(side, 2)),
            (three_near, three, layer_at(side, 2) - 2),
            (three_far, three, layer_at(side, 3) - 2),
        ):
            copy_plane(store_to((keep, (0, pair, side))), piece_of(ref, (pair, at)))
    products(last, acc, 0, weight, group == 0, nk)

    @pl.when(group == groups - 1)
    def _():
        write_out(out, acc, 0)


def middle_kernel(freq, *refs):
    sides = []
    for side in range(2):
        part = refs[12 * side : 12 * side + 12]
        sides.append([[part[at + 2 * n : at + 2 * n + 2] for n in range(3)] for at in (0, 6)])
    core_field, core_slow, chip_field, chip_slow, second, two_next, three_near, three_far = refs[24:32]
    out, base_three, base_next, base_four, factors = refs[32:37]
    force, beyond, one, first_two, first_three, halo, halo_slow, change, last, acc = refs[37:]
    group = pl.program_id(0)
    groups = pl.num_programs(0)
    rows = second.shape[-2]
    nk = rows // 8
    marks = masks()
    weight, scale = scale_of(freq, group)
    weight = weight * 4096.0
    chains = [(side, pair) for side in range(2) for pair in range(2)]
    to_chip, to_core = parity(), 1 - parity()
    halo[to_core] = core_field[...]
    halo[to_chip] = chip_field[...]
    halo_slow[to_core] = core_slow[0]
    halo_slow[to_chip] = chip_slow[0]

    for side in range(2):
        coefficients(
            store_to((beyond, (side,))),
            lambda h, k, side=side: halo_slow[side, h, pl.ds(8 * k, 8), :],
            scale,
            paired(side),
            nk,
        )
        for at in range(3):
            slows = sides[side][1][at]
            coefficients(
                store_to((factors, (0, side, at))),
                lambda h, k, slows=slows: slows[h][0, pl.ds(k, 8, stride=nk), :],
                scale,
                1.0 / 64.0,
                nk,
            )
            for pair in range(2):
                rows_of = row_piece(sides[side][0][at], (0,), 2 * pair, (0,), nk)
                keep = store_to((force, (side, pair, at)))
                for c in range(2):
                    for h in range(2):
                        for k in range(nk):
                            keep(c, h, k, rows_of(c, h, k))
                if at < 2:
                    start_layer(
                        store_to((one, (side, pair, at))),
                        rows_of,
                        piece_of(factors, (0, side, at)),
                        nk,
                    )

    def step(target, side, pair, at, near):
        relax(
            store_to(target),
            piece_of(force, (side, pair, at)),
            near,
            piece_of(factors, (0, side, at)),
            marks,
            nk,
        )

    def held(ref, side, pair):
        return piece_of(ref, (0, pair, side))

    for side, pair in chains:
        near = [sent_piece(halo, (side,), 2 * pair)]
        near += [piece_of(one, (side, pair, at)) for at in range(2)]
        step((first_two, (side, pair)), side, pair, 0, near)
    for side, pair in chains:
        near = [None, None, piece_of(one, (side, pair, 0))]
        relax(store_to((change, (0, side, pair))), None, near, piece_of(beyond, (side,)), marks, nk)
    for side, pair in chains:
        near = [
            piece_of(first_two, (side, pair)),
            held(second, side, pair),
            held(two_next, side, pair),
        ]
        step((first_three, (side, pair)), side, pair, 1, near)
    for side, pair in chains:
        near = [
            None,
            piece_of(change, (0, side, pair)),
            piece_of(first_two, (side, pair)),
        ]
        relax(store_to((change, (1, side, pair))), None, near, piece_of(beyond, (side,)), marks, nk)
    for side, pair in chains:
        three = piece_of(first_three, (side, pair))
        near = [three, held(three_near, side, pair), held(three_far, side, pair)]
        step((last, (side, pair)), side, pair, 2, near)
    products(last, acc, 0, weight, group == 0, nk)
    for side, pair in chains:
        three = piece_of(first_three, (side, pair))
        twos = [piece_of(first_two, (side, pair)), held(second, side, pair)]
        changes = [piece_of(change, (number, side, pair)) for number in range(2)]
        for target, at, near in (
            (base_three, 0, [changes[0], *twos]),
            (base_next, 1, [None, three, held(three_near, side, pair)]),
            (base_four, 0, [changes[1], None, three]),
        ):
            step((target, (0, pair, side)), side, pair, at, near)

    @pl.when(group == groups - 1)
    def _():
        write_out(out, acc, 0)


def outer_kernel(freq, core, chip, base_three, base_next, base_four, factors, out, sent_fields, fresh, last, acc):
    group = pl.program_id(0)
    groups = pl.num_programs(0)
    rows = base_three.shape[-2]
    nk = rows // 8
    marks = masks()
    weight = scale_of(freq, group)[0] * 4096.0
    chains = [(side, pair) for side in range(2) for pair in range(2)]
    to_chip, to_core = parity(), 1 - parity()
    for number in range(2):
        sent_fields[to_core, number] = core[number, 0]
        sent_fields[to_chip, number] = chip[number, 0]

    def step(target, base, side, pair, at, near):
        relax(
            store_to(target),
            None,
            near,
            piece_of(factors, (0, side, at)),
            marks,
            nk,
            base=piece_of(base, (0, pair, side)),
        )

    for side, pair in chains:
        near = [sent_piece(sent_fields, (side, 0), 2 * pair), None, None]
        step((fresh, (side, pair)), base_three, side, pair, 0, near)
    for side, pair in chains:
        near = [piece_of(fresh, (side, pair)), None, None]
        step((last, (0, side, pair)), base_next, side, pair, 1, near)
    for side, pair in chains:
        near = [sent_piece(sent_fields, (side, 1), 2 * pair), piece_of(fresh, (side, pair)), None]
        step((last, (1, side, pair)), base_four, side, pair, 0, near)
    for place in range(2):
        products(last.at[place], acc, place, weight, group == 0, nk)

    @pl.when(group == groups - 1)
    def _():
        write_out(out, acc, 0)


def precond_kernel(pick, *refs):
    chunks, (precond, outgoing) = refs[:-2], refs[-2:]
    layers = precond.shape[0]
    step = 0
    for chunk in chunks:
        for place in range(chunk.shape[1]):
            for side in range(2):
                layer = layers // 2 - 1 - step if side == 0 else layers // 2 + step
                grad = chunk[0, place, 0, side]
                illum = chunk[0, place, 1, side]
                for other in range(1, chunk.shape[0]):
                    grad = grad + chunk[other, place, 0, side]
                    illum = illum + chunk[other, place, 1, side]
                precond[layer] = grad / jnp.sqrt(illum + 1.0)
            step += 1

    @pl.loop(0, outgoing.shape[0])
    def _(slot):
        outgoing[slot] = precond[pick[slot]]


def deliver_kernel(slots, incoming, out):
    @pl.loop(0, out.shape[2])
    def _(number):
        out[0, 0, number] = incoming[slots[number]]


def smem():
    return pl.BlockSpec(memory_space=pltpu.SMEM)


def vmem():
    return pl.BlockSpec(memory_space=pltpu.VMEM)


def plane_scratch(*lead, rows):
    return pltpu.VMEM(lead + (2, rows, HALF), jnp.float32)


def compiler_params(mebibytes):
    return pltpu.CompilerParams(vmem_limit_bytes=mebibytes * 1024 * 1024)


def light():
    return pl.CostEstimate(flops=1000, bytes_accessed=1000, transcendentals=0)


def in_hbm(array):
    return pltpu.with_memory_space_constraint(array, pltpu.HBM)


def hbm(*shape):
    return pltpu.HBM(shape, jnp.float32)


def state(groups, rows):
    return (
        hbm(groups, 2, 2, 2, 2, rows, HALF),
        pl.BlockSpec((1, 2, 2, 2, 2, rows, HALF), lambda g: (g, 0, 0, 0, 0, 0, 0)),
    )


def sent(groups, rows):
    return (
        hbm(2, groups, 4, 2, rows, HALF),
        pl.BlockSpec((2, 1, 4, 2, rows, HALF), lambda g: (0, g, 0, 0, 0, 0)),
    )


def factor_state(groups, rows):
    return (
        hbm(groups, 2, 3, 2, 2, rows, HALF),
        pl.BlockSpec((1, 2, 3, 2, 2, rows, HALF), lambda g: (g, 0, 0, 0, 0, 0, 0)),
    )


def sums(bands, rows, columns, steps=1):
    shape = (bands, steps, 2, 2, rows // bands, columns)
    return hbm(*shape), pl.BlockSpec(shape, lambda g: (0,) * 6)


def split(pairs):
    return dict(out_shape=[p[0] for p in pairs], out_specs=[p[1] for p in pairs])


def layer_specs(sources, own):
    rows = sources.shape[3]
    return (
        [pl.BlockSpec((1, 4, 1, rows, HALF), lambda g, h=h: (g, 0, own, 0, h)) for h in range(2)],
        [pl.BlockSpec((1, rows, HALF), lambda g, h=h: (own, 0, h)) for h in range(2)],
    )


def first_edges(freq, sources, slowness):
    groups, _, _, rows, _ = sources.shape
    anywhere = pl.BlockSpec(memory_space=pl.ANY)
    return pl.pallas_call(
        first_kernel,
        in_specs=[smem(), anywhere, anywhere],
        out_specs=[vmem()] * 2,
        out_shape=[hbm(4 * groups + 1, 2, rows, HALF)] * 2,
        scratch_shapes=[
            pltpu.VMEM((2, 2, groups, 4, rows, HALF), jnp.float32),
            plane_scratch(2, rows=rows),
            plane_scratch(2, groups, 2, rows=rows),
            pltpu.SemaphoreType.DMA((2, 2, 2)),
        ],
        compiler_params=compiler_params(8),
        cost_estimate=light(),
        name="first",
    )(freq, in_hbm(sources), in_hbm(slowness))


def edge_layers(sources, slowness):
    layers = sources.shape[2]
    sources, slowness = in_hbm(sources), in_hbm(slowness)
    operands, specs = [], []
    for side in range(2):
        parts = [layer_specs(sources, at if side == 0 else layers - 1 - at) for at in range(3)]
        for what, array in enumerate((sources, slowness)):
            for part in parts:
                operands += [array] * 2
                specs += part[what]
    return operands, specs


def later_edges(freq, sources, slowness):
    groups, _, _, rows, _ = sources.shape
    operands, specs = edge_layers(sources, slowness)
    operands, specs = [freq] + operands, [smem()] + specs
    return pl.pallas_call(
        edge_kernel,
        grid=(groups,),
        in_specs=specs,
        **split([sent(groups, rows)] * 2 + [state(groups, rows)]),
        scratch_shapes=[
            plane_scratch(2, 3, 2, rows=rows),
            plane_scratch(2, 2, 3, 2, rows=rows),
            plane_scratch(2, 2, 2, 2, rows=rows),
        ],
        compiler_params=compiler_params(32),
        cost_estimate=light(),
        name="edges",
    )(*operands)


def inner(freq, sources, slowness, second, bands):
    groups, _, layers, rows, columns = sources.shape
    half = [
        pl.BlockSpec((1, 4, layers, rows, HALF), lambda g, h=h: (g, 0, 0, 0, h)) for h in range(2)
    ]
    slow = [pl.BlockSpec((layers, rows, HALF), lambda g, h=h: (0, 0, h)) for h in range(2)]
    sources, slowness = in_hbm(sources), in_hbm(slowness)
    return pl.pallas_call(
        inner_kernel,
        grid=(groups,),
        in_specs=[smem()] + half + slow + [state(groups, rows)[1]],
        **split([sums(bands, rows, columns)] + [state(groups, rows)] * 3),
        scratch_shapes=[
            plane_scratch(layers, 2, rows=rows),
            plane_scratch(2, layers, 2, rows=rows),
            plane_scratch(2, layers, 2, rows=rows),
            plane_scratch(2, layers, 2, rows=rows),
            plane_scratch(2, layers - 4, 2, rows=rows),
            plane_scratch(2, 2, 2, rows=rows),
            plane_scratch(1, 2, 2, rows=rows),
        ],
        compiler_params=compiler_params(40),
        cost_estimate=light(),
        name="inner",
    )(freq, sources, sources, slowness, slowness, in_hbm(second))


def middle(freq, sources, slowness, from_core, from_chip, held, bands):
    groups, _, _, rows, columns = sources.shape
    operands, specs = edge_layers(sources, slowness)
    near = [
        pl.BlockSpec((4, 2, rows, HALF), lambda g: (g, 0, 0, 0)),
        pl.BlockSpec((1, 2, rows, HALF), lambda g: (4 * groups, 0, 0, 0)),
    ]
    return pl.pallas_call(
        middle_kernel,
        grid=(groups,),
        in_specs=[smem()] + specs + near * 2 + [state(groups, rows)[1]] * 4,
        **split(
            [sums(bands, rows, columns)] + [state(groups, rows)] * 3 + [factor_state(groups, rows)]
        ),
        scratch_shapes=[
            plane_scratch(2, 2, 3, 2, rows=rows),
            plane_scratch(2, 2, rows=rows),
            plane_scratch(2, 2, 2, 2, rows=rows),
            plane_scratch(2, 2, 2, rows=rows),
            plane_scratch(2, 2, 2, rows=rows),
            plane_scratch(2, 4, rows=rows),
            plane_scratch(2, rows=rows),
            plane_scratch(2, 2, 2, 2, rows=rows),
            plane_scratch(2, 2, 2, rows=rows),
            plane_scratch(1, 2, 2, rows=rows),
        ],
        compiler_params=compiler_params(40),
        cost_estimate=light(),
        name="middle",
    )(
        freq, *operands, from_core, from_core, from_chip, from_chip,
        *[in_hbm(array) for array in held],
    )


def outer(freq, from_core, from_chip, held, bands, rows, columns):
    groups = from_core.shape[1]
    return pl.pallas_call(
        outer_kernel,
        grid=(groups,),
        in_specs=[smem()] + [sent(groups, rows)[1]] * 2 + [state(groups, rows)[1]] * 3
        + [factor_state(groups, rows)[1]],
        **split([sums(bands, rows, columns, 2)]),
        scratch_shapes=[
            plane_scratch(2, 2, 4, rows=rows),
            plane_scratch(2, 2, 2, rows=rows),
            plane_scratch(2, 2, 2, 2, rows=rows),
            plane_scratch(2, 2, 2, rows=rows),
        ],
        compiler_params=compiler_params(32),
        cost_estimate=light(),
        name="outer",
    )(freq, from_core, from_chip, *[in_hbm(array) for array in held])[0]


def route(coverage, own_index):
    lists = coverage[0]
    owner, local = lists // TPD, lists % TPD
    position = jnp.arange(lists.shape[1], dtype=jnp.int32)
    same_owner = owner[:, :, None] == owner[:, None, :]
    earlier = position[None, :] < position[:, None]
    rank = jnp.sum((same_owner & earlier[None]).astype(jnp.int32), axis=2)
    slots = jnp.arange(CAP, dtype=jnp.int32)
    hit = (owner == own_index)[:, :, None] & (rank[:, :, None] == slots[None, None, :])
    pick = jnp.sum(jnp.where(hit, local[:, :, None], 0), axis=1).reshape(-1)
    own_slots = owner * CAP + rank
    return pick, lax.dynamic_index_in_dim(own_slots, own_index, 0, keepdims=False)


def body(sources, slowness, freq_index, coverage):
    groups, _, layers, rows, columns = sources.shape
    bands, members = lax.axis_size("freq"), lax.axis_size("sub")
    own_index = lax.axis_index("sub")
    cores = [(i, i ^ 1) for i in range(members)]
    chips = [(i, i + step) for i in range(members) for step in (2 * (i % 2) - 1,) if 0 <= i + step < members]
    def exchange(to_chip, to_core):
        return lax.ppermute(to_chip, "sub", chips), lax.ppermute(to_core, "sub", cores)

    near_chip, near_core = exchange(*first_edges(freq_index, sources, slowness))
    *edges, second = later_edges(freq_index, sources, slowness)
    far_chip, far_core = exchange(*edges)
    pick, slots = route(coverage, own_index)

    def spread(chunk):
        return lax.all_to_all(chunk, "freq", split_axis=0, concat_axis=0, tiled=True)

    def spread_next(chunk):
        if chunks:
            chunks[-1], chunk = lax.optimization_barrier((chunks[-1], chunk))
        chunks.append(spread(chunk))

    chunks = []
    chunk, *held = inner(freq_index, sources, slowness, second, bands)
    spread_next(chunk)
    held = [second] + held
    chunk, *held = middle(freq_index, sources, slowness, near_core, near_chip, held, bands)
    spread_next(chunk)
    spread_next(outer(freq_index, far_core, far_chip, held, bands, rows, columns))
    depth = rows // bands
    precond, outgoing = pl.pallas_call(
        precond_kernel,
        in_specs=[smem()] + [vmem()] * len(chunks),
        out_specs=[vmem()] * 2,
        out_shape=[
            jax.ShapeDtypeStruct((layers, depth, columns), jnp.float32),
            jax.ShapeDtypeStruct((members * CAP, depth, columns), jnp.float32),
        ],
        compiler_params=compiler_params(12),
        name="precond",
    )(pick, *chunks)
    incoming = lax.all_to_all(outgoing, "sub", split_axis=0, concat_axis=0, tiled=True)
    delivered = pl.pallas_call(
        deliver_kernel,
        in_specs=[smem(), vmem()],
        out_specs=vmem(),
        out_shape=jax.ShapeDtypeStruct((1, 1, coverage.shape[2], depth, columns), jnp.float32),
        compiler_params=compiler_params(12),
        name="deliver",
    )(slots, incoming)
    return precond, delivered


def solution(mesh):
    placed = (
        P("freq", None, "sub", None, None),
        P("sub", None, None),
        P("freq"),
        P("freq", None, None),
    )
    return jax.shard_map(
        body,
        mesh=mesh,
        in_specs=placed,
        out_specs=(P("sub", "freq", None), P("freq", "sub", None, None, None)),
        check_vma=False,
    )
```

```python
import functools

import jax
import jax.numpy as jnp
from jax import lax
from jax.experimental import pallas as pl
from jax.experimental.pallas import tpu as pltpu
from jax.sharding import PartitionSpec as P

TPD = 8
CAP = 2
HALF = 128


def masks():
    lane = lax.broadcasted_iota(jnp.int32, (8, HALF), 1)
    row = lax.broadcasted_iota(jnp.int32, (8, HALF), 0)
    return lane == 0, lane == HALF - 1, row == 0, row == 7


def turn(real, imag, coef_real, coef_imag):
    return real * coef_real + imag * coef_imag, imag * coef_real - real * coef_imag


def coefficients(store, slow, scale, factor, nk):
    for k in range(nk):
        for h in range(2):
            sigma = scale * slow(h, k)
            diag = 0.875 - sigma
            inverse = factor / (diag * diag + sigma * sigma)
            store(0, h, k, diag * inverse)
            store(1, h, k, sigma * inverse)


def relax(store, force, near, coef, marks, nk, base=None):
    lane_first, lane_last, row_first, row_last = marks

    def across(c, h, k):
        before, middle, after = [None if layer is None else layer(c, h, k) for layer in near]
        parts = [part for part in (before, after) if part is not None]
        if middle is not None:
            parts.append(middle + middle)
        return functools.reduce(lambda total, part: total + part, parts)

    both = [(c, h) for c in range(2) for h in range(2)]
    top = {at: across(*at, 0) for at in both}
    bottom = {at: across(*at, nk - 1) for at in both}
    here = top
    pair = {at: jnp.where(row_first, 0.0, pltpu.roll(bottom[at], 1, 0)) + top[at] for at in both}
    for k in range(nk):
        if k < nk - 2:
            following = {at: across(*at, k + 1) for at in both}
        elif k == nk - 2:
            following = bottom
        else:
            following = {at: jnp.where(row_last, 0.0, pltpu.roll(top[at], 7, 0)) for at in both}
        terms = []
        for c in range(2):
            depth = []
            for h in range(2):
                later = here[c, h] + following[c, h]
                depth.append(pair[c, h] + later)
                pair[c, h] = later
            left, right = depth
            left_up, right_up = pltpu.roll(left, HALF - 1, 1), pltpu.roll(right, HALF - 1, 1)
            left_down, right_down = pltpu.roll(left, 1, 1), pltpu.roll(right, 1, 1)
            left_sides = jnp.where(lane_last, right_up, left_up) + jnp.where(lane_first, 0.0, left_down)
            right_sides = jnp.where(lane_last, 0.0, right_up) + jnp.where(
                lane_first, left_down, right_down
            )
            for h, (middle, ends) in enumerate(((left, left_sides), (right, right_sides))):
                total = ends + (middle + middle)
                if near[1] is not None:
                    total = total - 8.0 * near[1](c, h, k)
                terms.append(total if force is None else force(c, h, k) + total)
        here = following
        for h in range(2):
            planes = turn(terms[h], terms[2 + h], coef(0, h, k), coef(1, h, k))
            for c in range(2):
                store(c, h, k, planes[c] if base is None else base(c, h, k) + planes[c])


def piece_of(ref, lead):
    return lambda c, h, k: ref[lead + (c, h, pl.ds(8 * k, 8), slice(None))]


def row_piece(refs, lead, offset, tail, nk):
    return lambda c, h, k: refs[h][
        lead + (offset + c,) + tail + (pl.ds(k, 8, stride=nk), slice(None))
    ]


def store_to(*places):
    def store(c, h, k, piece):
        for ref, lead in places:
            ref[lead + (c, h, pl.ds(8 * k, 8), slice(None))] = piece

    return store


def start_layer(store, force, coef, nk):
    for k in range(nk):
        for h in range(2):
            planes = turn(force(0, h, k), force(1, h, k), coef(0, h, k), coef(1, h, k))
            for c in range(2):
                store(c, h, k, planes[c])


def products(last, acc, place, weight, first, nk):
    for side in range(2):
        forward, adjoint = [piece_of(last, (side, pair)) for pair in range(2)]
        for h in range(2):
            for k in range(nk):
                fr, fi = forward(0, h, k), forward(1, h, k)
                ar, ai = adjoint(0, h, k), adjoint(1, h, k)
                terms = (weight * (fr * ar - fi * ai), weight * (fr * fr + fi * fi))
                for number, term in enumerate(terms):
                    at = (place, number, side, h, pl.ds(k, 8, stride=nk), slice(None))
                    acc[at] = jnp.where(first, term, acc[at] + term)


def write_out(out, acc, offset):
    bands, _, _, _, depth, _ = out.shape
    for band in range(bands):
        for place in range(acc.shape[0]):
            for number in range(2):
                for side in range(2):
                    for h in range(2):
                        out[band, offset + place, number, side, :, pl.ds(h * HALF, HALF)] = acc[
                            place, number, side, h, pl.ds(band * depth, depth), :
                        ]


def scale_of(freq, group):
    weight = 1.0 + freq[group].astype(jnp.float32) / 16.0
    return weight, 0.12 * weight


def parity():
    return lax.axis_index("sub") % 2


def paired(side):
    index = lax.axis_index("sub")
    there = index > 0 if side == 0 else index < lax.axis_size("sub") - 1
    return jnp.where(there, 1.0 / 64.0, 0.0)


def first_kernel(freq, sources, slowness, to_chip, to_core, raw, slow, coef, sems):
    groups, _, layers, rows = sources.shape[:4]
    nk = rows // 8
    places = (parity() * (layers - 1), (1 - parity()) * (layers - 1))
    copies = []
    for side, own in enumerate(places):
        for h in range(2):
            lanes = pl.ds(h * HALF, HALF)
            pairs = ((slowness.at[own, :, lanes], slow), (sources.at[:, :, own, :, lanes], raw))
            for number, (ref, held) in enumerate(pairs):
                copies.append(
                    pltpu.make_async_copy(ref, held.at[side, h], sems.at[side, h, number])
                )
    for copy in copies:
        copy.start()
    for side, out in enumerate((to_chip, to_core)):
        for copy in copies[4 * side : 4 * side + 4]:
            copy.wait()

        def sigma(h, k):
            return slow[side, h, pl.ds(k, 8, stride=nk), :]

        for h in range(2):
            for k in range(nk):
                out[4 * groups, h, pl.ds(8 * k, 8), :] = sigma(h, k)
        for group in range(groups):
            scale = scale_of(freq, group)[1]
            coefficients(store_to((coef, (side, group))), sigma, scale, 1.0 / 64.0, nk)
            for pair in range(2):
                start_layer(
                    store_from(out, (), 4 * group + 2 * pair),
                    row_piece((raw.at[side, 0], raw.at[side, 1]), (group,), 2 * pair, (), nk),
                    piece_of(coef, (side, group)),
                    nk,
                )


def store_from(ref, lead, offset):
    def store(c, h, k, piece):
        ref[lead + (offset + c, h, pl.ds(8 * k, 8), slice(None))] = piece

    return store


def sent_piece(ref, lead, offset):
    return lambda c, h, k: ref[lead + (offset + c, h, pl.ds(8 * k, 8), slice(None))]


def edge_kernel(freq, _, *refs):
    sides = []
    for side in range(2):
        part = refs[12 * side : 12 * side + 12]
        sides.append([[part[at + 2 * n : at + 2 * n + 2] for n in range(3)] for at in (0, 6)])
    far_chip, far_core, second, coef, one, fields = refs[24:]
    group = pl.program_id(0)
    rows = sides[0][1][0][0].shape[-2]
    nk = rows // 8
    marks = masks()
    scale = scale_of(freq, group)[1]
    chains = [(side, pair) for side in range(2) for pair in range(2)]

    def force(side, pair, at):
        return row_piece(sides[side][0][at], (0,), 2 * pair, (0,), nk)

    for side in range(2):
        for at in range(3):
            slows = sides[side][1][at]
            coefficients(
                store_to((coef, (side, at))),
                lambda h, k, slows=slows: slows[h][0, pl.ds(k, 8, stride=nk), :],
                scale,
                1.0 / 64.0,
                nk,
            )
            for pair in range(2):
                start_layer(
                    store_to((one, (side, pair, at))),
                    force(side, pair, at),
                    piece_of(coef, (side, at)),
                    nk,
                )
    for at in range(2):
        for side, pair in chains:
            near = [piece_of(one, (side, pair, n)) if n >= 0 else None for n in (at - 1, at, at + 1)]
            target = (fields, (side, 0, pair)) if at == 0 else (second, (0, pair, side))
            relax(
                store_to(target), force(side, pair, at), near, piece_of(coef, (side, at)), marks, nk
            )
    for side, pair in chains:
        near = [None, piece_of(fields, (side, 0, pair)), piece_of(second, (0, pair, side))]
        relax(
            store_to((fields, (side, 1, pair))),
            force(side, pair, 0),
            near,
            piece_of(coef, (side, 0)),
            marks,
            nk,
        )
    for out, side in ((far_chip, parity()), (far_core, 1 - parity())):
        for level in range(2):
            for pair in range(2):
                for c in range(2):
                    out[level, 0, 2 * pair + c] = fields[side, level, pair, c]


def inner_kernel(
    freq, src_l, src_r, slow_l, slow_r, second,
    out, two_next, three_near, three_far, coef, one, force, two, three, last, acc,
):
    group = pl.program_id(0)
    groups = pl.num_programs(0)
    layers, rows = src_l.shape[2], src_l.shape[3]
    nk = rows // 8
    marks = masks()
    weight, scale = scale_of(freq, group)
    weight = weight * 4096.0
    sources, slows = (src_l, src_r), (slow_l, slow_r)
    chains = [(side, pair) for side in range(2) for pair in range(2)]

    @pl.loop(0, layers - 2)
    def _(place):
        layer = place + 1
        coefficients(
            store_to((coef, (layer,))),
            lambda h, k: slows[h][layer, pl.ds(k, 8, stride=nk), :],
            scale,
            1.0 / 64.0,
            nk,
        )
        for pair in range(2):
            rows_of = row_piece(sources, (0,), 2 * pair, (layer,), nk)
            keep = store_to((force, (pair, layer)))
            for c in range(2):
                for h in range(2):
                    for k in range(nk):
                        keep(c, h, k, rows_of(c, h, k))
            start_layer(store_to((one, (pair, layer))), rows_of, piece_of(coef, (layer,)), nk)

    def copy_plane(keep, given):
        for c in range(2):
            for h in range(2):
                for k in range(nk):
                    keep(c, h, k, given(c, h, k))

    def layer_at(side, at):
        return at if side == 0 else layers - 1 - at

    def step(target, pair, layer, ref, skip):
        near = [piece_of(ref, (pair, layer + shift - skip)) for shift in (-1, 0, 1)]
        relax(
            store_to(target),
            piece_of(force, (pair, layer)),
            near,
            piece_of(coef, (layer,)),
            marks,
            nk,
        )

    for side, pair in chains:
        copy_plane(
            store_to((two, (pair, layer_at(side, 1)))), piece_of(second, (0, pair, side))
        )

    @pl.loop(0, (layers - 4) // 2)
    def _(turn_at):
        for offset in range(2):
            for pair in range(2):
                layer = 2 + 2 * turn_at + offset
                step((two, (pair, layer)), pair, layer, one, 0)

    @pl.loop(0, (layers - 4) // 2)
    def _(turn_at):
        for offset in range(2):
            for pair in range(2):
                layer = 2 + 2 * turn_at + offset
                step((three, (pair, layer - 2)), pair, layer, two, 0)

    for side, pair in chains:
        step((last, (side, pair)), pair, layers // 2 - 1 + side, three, 2)
        for keep, ref, at in (
            (two_next, two, layer_at(side, 2)),
            (three_near, three, layer_at(side, 2) - 2),
            (three_far, three, layer_at(side, 3) - 2),
        ):
            copy_plane(store_to((keep, (0, pair, side))), piece_of(ref, (pair, at)))
    products(last, acc, 0, weight, group == 0, nk)

    @pl.when(group == groups - 1)
    def _():
        write_out(out, acc, 0)


def middle_kernel(freq, *refs):
    sides = []
    for side in range(2):
        part = refs[12 * side : 12 * side + 12]
        sides.append([[part[at + 2 * n : at + 2 * n + 2] for n in range(3)] for at in (0, 6)])
    core_field, core_slow, chip_field, chip_slow, second, two_next, three_near, three_far = refs[24:32]
    out, base_three, base_next, base_four, factors = refs[32:37]
    force, beyond, one, first_two, first_three, halo, halo_slow, change, last, acc = refs[37:]
    group = pl.program_id(0)
    groups = pl.num_programs(0)
    rows = second.shape[-2]
    nk = rows // 8
    marks = masks()
    weight, scale = scale_of(freq, group)
    weight = weight * 4096.0
    chains = [(side, pair) for side in range(2) for pair in range(2)]
    to_chip, to_core = parity(), 1 - parity()
    halo[to_core] = core_field[...]
    halo[to_chip] = chip_field[...]
    halo_slow[to_core] = core_slow[0]
    halo_slow[to_chip] = chip_slow[0]

    for side in range(2):
        coefficients(
            store_to((beyond, (side,))),
            lambda h, k, side=side: halo_slow[side, h, pl.ds(8 * k, 8), :],
            scale,
            paired(side),
            nk,
        )
        for at in range(3):
            slows = sides[side][1][at]
            coefficients(
                store_to((factors, (0, side, at))),
                lambda h, k, slows=slows: slows[h][0, pl.ds(k, 8, stride=nk), :],
                scale,
                1.0 / 64.0,
                nk,
            )
            for pair in range(2):
                rows_of = row_piece(sides[side][0][at], (0,), 2 * pair, (0,), nk)
                keep = store_to((force, (side, pair, at)))
                for c in range(2):
                    for h in range(2):
                        for k in range(nk):
                            keep(c, h, k, rows_of(c, h, k))
                if at < 2:
                    start_layer(
                        store_to((one, (side, pair, at))),
                        rows_of,
                        piece_of(factors, (0, side, at)),
                        nk,
                    )

    def step(target, side, pair, at, near):
        relax(
            store_to(target),
            piece_of(force, (side, pair, at)),
            near,
            piece_of(factors, (0, side, at)),
            marks,
            nk,
        )

    def held(ref, side, pair):
        return piece_of(ref, (0, pair, side))

    for side, pair in chains:
        near = [sent_piece(halo, (side,), 2 * pair)]
        near += [piece_of(one, (side, pair, at)) for at in range(2)]
        step((first_two, (side, pair)), side, pair, 0, near)
    for side, pair in chains:
        near = [None, None, piece_of(one, (side, pair, 0))]
        relax(store_to((change, (0, side, pair))), None, near, piece_of(beyond, (side,)), marks, nk)
    for side, pair in chains:
        near = [
            piece_of(first_two, (side, pair)),
            held(second, side, pair),
            held(two_next, side, pair),
        ]
        step((first_three, (side, pair)), side, pair, 1, near)
    for side, pair in chains:
        near = [
            None,
            piece_of(change, (0, side, pair)),
            piece_of(first_two, (side, pair)),
        ]
        relax(store_to((change, (1, side, pair))), None, near, piece_of(beyond, (side,)), marks, nk)
    for side, pair in chains:
        three = piece_of(first_three, (side, pair))
        near = [three, held(three_near, side, pair), held(three_far, side, pair)]
        step((last, (side, pair)), side, pair, 2, near)
    products(last, acc, 0, weight, group == 0, nk)
    for side, pair in chains:
        three = piece_of(first_three, (side, pair))
        twos = [piece_of(first_two, (side, pair)), held(second, side, pair)]
        changes = [piece_of(change, (number, side, pair)) for number in range(2)]
        for target, at, near in (
            (base_three, 0, [changes[0], *twos]),
            (base_next, 1, [None, three, held(three_near, side, pair)]),
            (base_four, 0, [changes[1], None, three]),
        ):
            step((target, (0, pair, side)), side, pair, at, near)

    @pl.when(group == groups - 1)
    def _():
        write_out(out, acc, 0)


def outer_kernel(freq, core, chip, base_three, base_next, base_four, factors, out, sent_fields, fresh, last, acc):
    group = pl.program_id(0)
    groups = pl.num_programs(0)
    rows = base_three.shape[-2]
    nk = rows // 8
    marks = masks()
    weight = scale_of(freq, group)[0] * 4096.0
    chains = [(side, pair) for side in range(2) for pair in range(2)]
    to_chip, to_core = parity(), 1 - parity()
    for number in range(2):
        sent_fields[to_core, number] = core[number, 0]
        sent_fields[to_chip, number] = chip[number, 0]

    def step(target, base, side, pair, at, near):
        relax(
            store_to(target),
            None,
            near,
            piece_of(factors, (0, side, at)),
            marks,
            nk,
            base=piece_of(base, (0, pair, side)),
        )

    for side, pair in chains:
        near = [sent_piece(sent_fields, (side, 0), 2 * pair), None, None]
        step((fresh, (side, pair)), base_three, side, pair, 0, near)
    for side, pair in chains:
        near = [piece_of(fresh, (side, pair)), None, None]
        step((last, (0, side, pair)), base_next, side, pair, 1, near)
    for side, pair in chains:
        near = [sent_piece(sent_fields, (side, 1), 2 * pair), piece_of(fresh, (side, pair)), None]
        step((last, (1, side, pair)), base_four, side, pair, 0, near)
    for place in range(2):
        products(last.at[place], acc, place, weight, group == 0, nk)

    @pl.when(group == groups - 1)
    def _():
        write_out(out, acc, 0)


def precond_kernel(pick, *refs):
    chunks, (precond, outgoing) = refs[:-2], refs[-2:]
    layers = precond.shape[0]
    step = 0
    for chunk in chunks:
        for place in range(chunk.shape[1]):
            for side in range(2):
                layer = layers // 2 - 1 - step if side == 0 else layers // 2 + step
                grad = chunk[0, place, 0, side]
                illum = chunk[0, place, 1, side]
                for other in range(1, chunk.shape[0]):
                    grad = grad + chunk[other, place, 0, side]
                    illum = illum + chunk[other, place, 1, side]
                precond[layer] = grad / jnp.sqrt(illum + 1.0)
            step += 1

    @pl.loop(0, outgoing.shape[0])
    def _(slot):
        outgoing[slot] = precond[pick[slot]]


def deliver_kernel(slots, incoming, out):
    @pl.loop(0, out.shape[2])
    def _(number):
        out[0, 0, number] = incoming[slots[number]]


def smem():
    return pl.BlockSpec(memory_space=pltpu.SMEM)


def vmem():
    return pl.BlockSpec(memory_space=pltpu.VMEM)


def plane_scratch(*lead, rows):
    return pltpu.VMEM(lead + (2, rows, HALF), jnp.float32)


def compiler_params(mebibytes):
    return pltpu.CompilerParams(vmem_limit_bytes=mebibytes * 1024 * 1024)


def light(size=1000):
    return pl.CostEstimate(flops=1000, bytes_accessed=size, transcendentals=0)


def in_hbm(array):
    return pltpu.with_memory_space_constraint(array, pltpu.HBM)


def hbm(*shape):
    return pltpu.HBM(shape, jnp.float32)


def state(groups, rows):
    return (
        hbm(groups, 2, 2, 2, 2, rows, HALF),
        pl.BlockSpec((1, 2, 2, 2, 2, rows, HALF), lambda g: (g, 0, 0, 0, 0, 0, 0)),
    )


def sent(groups, rows):
    return (
        hbm(2, groups, 4, 2, rows, HALF),
        pl.BlockSpec((2, 1, 4, 2, rows, HALF), lambda g: (0, g, 0, 0, 0, 0)),
    )


def factor_state(groups, rows):
    return (
        hbm(groups, 2, 3, 2, 2, rows, HALF),
        pl.BlockSpec((1, 2, 3, 2, 2, rows, HALF), lambda g: (g, 0, 0, 0, 0, 0, 0)),
    )


def sums(bands, rows, columns, steps=1):
    shape = (bands, steps, 2, 2, rows // bands, columns)
    return hbm(*shape), pl.BlockSpec(shape, lambda g: (0,) * 6)


def split(pairs):
    return dict(out_shape=[p[0] for p in pairs], out_specs=[p[1] for p in pairs])


def layer_specs(sources, own):
    rows = sources.shape[3]
    return (
        [pl.BlockSpec((1, 4, 1, rows, HALF), lambda g, h=h: (g, 0, own, 0, h)) for h in range(2)],
        [pl.BlockSpec((1, rows, HALF), lambda g, h=h: (own, 0, h)) for h in range(2)],
    )


def first_edges(freq, sources, slowness):
    groups, _, _, rows, _ = sources.shape
    anywhere = pl.BlockSpec(memory_space=pl.ANY)
    return pl.pallas_call(
        first_kernel,
        in_specs=[smem(), anywhere, anywhere],
        out_specs=[vmem()] * 2,
        out_shape=[hbm(4 * groups + 1, 2, rows, HALF)] * 2,
        scratch_shapes=[
            pltpu.VMEM((2, 2, groups, 4, rows, HALF), jnp.float32),
            plane_scratch(2, rows=rows),
            plane_scratch(2, groups, 2, rows=rows),
            pltpu.SemaphoreType.DMA((2, 2, 2)),
        ],
        compiler_params=compiler_params(8),
        cost_estimate=light(),
        name="first",
    )(freq, in_hbm(sources), in_hbm(slowness))


def edge_layers(sources, slowness):
    layers = sources.shape[2]
    sources, slowness = in_hbm(sources), in_hbm(slowness)
    operands, specs = [], []
    for side in range(2):
        parts = [layer_specs(sources, at if side == 0 else layers - 1 - at) for at in range(3)]
        for what, array in enumerate((sources, slowness)):
            for part in parts:
                operands += [array] * 2
                specs += part[what]
    return operands, specs


def later_edges(freq, sources, slowness, first):
    groups, _, _, rows, _ = sources.shape
    operands, specs = edge_layers(sources, slowness)
    operands = [freq, in_hbm(first)] + operands
    specs = [smem(), pl.BlockSpec(memory_space=pl.ANY)] + specs
    return pl.pallas_call(
        edge_kernel,
        grid=(groups,),
        in_specs=specs,
        **split([sent(groups, rows)] * 2 + [state(groups, rows)]),
        scratch_shapes=[
            plane_scratch(2, 3, 2, rows=rows),
            plane_scratch(2, 2, 3, 2, rows=rows),
            plane_scratch(2, 2, 2, 2, rows=rows),
        ],
        compiler_params=compiler_params(32),
        cost_estimate=light(),
        name="edges",
    )(*operands)


def inner(freq, sources, slowness, second, bands):
    groups, _, layers, rows, columns = sources.shape
    half = [
        pl.BlockSpec((1, 4, layers, rows, HALF), lambda g, h=h: (g, 0, 0, 0, h)) for h in range(2)
    ]
    slow = [pl.BlockSpec((layers, rows, HALF), lambda g, h=h: (0, 0, h)) for h in range(2)]
    sources, slowness = in_hbm(sources), in_hbm(slowness)
    return pl.pallas_call(
        inner_kernel,
        grid=(groups,),
        in_specs=[smem()] + half + slow + [state(groups, rows)[1]],
        **split([sums(bands, rows, columns)] + [state(groups, rows)] * 3),
        scratch_shapes=[
            plane_scratch(layers, 2, rows=rows),
            plane_scratch(2, layers, 2, rows=rows),
            plane_scratch(2, layers, 2, rows=rows),
            plane_scratch(2, layers, 2, rows=rows),
            plane_scratch(2, layers - 4, 2, rows=rows),
            plane_scratch(2, 2, 2, rows=rows),
            plane_scratch(1, 2, 2, rows=rows),
        ],
        compiler_params=compiler_params(40),
        cost_estimate=light(),
        name="inner",
    )(freq, sources, sources, slowness, slowness, in_hbm(second))


def middle(freq, sources, slowness, from_core, from_chip, held, bands):
    groups, _, _, rows, columns = sources.shape
    operands, specs = edge_layers(sources, slowness)
    near = [
        pl.BlockSpec((4, 2, rows, HALF), lambda g: (g, 0, 0, 0)),
        pl.BlockSpec((1, 2, rows, HALF), lambda g: (4 * groups, 0, 0, 0)),
    ]
    return pl.pallas_call(
        middle_kernel,
        grid=(groups,),
        in_specs=[smem()] + specs + near * 2 + [state(groups, rows)[1]] * 4,
        **split(
            [sums(bands, rows, columns)] + [state(groups, rows)] * 3 + [factor_state(groups, rows)]
        ),
        scratch_shapes=[
            plane_scratch(2, 2, 3, 2, rows=rows),
            plane_scratch(2, 2, rows=rows),
            plane_scratch(2, 2, 2, 2, rows=rows),
            plane_scratch(2, 2, 2, rows=rows),
            plane_scratch(2, 2, 2, rows=rows),
            plane_scratch(2, 4, rows=rows),
            plane_scratch(2, rows=rows),
            plane_scratch(2, 2, 2, 2, rows=rows),
            plane_scratch(2, 2, 2, rows=rows),
            plane_scratch(1, 2, 2, rows=rows),
        ],
        compiler_params=compiler_params(40),
        cost_estimate=light(100_000_000),
        name="middle",
    )(
        freq, *operands, from_core, from_core, from_chip, from_chip,
        *[in_hbm(array) for array in held],
    )


def outer(freq, from_core, from_chip, held, bands, rows, columns):
    groups = from_core.shape[1]
    return pl.pallas_call(
        outer_kernel,
        grid=(groups,),
        in_specs=[smem()] + [sent(groups, rows)[1]] * 2 + [state(groups, rows)[1]] * 3
        + [factor_state(groups, rows)[1]],
        **split([sums(bands, rows, columns, 2)]),
        scratch_shapes=[
            plane_scratch(2, 2, 4, rows=rows),
            plane_scratch(2, 2, 2, rows=rows),
            plane_scratch(2, 2, 2, 2, rows=rows),
            plane_scratch(2, 2, 2, rows=rows),
        ],
        compiler_params=compiler_params(32),
        cost_estimate=light(),
        name="outer",
    )(freq, from_core, from_chip, *[in_hbm(array) for array in held])[0]


def route(coverage, own_index):
    lists = coverage[0]
    owner, local = lists // TPD, lists % TPD
    position = jnp.arange(lists.shape[1], dtype=jnp.int32)
    same_owner = owner[:, :, None] == owner[:, None, :]
    earlier = position[None, :] < position[:, None]
    rank = jnp.sum((same_owner & earlier[None]).astype(jnp.int32), axis=2)
    slots = jnp.arange(CAP, dtype=jnp.int32)
    hit = (owner == own_index)[:, :, None] & (rank[:, :, None] == slots[None, None, :])
    pick = jnp.sum(jnp.where(hit, local[:, :, None], 0), axis=1).reshape(-1)
    own_slots = owner * CAP + rank
    return pick, lax.dynamic_index_in_dim(own_slots, own_index, 0, keepdims=False)


def body(sources, slowness, freq_index, coverage):
    groups, _, layers, rows, columns = sources.shape
    bands, members = lax.axis_size("freq"), lax.axis_size("sub")
    own_index = lax.axis_index("sub")
    cores = [(i, i ^ 1) for i in range(members)]
    chips = [(i, i + step) for i in range(members) for step in (2 * (i % 2) - 1,) if 0 <= i + step < members]
    def exchange(to_chip, to_core):
        return lax.ppermute(to_chip, "sub", chips), lax.ppermute(to_core, "sub", cores)

    near = first_edges(freq_index, sources, slowness)
    near_chip, near_core = exchange(*near)
    *edges, second = later_edges(freq_index, sources, slowness, near[0])
    far_chip, far_core = exchange(*edges)
    pick, slots = route(coverage, own_index)

    def spread(chunk):
        return lax.all_to_all(chunk, "freq", split_axis=0, concat_axis=0, tiled=True)

    def spread_next(chunk):
        if chunks:
            chunks[-1], chunk = lax.optimization_barrier((chunks[-1], chunk))
        chunks.append(spread(chunk))

    chunks = []
    chunk, *held = inner(freq_index, sources, slowness, second, bands)
    spread_next(chunk)
    held = [second] + held
    chunk, *held = middle(freq_index, sources, slowness, near_core, near_chip, held, bands)
    spread_next(chunk)
    spread_next(outer(freq_index, far_core, far_chip, held, bands, rows, columns))
    depth = rows // bands
    precond, outgoing = pl.pallas_call(
        precond_kernel,
        in_specs=[smem()] + [vmem()] * len(chunks),
        out_specs=[vmem()] * 2,
        out_shape=[
            jax.ShapeDtypeStruct((layers, depth, columns), jnp.float32),
            jax.ShapeDtypeStruct((members * CAP, depth, columns), jnp.float32),
        ],
        compiler_params=compiler_params(12),
        name="precond",
    )(pick, *chunks)
    incoming = lax.all_to_all(outgoing, "sub", split_axis=0, concat_axis=0, tiled=True)
    delivered = pl.pallas_call(
        deliver_kernel,
        in_specs=[smem(), vmem()],
        out_specs=vmem(),
        out_shape=jax.ShapeDtypeStruct((1, 1, coverage.shape[2], depth, columns), jnp.float32),
        compiler_params=compiler_params(12),
        name="deliver",
    )(slots, incoming)
    return precond, delivered


def solution(mesh):
    placed = (
        P("freq", None, "sub", None, None),
        P("sub", None, None),
        P("freq"),
        P("freq", None, None),
    )
    return jax.shard_map(
        body,
        mesh=mesh,
        in_specs=placed,
        out_specs=(P("sub", "freq", None), P("freq", "sub", None, None, None)),
        check_vma=False,
    )
```

```python
import functools

import jax
import jax.numpy as jnp
from jax import lax
from jax.experimental import pallas as pl
from jax.experimental.pallas import tpu as pltpu
from jax.sharding import PartitionSpec as P

TPD = 8
CAP = 2
HALF = 128


def masks():
    lane = lax.broadcasted_iota(jnp.int32, (8, HALF), 1)
    row = lax.broadcasted_iota(jnp.int32, (8, HALF), 0)
    return lane == 0, lane == HALF - 1, row == 0, row == 7


def turn(real, imag, coef_real, coef_imag):
    return real * coef_real + imag * coef_imag, imag * coef_real - real * coef_imag


def coefficients(store, slow, scale, factor, nk):
    for k in range(nk):
        for h in range(2):
            sigma = scale * slow(h, k)
            diag = 0.875 - sigma
            inverse = factor / (diag * diag + sigma * sigma)
            store(0, h, k, diag * inverse)
            store(1, h, k, sigma * inverse)


def relax(store, force, near, coef, marks, nk, base=None):
    lane_first, lane_last, row_first, row_last = marks

    def across(c, h, k):
        before, middle, after = [None if layer is None else layer(c, h, k) for layer in near]
        parts = [part for part in (before, after) if part is not None]
        if middle is not None:
            parts.append(middle + middle)
        return functools.reduce(lambda total, part: total + part, parts)

    both = [(c, h) for c in range(2) for h in range(2)]
    top = {at: across(*at, 0) for at in both}
    bottom = {at: across(*at, nk - 1) for at in both}
    here = top
    pair = {at: jnp.where(row_first, 0.0, pltpu.roll(bottom[at], 1, 0)) + top[at] for at in both}
    for k in range(nk):
        if k < nk - 2:
            following = {at: across(*at, k + 1) for at in both}
        elif k == nk - 2:
            following = bottom
        else:
            following = {at: jnp.where(row_last, 0.0, pltpu.roll(top[at], 7, 0)) for at in both}
        terms = []
        for c in range(2):
            depth = []
            for h in range(2):
                later = here[c, h] + following[c, h]
                depth.append(pair[c, h] + later)
                pair[c, h] = later
            left, right = depth
            left_up, right_up = pltpu.roll(left, HALF - 1, 1), pltpu.roll(right, HALF - 1, 1)
            left_down, right_down = pltpu.roll(left, 1, 1), pltpu.roll(right, 1, 1)
            left_sides = jnp.where(lane_last, right_up, left_up) + jnp.where(lane_first, 0.0, left_down)
            right_sides = jnp.where(lane_last, 0.0, right_up) + jnp.where(
                lane_first, left_down, right_down
            )
            for h, (middle, ends) in enumerate(((left, left_sides), (right, right_sides))):
                total = ends + (middle + middle)
                if near[1] is not None:
                    total = total - 8.0 * near[1](c, h, k)
                terms.append(total if force is None else force(c, h, k) + total)
        here = following
        for h in range(2):
            planes = turn(terms[h], terms[2 + h], coef(0, h, k), coef(1, h, k))
            for c in range(2):
                store(c, h, k, planes[c] if base is None else base(c, h, k) + planes[c])


def piece_of(ref, lead):
    return lambda c, h, k: ref[lead + (c, h, pl.ds(8 * k, 8), slice(None))]


def row_piece(refs, lead, offset, tail, nk):
    return lambda c, h, k: refs[h][
        lead + (offset + c,) + tail + (pl.ds(k, 8, stride=nk), slice(None))
    ]


def store_to(*places):
    def store(c, h, k, piece):
        for ref, lead in places:
            ref[lead + (c, h, pl.ds(8 * k, 8), slice(None))] = piece

    return store


def start_layer(store, force, coef, nk):
    for k in range(nk):
        for h in range(2):
            planes = turn(force(0, h, k), force(1, h, k), coef(0, h, k), coef(1, h, k))
            for c in range(2):
                store(c, h, k, planes[c])


def products(last, acc, place, weight, first, nk):
    for side in range(2):
        forward, adjoint = [piece_of(last, (side, pair)) for pair in range(2)]
        for h in range(2):
            for k in range(nk):
                fr, fi = forward(0, h, k), forward(1, h, k)
                ar, ai = adjoint(0, h, k), adjoint(1, h, k)
                terms = (weight * (fr * ar - fi * ai), weight * (fr * fr + fi * fi))
                for number, term in enumerate(terms):
                    at = (place, number, side, h, pl.ds(k, 8, stride=nk), slice(None))
                    acc[at] = jnp.where(first, term, acc[at] + term)


def write_out(out, acc, offset):
    bands, _, _, _, depth, _ = out.shape
    for band in range(bands):
        for place in range(acc.shape[0]):
            for number in range(2):
                for side in range(2):
                    for h in range(2):
                        out[band, offset + place, number, side, :, pl.ds(h * HALF, HALF)] = acc[
                            place, number, side, h, pl.ds(band * depth, depth), :
                        ]


def scale_of(freq, group):
    weight = 1.0 + freq[group].astype(jnp.float32) / 16.0
    return weight, 0.12 * weight


def parity():
    return lax.axis_index("sub") % 2


def paired(side):
    index = lax.axis_index("sub")
    there = index > 0 if side == 0 else index < lax.axis_size("sub") - 1
    return jnp.where(there, 1.0 / 64.0, 0.0)


def first_kernel(freq, sources, slowness, to_chip, to_core, raw, slow, coef, sems):
    groups, _, layers, rows = sources.shape[:4]
    nk = rows // 8
    places = (parity() * (layers - 1), (1 - parity()) * (layers - 1))
    copies = []
    for side, own in enumerate(places):
        for h in range(2):
            lanes = pl.ds(h * HALF, HALF)
            pairs = ((slowness.at[own, :, lanes], slow), (sources.at[:, :, own, :, lanes], raw))
            for number, (ref, held) in enumerate(pairs):
                copies.append(
                    pltpu.make_async_copy(ref, held.at[side, h], sems.at[side, h, number])
                )
    for copy in copies:
        copy.start()
    for side, out in enumerate((to_chip, to_core)):
        for copy in copies[4 * side : 4 * side + 4]:
            copy.wait()

        def sigma(h, k):
            return slow[side, h, pl.ds(k, 8, stride=nk), :]

        for h in range(2):
            for k in range(nk):
                out[4 * groups, h, pl.ds(8 * k, 8), :] = sigma(h, k)
        for group in range(groups):
            scale = scale_of(freq, group)[1]
            coefficients(store_to((coef, (side, group))), sigma, scale, 1.0 / 64.0, nk)
            for pair in range(2):
                start_layer(
                    store_from(out, (), 4 * group + 2 * pair),
                    row_piece((raw.at[side, 0], raw.at[side, 1]), (group,), 2 * pair, (), nk),
                    piece_of(coef, (side, group)),
                    nk,
                )


def store_from(ref, lead, offset):
    def store(c, h, k, piece):
        ref[lead + (offset + c, h, pl.ds(8 * k, 8), slice(None))] = piece

    return store


def sent_piece(ref, lead, offset):
    return lambda c, h, k: ref[lead + (offset + c, h, pl.ds(8 * k, 8), slice(None))]


def edge_kernel(freq, _, *refs):
    sides = []
    for side in range(2):
        part = refs[12 * side : 12 * side + 12]
        sides.append([[part[at + 2 * n : at + 2 * n + 2] for n in range(3)] for at in (0, 6)])
    far_chip, far_core, second, coef, one, fields = refs[24:]
    group = pl.program_id(0)
    rows = sides[0][1][0][0].shape[-2]
    nk = rows // 8
    marks = masks()
    scale = scale_of(freq, group)[1]
    chains = [(side, pair) for side in range(2) for pair in range(2)]

    def force(side, pair, at):
        return row_piece(sides[side][0][at], (0,), 2 * pair, (0,), nk)

    for side in range(2):
        for at in range(3):
            slows = sides[side][1][at]
            coefficients(
                store_to((coef, (side, at))),
                lambda h, k, slows=slows: slows[h][0, pl.ds(k, 8, stride=nk), :],
                scale,
                1.0 / 64.0,
                nk,
            )
            for pair in range(2):
                start_layer(
                    store_to((one, (side, pair, at))),
                    force(side, pair, at),
                    piece_of(coef, (side, at)),
                    nk,
                )
    for at in range(2):
        for side, pair in chains:
            near = [piece_of(one, (side, pair, n)) if n >= 0 else None for n in (at - 1, at, at + 1)]
            target = (fields, (side, 0, pair)) if at == 0 else (second, (0, pair, side))
            relax(
                store_to(target), force(side, pair, at), near, piece_of(coef, (side, at)), marks, nk
            )
    for side, pair in chains:
        near = [None, piece_of(fields, (side, 0, pair)), piece_of(second, (0, pair, side))]
        relax(
            store_to((fields, (side, 1, pair))),
            force(side, pair, 0),
            near,
            piece_of(coef, (side, 0)),
            marks,
            nk,
        )
    for out, side in ((far_chip, parity()), (far_core, 1 - parity())):
        for level in range(2):
            for pair in range(2):
                for c in range(2):
                    out[level, 0, 2 * pair + c] = fields[side, level, pair, c]


def inner_kernel(
    freq, src_l, src_r, slow_l, slow_r, second,
    out, two_next, three_near, three_far, coef, one, force, two, three, last, acc,
):
    group = pl.program_id(0)
    groups = pl.num_programs(0)
    layers, rows = src_l.shape[2], src_l.shape[3]
    nk = rows // 8
    marks = masks()
    weight, scale = scale_of(freq, group)
    weight = weight * 4096.0
    sources, slows = (src_l, src_r), (slow_l, slow_r)
    chains = [(side, pair) for side in range(2) for pair in range(2)]

    @pl.loop(0, layers - 2)
    def _(place):
        layer = place + 1
        coefficients(
            store_to((coef, (layer,))),
            lambda h, k: slows[h][layer, pl.ds(k, 8, stride=nk), :],
            scale,
            1.0 / 64.0,
            nk,
        )
        for pair in range(2):
            rows_of = row_piece(sources, (0,), 2 * pair, (layer,), nk)
            keep = store_to((force, (pair, layer)))
            for c in range(2):
                for h in range(2):
                    for k in range(nk):
                        keep(c, h, k, rows_of(c, h, k))
            start_layer(store_to((one, (pair, layer))), rows_of, piece_of(coef, (layer,)), nk)

    def copy_plane(keep, given):
        for c in range(2):
            for h in range(2):
                for k in range(nk):
                    keep(c, h, k, given(c, h, k))

    def layer_at(side, at):
        return at if side == 0 else layers - 1 - at

    def step(target, pair, layer, ref, skip):
        near = [piece_of(ref, (pair, layer + shift - skip)) for shift in (-1, 0, 1)]
        relax(
            store_to(target),
            piece_of(force, (pair, layer)),
            near,
            piece_of(coef, (layer,)),
            marks,
            nk,
        )

    for side, pair in chains:
        copy_plane(
            store_to((two, (pair, layer_at(side, 1)))), piece_of(second, (0, pair, side))
        )

    @pl.loop(0, (layers - 4) // 2)
    def _(turn_at):
        for offset in range(2):
            for pair in range(2):
                layer = 2 + 2 * turn_at + offset
                step((two, (pair, layer)), pair, layer, one, 0)

    @pl.loop(0, (layers - 4) // 2)
    def _(turn_at):
        for offset in range(2):
            for pair in range(2):
                layer = 2 + 2 * turn_at + offset
                step((three, (pair, layer - 2)), pair, layer, two, 0)

    for side, pair in chains:
        step((last, (side, pair)), pair, layers // 2 - 1 + side, three, 2)
        for keep, ref, at in (
            (two_next, two, layer_at(side, 2)),
            (three_near, three, layer_at(side, 2) - 2),
            (three_far, three, layer_at(side, 3) - 2),
        ):
            copy_plane(store_to((keep, (0, pair, side))), piece_of(ref, (pair, at)))
    products(last, acc, 0, weight, group == 0, nk)

    @pl.when(group == groups - 1)
    def _():
        write_out(out, acc, 0)


def middle_kernel(freq, *refs):
    sides = []
    for side in range(2):
        part = refs[12 * side : 12 * side + 12]
        sides.append([[part[at + 2 * n : at + 2 * n + 2] for n in range(3)] for at in (0, 6)])
    core_field, core_slow, chip_field, chip_slow, second, two_next, three_near, three_far = refs[24:32]
    out, base_three, base_next, base_four, factors = refs[32:37]
    force, beyond, one, first_two, first_three, halo, halo_slow, change, last, acc = refs[37:]
    group = pl.program_id(0)
    groups = pl.num_programs(0)
    rows = second.shape[-2]
    nk = rows // 8
    marks = masks()
    weight, scale = scale_of(freq, group)
    weight = weight * 4096.0
    chains = [(side, pair) for side in range(2) for pair in range(2)]
    to_chip, to_core = parity(), 1 - parity()
    halo[to_core] = core_field[...]
    halo[to_chip] = chip_field[...]
    halo_slow[to_core] = core_slow[0]
    halo_slow[to_chip] = chip_slow[0]

    for side in range(2):
        coefficients(
            store_to((beyond, (side,))),
            lambda h, k, side=side: halo_slow[side, h, pl.ds(8 * k, 8), :],
            scale,
            paired(side),
            nk,
        )
        for at in range(3):
            slows = sides[side][1][at]
            coefficients(
                store_to((factors, (0, side, at))),
                lambda h, k, slows=slows: slows[h][0, pl.ds(k, 8, stride=nk), :],
                scale,
                1.0 / 64.0,
                nk,
            )
            for pair in range(2):
                rows_of = row_piece(sides[side][0][at], (0,), 2 * pair, (0,), nk)
                keep = store_to((force, (side, pair, at)))
                for c in range(2):
                    for h in range(2):
                        for k in range(nk):
                            keep(c, h, k, rows_of(c, h, k))
                if at < 2:
                    start_layer(
                        store_to((one, (side, pair, at))),
                        rows_of,
                        piece_of(factors, (0, side, at)),
                        nk,
                    )

    def step(target, side, pair, at, near):
        relax(
            store_to(target),
            piece_of(force, (side, pair, at)),
            near,
            piece_of(factors, (0, side, at)),
            marks,
            nk,
        )

    def held(ref, side, pair):
        return piece_of(ref, (0, pair, side))

    for side, pair in chains:
        near = [sent_piece(halo, (side,), 2 * pair)]
        near += [piece_of(one, (side, pair, at)) for at in range(2)]
        step((first_two, (side, pair)), side, pair, 0, near)
    for side, pair in chains:
        near = [None, None, piece_of(one, (side, pair, 0))]
        relax(store_to((change, (0, side, pair))), None, near, piece_of(beyond, (side,)), marks, nk)
    for side, pair in chains:
        near = [
            piece_of(first_two, (side, pair)),
            held(second, side, pair),
            held(two_next, side, pair),
        ]
        step((first_three, (side, pair)), side, pair, 1, near)
    for side, pair in chains:
        near = [
            None,
            piece_of(change, (0, side, pair)),
            piece_of(first_two, (side, pair)),
        ]
        relax(store_to((change, (1, side, pair))), None, near, piece_of(beyond, (side,)), marks, nk)
    for side, pair in chains:
        three = piece_of(first_three, (side, pair))
        near = [three, held(three_near, side, pair), held(three_far, side, pair)]
        step((last, (side, pair)), side, pair, 2, near)
    products(last, acc, 0, weight, group == 0, nk)
    for side, pair in chains:
        three = piece_of(first_three, (side, pair))
        twos = [piece_of(first_two, (side, pair)), held(second, side, pair)]
        changes = [piece_of(change, (number, side, pair)) for number in range(2)]
        for target, at, near in (
            (base_three, 0, [changes[0], *twos]),
            (base_next, 1, [None, three, held(three_near, side, pair)]),
            (base_four, 0, [changes[1], None, three]),
        ):
            step((target, (0, pair, side)), side, pair, at, near)

    @pl.when(group == groups - 1)
    def _():
        write_out(out, acc, 0)


def outer_kernel(freq, core, chip, base_three, base_next, base_four, factors, out, sent_fields, fresh, last, acc):
    group = pl.program_id(0)
    groups = pl.num_programs(0)
    rows = base_three.shape[-2]
    nk = rows // 8
    marks = masks()
    weight = scale_of(freq, group)[0] * 4096.0
    chains = [(side, pair) for side in range(2) for pair in range(2)]
    to_chip, to_core = parity(), 1 - parity()
    for number in range(2):
        sent_fields[to_core, number] = core[number, 0]
        sent_fields[to_chip, number] = chip[number, 0]

    def step(target, base, side, pair, at, near):
        relax(
            store_to(target),
            None,
            near,
            piece_of(factors, (0, side, at)),
            marks,
            nk,
            base=piece_of(base, (0, pair, side)),
        )

    for side, pair in chains:
        near = [sent_piece(sent_fields, (side, 0), 2 * pair), None, None]
        step((fresh, (side, pair)), base_three, side, pair, 0, near)
    for side, pair in chains:
        near = [piece_of(fresh, (side, pair)), None, None]
        step((last, (0, side, pair)), base_next, side, pair, 1, near)
    for side, pair in chains:
        near = [sent_piece(sent_fields, (side, 1), 2 * pair), piece_of(fresh, (side, pair)), None]
        step((last, (1, side, pair)), base_four, side, pair, 0, near)
    for place in range(2):
        products(last.at[place], acc, place, weight, group == 0, nk)

    @pl.when(group == groups - 1)
    def _():
        write_out(out, acc, 0)


def precond_kernel(pick, *refs):
    chunks, (precond, outgoing) = refs[:-2], refs[-2:]
    layers = precond.shape[0]
    step = 0
    for chunk in chunks:
        for place in range(chunk.shape[1]):
            for side in range(2):
                layer = layers // 2 - 1 - step if side == 0 else layers // 2 + step
                grad = chunk[0, place, 0, side]
                illum = chunk[0, place, 1, side]
                for other in range(1, chunk.shape[0]):
                    grad = grad + chunk[other, place, 0, side]
                    illum = illum + chunk[other, place, 1, side]
                precond[layer] = grad / jnp.sqrt(illum + 1.0)
            step += 1

    @pl.loop(0, outgoing.shape[0])
    def _(slot):
        outgoing[slot] = precond[pick[slot]]


def deliver_kernel(slots, incoming, out):
    @pl.loop(0, out.shape[2])
    def _(number):
        out[0, 0, number] = incoming[slots[number]]


def smem():
    return pl.BlockSpec(memory_space=pltpu.SMEM)


def vmem():
    return pl.BlockSpec(memory_space=pltpu.VMEM)


def plane_scratch(*lead, rows):
    return pltpu.VMEM(lead + (2, rows, HALF), jnp.float32)


def compiler_params(mebibytes):
    return pltpu.CompilerParams(vmem_limit_bytes=mebibytes * 1024 * 1024)


def light(size=1000):
    return pl.CostEstimate(flops=1000, bytes_accessed=size, transcendentals=0)


def in_hbm(array):
    return pltpu.with_memory_space_constraint(array, pltpu.HBM)


def hbm(*shape):
    return pltpu.HBM(shape, jnp.float32)


def state(groups, rows):
    return (
        hbm(groups, 2, 2, 2, 2, rows, HALF),
        pl.BlockSpec((1, 2, 2, 2, 2, rows, HALF), lambda g: (g, 0, 0, 0, 0, 0, 0)),
    )


def sent(groups, rows):
    return (
        hbm(2, groups, 4, 2, rows, HALF),
        pl.BlockSpec((2, 1, 4, 2, rows, HALF), lambda g: (0, g, 0, 0, 0, 0)),
    )


def factor_state(groups, rows):
    return (
        hbm(groups, 2, 3, 2, 2, rows, HALF),
        pl.BlockSpec((1, 2, 3, 2, 2, rows, HALF), lambda g: (g, 0, 0, 0, 0, 0, 0)),
    )


def sums(bands, rows, columns, steps=1):
    shape = (bands, steps, 2, 2, rows // bands, columns)
    return hbm(*shape), pl.BlockSpec(shape, lambda g: (0,) * 6)


def split(pairs):
    return dict(out_shape=[p[0] for p in pairs], out_specs=[p[1] for p in pairs])


def layer_specs(sources, own):
    rows = sources.shape[3]
    return (
        [pl.BlockSpec((1, 4, 1, rows, HALF), lambda g, h=h: (g, 0, own, 0, h)) for h in range(2)],
        [pl.BlockSpec((1, rows, HALF), lambda g, h=h: (own, 0, h)) for h in range(2)],
    )


def first_edges(freq, sources, slowness):
    groups, _, _, rows, _ = sources.shape
    anywhere = pl.BlockSpec(memory_space=pl.ANY)
    return pl.pallas_call(
        first_kernel,
        in_specs=[smem(), anywhere, anywhere],
        out_specs=[vmem()] * 2,
        out_shape=[hbm(4 * groups + 1, 2, rows, HALF)] * 2,
        scratch_shapes=[
            pltpu.VMEM((2, 2, groups, 4, rows, HALF), jnp.float32),
            plane_scratch(2, rows=rows),
            plane_scratch(2, groups, 2, rows=rows),
            pltpu.SemaphoreType.DMA((2, 2, 2)),
        ],
        compiler_params=compiler_params(8),
        cost_estimate=light(),
        name="first",
    )(freq, in_hbm(sources), in_hbm(slowness))


def edge_layers(sources, slowness):
    layers = sources.shape[2]
    sources, slowness = in_hbm(sources), in_hbm(slowness)
    operands, specs = [], []
    for side in range(2):
        parts = [layer_specs(sources, at if side == 0 else layers - 1 - at) for at in range(3)]
        for what, array in enumerate((sources, slowness)):
            for part in parts:
                operands += [array] * 2
                specs += part[what]
    return operands, specs


def later_edges(freq, sources, slowness, first):
    groups, _, _, rows, _ = sources.shape
    operands, specs = edge_layers(sources, slowness)
    operands = [freq, in_hbm(first)] + operands
    specs = [smem(), pl.BlockSpec(memory_space=pl.ANY)] + specs
    return pl.pallas_call(
        edge_kernel,
        grid=(groups,),
        in_specs=specs,
        **split([sent(groups, rows)] * 2 + [state(groups, rows)]),
        scratch_shapes=[
            plane_scratch(2, 3, 2, rows=rows),
            plane_scratch(2, 2, 3, 2, rows=rows),
            plane_scratch(2, 2, 2, 2, rows=rows),
        ],
        compiler_params=compiler_params(32),
        cost_estimate=light(),
        name="edges",
    )(*operands)


def inner(freq, sources, slowness, second, bands):
    groups, _, layers, rows, columns = sources.shape
    half = [
        pl.BlockSpec((1, 4, layers, rows, HALF), lambda g, h=h: (g, 0, 0, 0, h)) for h in range(2)
    ]
    slow = [pl.BlockSpec((layers, rows, HALF), lambda g, h=h: (0, 0, h)) for h in range(2)]
    sources, slowness = in_hbm(sources), in_hbm(slowness)
    return pl.pallas_call(
        inner_kernel,
        grid=(groups,),
        in_specs=[smem()] + half + slow + [state(groups, rows)[1]],
        **split([sums(bands, rows, columns)] + [state(groups, rows)] * 3),
        scratch_shapes=[
            plane_scratch(layers, 2, rows=rows),
            plane_scratch(2, layers, 2, rows=rows),
            plane_scratch(2, layers, 2, rows=rows),
            plane_scratch(2, layers, 2, rows=rows),
            plane_scratch(2, layers - 4, 2, rows=rows),
            plane_scratch(2, 2, 2, rows=rows),
            plane_scratch(1, 2, 2, rows=rows),
        ],
        compiler_params=compiler_params(40),
        cost_estimate=light(),
        name="inner",
    )(freq, sources, sources, slowness, slowness, in_hbm(second))


def middle(freq, sources, slowness, from_core, from_chip, held, bands):
    groups, _, _, rows, columns = sources.shape
    operands, specs = edge_layers(sources, slowness)
    near = [
        pl.BlockSpec((4, 2, rows, HALF), lambda g: (g, 0, 0, 0)),
        pl.BlockSpec((1, 2, rows, HALF), lambda g: (4 * groups, 0, 0, 0)),
    ]
    return pl.pallas_call(
        middle_kernel,
        grid=(groups,),
        in_specs=[smem()] + specs + near * 2 + [state(groups, rows)[1]] * 4,
        **split(
            [sums(bands, rows, columns)] + [state(groups, rows)] * 3 + [factor_state(groups, rows)]
        ),
        scratch_shapes=[
            plane_scratch(2, 2, 3, 2, rows=rows),
            plane_scratch(2, 2, rows=rows),
            plane_scratch(2, 2, 2, 2, rows=rows),
            plane_scratch(2, 2, 2, rows=rows),
            plane_scratch(2, 2, 2, rows=rows),
            plane_scratch(2, 4, rows=rows),
            plane_scratch(2, rows=rows),
            plane_scratch(2, 2, 2, 2, rows=rows),
            plane_scratch(2, 2, 2, rows=rows),
            plane_scratch(1, 2, 2, rows=rows),
        ],
        compiler_params=compiler_params(40),
        cost_estimate=light(100_000_000),
        name="middle",
    )(
        freq, *operands, from_core, from_core, from_chip, from_chip,
        *[in_hbm(array) for array in held],
    )


def outer(freq, from_core, from_chip, held, bands, rows, columns):
    groups = from_core.shape[1]
    return pl.pallas_call(
        outer_kernel,
        grid=(groups,),
        in_specs=[smem()] + [sent(groups, rows)[1]] * 2 + [state(groups, rows)[1]] * 3
        + [factor_state(groups, rows)[1]],
        **split([sums(bands, rows, columns, 2)]),
        scratch_shapes=[
            plane_scratch(2, 2, 4, rows=rows),
            plane_scratch(2, 2, 2, rows=rows),
            plane_scratch(2, 2, 2, 2, rows=rows),
            plane_scratch(2, 2, 2, rows=rows),
        ],
        compiler_params=compiler_params(32),
        cost_estimate=light(),
        name="outer",
    )(freq, from_core, from_chip, *[in_hbm(array) for array in held])[0]


def route(coverage, own_index):
    lists = coverage[0]
    owner, local = lists // TPD, lists % TPD
    position = jnp.arange(lists.shape[1], dtype=jnp.int32)
    same_owner = owner[:, :, None] == owner[:, None, :]
    earlier = position[None, :] < position[:, None]
    rank = jnp.sum((same_owner & earlier[None]).astype(jnp.int32), axis=2)
    slots = jnp.arange(CAP, dtype=jnp.int32)
    hit = (owner == own_index)[:, :, None] & (rank[:, :, None] == slots[None, None, :])
    pick = jnp.sum(jnp.where(hit, local[:, :, None], 0), axis=1).reshape(-1)
    own_slots = owner * CAP + rank
    return pick, lax.dynamic_index_in_dim(own_slots, own_index, 0, keepdims=False)


def body(sources, slowness, freq_index, coverage):
    groups, _, layers, rows, columns = sources.shape
    bands, members = lax.axis_size("freq"), lax.axis_size("sub")
    own_index = lax.axis_index("sub")
    cores = [(i, i ^ 1) for i in range(members)]
    chips = [(i, i + step) for i in range(members) for step in (2 * (i % 2) - 1,) if 0 <= i + step < members]
    def exchange(to_chip, to_core):
        return lax.ppermute(to_chip, "sub", chips), lax.ppermute(to_core, "sub", cores)

    near = first_edges(freq_index, sources, slowness)
    near_chip, near_core = exchange(*near)
    *edges, second = later_edges(freq_index, sources, slowness, near[0])
    far_chip, far_core = exchange(*edges)
    pick, slots = route(coverage, own_index)

    def spread(chunk):
        return lax.all_to_all(chunk, "freq", split_axis=0, concat_axis=0, tiled=True)

    def spread_next(chunk):
        if chunks:
            chunks[-1], chunk = lax.optimization_barrier((chunks[-1], chunk))
        chunks.append(spread(chunk))

    chunks = []
    chunk, *held = inner(freq_index, sources, slowness, second, bands)
    chunk, near_chip, near_core = lax.optimization_barrier((chunk, near_chip, near_core))
    spread_next(chunk)
    held = [second] + held
    chunk, *held = middle(freq_index, sources, slowness, near_core, near_chip, held, bands)
    spread_next(chunk)
    spread_next(outer(freq_index, far_core, far_chip, held, bands, rows, columns))
    depth = rows // bands
    precond, outgoing = pl.pallas_call(
        precond_kernel,
        in_specs=[smem()] + [vmem()] * len(chunks),
        out_specs=[vmem()] * 2,
        out_shape=[
            jax.ShapeDtypeStruct((layers, depth, columns), jnp.float32),
            jax.ShapeDtypeStruct((members * CAP, depth, columns), jnp.float32),
        ],
        compiler_params=compiler_params(12),
        name="precond",
    )(pick, *chunks)
    incoming = lax.all_to_all(outgoing, "sub", split_axis=0, concat_axis=0, tiled=True)
    delivered = pl.pallas_call(
        deliver_kernel,
        in_specs=[smem(), vmem()],
        out_specs=vmem(),
        out_shape=jax.ShapeDtypeStruct((1, 1, coverage.shape[2], depth, columns), jnp.float32),
        compiler_params=compiler_params(12),
        name="deliver",
    )(slots, incoming)
    return precond, delivered


def solution(mesh):
    placed = (
        P("freq", None, "sub", None, None),
        P("sub", None, None),
        P("freq"),
        P("freq", None, None),
    )
    return jax.shard_map(
        body,
        mesh=mesh,
        in_specs=placed,
        out_specs=(P("sub", "freq", None), P("freq", "sub", None, None, None)),
        check_vma=False,
    )
```

```python
import functools

import jax
import jax.numpy as jnp
from jax import lax
from jax.experimental import pallas as pl
from jax.experimental.pallas import tpu as pltpu
from jax.sharding import PartitionSpec as P

TPD = 8
CAP = 2
HALF = 128


def masks():
    lane = lax.broadcasted_iota(jnp.int32, (8, HALF), 1)
    row = lax.broadcasted_iota(jnp.int32, (8, HALF), 0)
    return lane == 0, lane == HALF - 1, row == 0, row == 7


def turn(real, imag, coef_real, coef_imag):
    return real * coef_real + imag * coef_imag, imag * coef_real - real * coef_imag


def coefficients(store, slow, scale, factor, nk):
    for k in range(nk):
        for h in range(2):
            sigma = scale * slow(h, k)
            diag = 0.875 - sigma
            inverse = factor / (diag * diag + sigma * sigma)
            store(0, h, k, diag * inverse)
            store(1, h, k, sigma * inverse)


def relax(store, force, near, coef, marks, nk, base=None):
    lane_first, lane_last, row_first, row_last = marks

    def across(c, h, k):
        before, middle, after = [None if layer is None else layer(c, h, k) for layer in near]
        parts = [part for part in (before, after) if part is not None]
        if middle is not None:
            parts.append(middle + middle)
        return functools.reduce(lambda total, part: total + part, parts)

    both = [(c, h) for c in range(2) for h in range(2)]
    top = {at: across(*at, 0) for at in both}
    bottom = {at: across(*at, nk - 1) for at in both}
    here = top
    pair = {at: jnp.where(row_first, 0.0, pltpu.roll(bottom[at], 1, 0)) + top[at] for at in both}
    for k in range(nk):
        if k < nk - 2:
            following = {at: across(*at, k + 1) for at in both}
        elif k == nk - 2:
            following = bottom
        else:
            following = {at: jnp.where(row_last, 0.0, pltpu.roll(top[at], 7, 0)) for at in both}
        terms = []
        for c in range(2):
            depth = []
            for h in range(2):
                later = here[c, h] + following[c, h]
                depth.append(pair[c, h] + later)
                pair[c, h] = later
            left, right = depth
            left_up, right_up = pltpu.roll(left, HALF - 1, 1), pltpu.roll(right, HALF - 1, 1)
            left_down, right_down = pltpu.roll(left, 1, 1), pltpu.roll(right, 1, 1)
            left_sides = jnp.where(lane_last, right_up, left_up) + jnp.where(lane_first, 0.0, left_down)
            right_sides = jnp.where(lane_last, 0.0, right_up) + jnp.where(
                lane_first, left_down, right_down
            )
            for h, (middle, ends) in enumerate(((left, left_sides), (right, right_sides))):
                total = ends + (middle + middle)
                if near[1] is not None:
                    total = total - 8.0 * near[1](c, h, k)
                terms.append(total if force is None else force(c, h, k) + total)
        here = following
        for h in range(2):
            planes = turn(terms[h], terms[2 + h], coef(0, h, k), coef(1, h, k))
            for c in range(2):
                store(c, h, k, planes[c] if base is None else base(c, h, k) + planes[c])


def piece_of(ref, lead):
    return lambda c, h, k: ref[lead + (c, h, pl.ds(8 * k, 8), slice(None))]


def row_piece(refs, lead, offset, tail, nk):
    return lambda c, h, k: refs[h][
        lead + (offset + c,) + tail + (pl.ds(k, 8, stride=nk), slice(None))
    ]


def store_to(*places):
    def store(c, h, k, piece):
        for ref, lead in places:
            ref[lead + (c, h, pl.ds(8 * k, 8), slice(None))] = piece

    return store


def start_layer(store, force, coef, nk):
    for k in range(nk):
        for h in range(2):
            planes = turn(force(0, h, k), force(1, h, k), coef(0, h, k), coef(1, h, k))
            for c in range(2):
                store(c, h, k, planes[c])


def products(last, acc, place, weight, first, nk):
    for side in range(2):
        forward, adjoint = [piece_of(last, (side, pair)) for pair in range(2)]
        for h in range(2):
            for k in range(nk):
                fr, fi = forward(0, h, k), forward(1, h, k)
                ar, ai = adjoint(0, h, k), adjoint(1, h, k)
                terms = (weight * (fr * ar - fi * ai), weight * (fr * fr + fi * fi))
                for number, term in enumerate(terms):
                    at = (place, number, side, h, pl.ds(k, 8, stride=nk), slice(None))
                    acc[at] = jnp.where(first, term, acc[at] + term)


def write_out(out, acc, offset):
    bands, _, _, _, depth, _ = out.shape
    for band in range(bands):
        for place in range(acc.shape[0]):
            for number in range(2):
                for side in range(2):
                    for h in range(2):
                        out[band, offset + place, number, side, :, pl.ds(h * HALF, HALF)] = acc[
                            place, number, side, h, pl.ds(band * depth, depth), :
                        ]


def scale_of(freq, group):
    weight = 1.0 + freq[group].astype(jnp.float32) / 16.0
    return weight, 0.12 * weight


def parity():
    return lax.axis_index("sub") % 2


def paired(side):
    index = lax.axis_index("sub")
    there = index > 0 if side == 0 else index < lax.axis_size("sub") - 1
    return jnp.where(there, 1.0 / 64.0, 0.0)


def first_kernel(freq, sources, slowness, to_chip, to_core, raw, slow, coef, sems):
    groups, _, layers, rows = sources.shape[:4]
    nk = rows // 8
    places = (parity() * (layers - 1), (1 - parity()) * (layers - 1))
    copies = []
    for side, own in enumerate(places):
        for h in range(2):
            lanes = pl.ds(h * HALF, HALF)
            pairs = ((slowness.at[own, :, lanes], slow), (sources.at[:, :, own, :, lanes], raw))
            for number, (ref, held) in enumerate(pairs):
                copies.append(
                    pltpu.make_async_copy(ref, held.at[side, h], sems.at[side, h, number])
                )
    for copy in copies:
        copy.start()
    for side, out in enumerate((to_chip, to_core)):
        for copy in copies[4 * side : 4 * side + 4]:
            copy.wait()

        def sigma(h, k):
            return slow[side, h, pl.ds(k, 8, stride=nk), :]

        for h in range(2):
            for k in range(nk):
                out[4 * groups, h, pl.ds(8 * k, 8), :] = sigma(h, k)
        for group in range(groups):
            scale = scale_of(freq, group)[1]
            coefficients(store_to((coef, (side, group))), sigma, scale, 1.0 / 64.0, nk)
            for pair in range(2):
                start_layer(
                    store_from(out, (), 4 * group + 2 * pair),
                    row_piece((raw.at[side, 0], raw.at[side, 1]), (group,), 2 * pair, (), nk),
                    piece_of(coef, (side, group)),
                    nk,
                )


def store_from(ref, lead, offset):
    def store(c, h, k, piece):
        ref[lead + (offset + c, h, pl.ds(8 * k, 8), slice(None))] = piece

    return store


def sent_piece(ref, lead, offset):
    return lambda c, h, k: ref[lead + (offset + c, h, pl.ds(8 * k, 8), slice(None))]


def edge_kernel(freq, _, *refs):
    sides = []
    for side in range(2):
        part = refs[12 * side : 12 * side + 12]
        sides.append([[part[at + 2 * n : at + 2 * n + 2] for n in range(3)] for at in (0, 6)])
    far_chip, far_core, second, coef, one, fields = refs[24:]
    group = pl.program_id(0)
    rows = sides[0][1][0][0].shape[-2]
    nk = rows // 8
    marks = masks()
    scale = scale_of(freq, group)[1]
    chains = [(side, pair) for side in range(2) for pair in range(2)]

    def force(side, pair, at):
        return row_piece(sides[side][0][at], (0,), 2 * pair, (0,), nk)

    for side in range(2):
        for at in range(3):
            slows = sides[side][1][at]
            coefficients(
                store_to((coef, (side, at))),
                lambda h, k, slows=slows: slows[h][0, pl.ds(k, 8, stride=nk), :],
                scale,
                1.0 / 64.0,
                nk,
            )
            for pair in range(2):
                start_layer(
                    store_to((one, (side, pair, at))),
                    force(side, pair, at),
                    piece_of(coef, (side, at)),
                    nk,
                )
    for at in range(2):
        for side, pair in chains:
            near = [piece_of(one, (side, pair, n)) if n >= 0 else None for n in (at - 1, at, at + 1)]
            target = (fields, (side, 0, pair)) if at == 0 else (second, (0, pair, side))
            relax(
                store_to(target), force(side, pair, at), near, piece_of(coef, (side, at)), marks, nk
            )
    for side, pair in chains:
        near = [None, piece_of(fields, (side, 0, pair)), piece_of(second, (0, pair, side))]
        relax(
            store_to((fields, (side, 1, pair))),
            force(side, pair, 0),
            near,
            piece_of(coef, (side, 0)),
            marks,
            nk,
        )
    for out, side in ((far_chip, parity()), (far_core, 1 - parity())):
        for level in range(2):
            for pair in range(2):
                for c in range(2):
                    out[level, 0, 2 * pair + c] = fields[side, level, pair, c]


def inner_kernel(
    freq, src_l, src_r, slow_l, slow_r, second,
    out, two_next, three_near, three_far, coef, one, force, two, three, last, acc,
):
    group = pl.program_id(0)
    groups = pl.num_programs(0)
    layers, rows = src_l.shape[2], src_l.shape[3]
    nk = rows // 8
    marks = masks()
    weight, scale = scale_of(freq, group)
    weight = weight * 4096.0
    sources, slows = (src_l, src_r), (slow_l, slow_r)
    chains = [(side, pair) for side in range(2) for pair in range(2)]

    @pl.loop(0, layers - 2)
    def _(place):
        layer = place + 1
        coefficients(
            store_to((coef, (layer,))),
            lambda h, k: slows[h][layer, pl.ds(k, 8, stride=nk), :],
            scale,
            1.0 / 64.0,
            nk,
        )
        for pair in range(2):
            rows_of = row_piece(sources, (0,), 2 * pair, (layer,), nk)
            keep = store_to((force, (pair, layer)))
            for c in range(2):
                for h in range(2):
                    for k in range(nk):
                        keep(c, h, k, rows_of(c, h, k))
            start_layer(store_to((one, (pair, layer))), rows_of, piece_of(coef, (layer,)), nk)

    def copy_plane(keep, given):
        for c in range(2):
            for h in range(2):
                for k in range(nk):
                    keep(c, h, k, given(c, h, k))

    def layer_at(side, at):
        return at if side == 0 else layers - 1 - at

    def step(target, pair, layer, ref, skip):
        near = [piece_of(ref, (pair, layer + shift - skip)) for shift in (-1, 0, 1)]
        relax(
            store_to(target),
            piece_of(force, (pair, layer)),
            near,
            piece_of(coef, (layer,)),
            marks,
            nk,
        )

    for side, pair in chains:
        copy_plane(
            store_to((two, (pair, layer_at(side, 1)))), piece_of(second, (0, pair, side))
        )

    @pl.loop(0, (layers - 4) // 2)
    def _(turn_at):
        for offset in range(2):
            for pair in range(2):
                layer = 2 + 2 * turn_at + offset
                step((two, (pair, layer)), pair, layer, one, 0)

    @pl.loop(0, (layers - 4) // 2)
    def _(turn_at):
        for offset in range(2):
            for pair in range(2):
                layer = 2 + 2 * turn_at + offset
                step((three, (pair, layer - 2)), pair, layer, two, 0)

    for side, pair in chains:
        step((last, (side, pair)), pair, layers // 2 - 1 + side, three, 2)
        for keep, ref, at in (
            (two_next, two, layer_at(side, 2)),
            (three_near, three, layer_at(side, 2) - 2),
            (three_far, three, layer_at(side, 3) - 2),
        ):
            copy_plane(store_to((keep, (0, pair, side))), piece_of(ref, (pair, at)))
    products(last, acc, 0, weight, group == 0, nk)

    @pl.when(group == groups - 1)
    def _():
        write_out(out, acc, 0)


def middle_kernel(freq, *refs):
    sides = []
    for side in range(2):
        part = refs[12 * side : 12 * side + 12]
        sides.append([[part[at + 2 * n : at + 2 * n + 2] for n in range(3)] for at in (0, 6)])
    core_field, core_slow, chip_field, chip_slow, second, two_next, three_near, three_far = refs[24:32]
    out, base_three, base_next, base_four, factors = refs[32:37]
    force, beyond, one, first_two, first_three, halo, halo_slow, change, last, acc = refs[37:]
    group = pl.program_id(0)
    groups = pl.num_programs(0)
    rows = second.shape[-2]
    nk = rows // 8
    marks = masks()
    weight, scale = scale_of(freq, group)
    weight = weight * 4096.0
    chains = [(side, pair) for side in range(2) for pair in range(2)]
    to_chip, to_core = parity(), 1 - parity()
    halo[to_core] = core_field[...]
    halo[to_chip] = chip_field[...]
    halo_slow[to_core] = core_slow[0]
    halo_slow[to_chip] = chip_slow[0]

    for side in range(2):
        coefficients(
            store_to((beyond, (side,))),
            lambda h, k, side=side: halo_slow[side, h, pl.ds(8 * k, 8), :],
            scale,
            paired(side),
            nk,
        )
        for at in range(3):
            slows = sides[side][1][at]
            coefficients(
                store_to((factors, (0, side, at))),
                lambda h, k, slows=slows: slows[h][0, pl.ds(k, 8, stride=nk), :],
                scale,
                1.0 / 64.0,
                nk,
            )
            for pair in range(2):
                rows_of = row_piece(sides[side][0][at], (0,), 2 * pair, (0,), nk)
                keep = store_to((force, (side, pair, at)))
                for c in range(2):
                    for h in range(2):
                        for k in range(nk):
                            keep(c, h, k, rows_of(c, h, k))
                if at < 2:
                    start_layer(
                        store_to((one, (side, pair, at))),
                        rows_of,
                        piece_of(factors, (0, side, at)),
                        nk,
                    )

    def step(target, side, pair, at, near):
        relax(
            store_to(target),
            piece_of(force, (side, pair, at)),
            near,
            piece_of(factors, (0, side, at)),
            marks,
            nk,
        )

    def held(ref, side, pair):
        return piece_of(ref, (0, pair, side))

    for side, pair in chains:
        near = [sent_piece(halo, (side,), 2 * pair)]
        near += [piece_of(one, (side, pair, at)) for at in range(2)]
        step((first_two, (side, pair)), side, pair, 0, near)
    for side, pair in chains:
        near = [None, None, piece_of(one, (side, pair, 0))]
        relax(store_to((change, (0, side, pair))), None, near, piece_of(beyond, (side,)), marks, nk)
    for side, pair in chains:
        near = [
            piece_of(first_two, (side, pair)),
            held(second, side, pair),
            held(two_next, side, pair),
        ]
        step((first_three, (side, pair)), side, pair, 1, near)
    for side, pair in chains:
        near = [
            None,
            piece_of(change, (0, side, pair)),
            piece_of(first_two, (side, pair)),
        ]
        relax(store_to((change, (1, side, pair))), None, near, piece_of(beyond, (side,)), marks, nk)
    for side, pair in chains:
        three = piece_of(first_three, (side, pair))
        near = [three, held(three_near, side, pair), held(three_far, side, pair)]
        step((last, (side, pair)), side, pair, 2, near)
    products(last, acc, 0, weight, group == 0, nk)
    for side, pair in chains:
        three = piece_of(first_three, (side, pair))
        twos = [piece_of(first_two, (side, pair)), held(second, side, pair)]
        changes = [piece_of(change, (number, side, pair)) for number in range(2)]
        for target, at, near in (
            (base_three, 0, [changes[0], *twos]),
            (base_next, 1, [None, three, held(three_near, side, pair)]),
            (base_four, 0, [changes[1], None, three]),
        ):
            step((target, (0, pair, side)), side, pair, at, near)

    @pl.when(group == groups - 1)
    def _():
        write_out(out, acc, 0)


def write_halves(keep, send, acc, place):
    depth = keep.shape[-2]
    odd = lax.axis_index("freq") % 2
    for out, parity_of in ((keep, odd), (send, 1 - odd)):
        for high in range(2):
            start = pl.multiple_of((2 * high + parity_of) * depth, 8)
            for number in range(2):
                for side in range(2):
                    for h in range(2):
                        out[high, number, side, :, pl.ds(h * HALF, HALF)] = acc[
                            place, number, side, h, pl.ds(start, depth), :
                        ]


def outer_kernel(freq, core, chip, base_three, base_next, base_four, factors, *rest):
    outs, (sent_fields, fresh, last, acc) = rest[:4], rest[4:]
    group = pl.program_id(0)
    groups = pl.num_programs(0)
    rows = base_three.shape[-2]
    nk = rows // 8
    marks = masks()
    weight = scale_of(freq, group)[0] * 4096.0
    chains = [(side, pair) for side in range(2) for pair in range(2)]
    to_chip, to_core = parity(), 1 - parity()
    for number in range(2):
        sent_fields[to_core, number] = core[number, 0]
        sent_fields[to_chip, number] = chip[number, 0]

    def step(target, base, side, pair, at, near):
        relax(
            store_to(target),
            None,
            near,
            piece_of(factors, (0, side, at)),
            marks,
            nk,
            base=piece_of(base, (0, pair, side)),
        )

    for side, pair in chains:
        near = [sent_piece(sent_fields, (side, 0), 2 * pair), None, None]
        step((fresh, (side, pair)), base_three, side, pair, 0, near)
    for side, pair in chains:
        near = [piece_of(fresh, (side, pair)), None, None]
        step((last, (0, side, pair)), base_next, side, pair, 1, near)
    for side, pair in chains:
        near = [sent_piece(sent_fields, (side, 1), 2 * pair), piece_of(fresh, (side, pair)), None]
        step((last, (1, side, pair)), base_four, side, pair, 0, near)
    for place in range(2):
        products(last.at[place], acc, place, weight, group == 0, nk)

    @pl.when(group == groups - 1)
    def _():
        for place in range(2):
            write_halves(*outs[2 * place : 2 * place + 2], acc, place)


def fold_kernel(keep, got, send, own):
    high = lax.axis_index("freq") // 2
    send[...] = keep[1 - high] + got[1 - high]
    own[...] = keep[high] + got[high]


def precond_kernel(pick, *refs):
    chunks, (precond, outgoing) = refs[:-2], refs[-2:]
    layers = precond.shape[0]
    wide = [chunk for chunk in chunks if len(chunk.shape) == 6]
    terms = [
        [functools.partial(lambda chunk, other, at: chunk[other, 0, at[0], at[1]], chunk, other)
         for other in range(chunk.shape[0])]
        for chunk in wide
    ]
    flat = chunks[len(wide) :]
    for place in range(0, len(flat), 2):
        terms.append([lambda at, ref=ref: ref[at[0], at[1]] for ref in flat[place : place + 2]])
    for step, parts in enumerate(terms):
        for side in range(2):
            layer = layers // 2 - 1 - step if side == 0 else layers // 2 + step
            grad, illum = [
                functools.reduce(lambda a, b: a + b, [part((number, side)) for part in parts])
                for number in range(2)
            ]
            precond[layer] = grad / jnp.sqrt(illum + 1.0)

    @pl.loop(0, outgoing.shape[0])
    def _(slot):
        outgoing[slot] = precond[pick[slot]]


def deliver_kernel(slots, incoming, out):
    @pl.loop(0, out.shape[2])
    def _(number):
        out[0, 0, number] = incoming[slots[number]]


def smem():
    return pl.BlockSpec(memory_space=pltpu.SMEM)


def vmem():
    return pl.BlockSpec(memory_space=pltpu.VMEM)


def plane_scratch(*lead, rows):
    return pltpu.VMEM(lead + (2, rows, HALF), jnp.float32)


def compiler_params(mebibytes):
    return pltpu.CompilerParams(vmem_limit_bytes=mebibytes * 1024 * 1024)


def light(size=1000):
    return pl.CostEstimate(flops=1000, bytes_accessed=size, transcendentals=0)


def in_hbm(array):
    return pltpu.with_memory_space_constraint(array, pltpu.HBM)


def hbm(*shape):
    return pltpu.HBM(shape, jnp.float32)


def state(groups, rows):
    return (
        hbm(groups, 2, 2, 2, 2, rows, HALF),
        pl.BlockSpec((1, 2, 2, 2, 2, rows, HALF), lambda g: (g, 0, 0, 0, 0, 0, 0)),
    )


def sent(groups, rows):
    return (
        hbm(2, groups, 4, 2, rows, HALF),
        pl.BlockSpec((2, 1, 4, 2, rows, HALF), lambda g: (0, g, 0, 0, 0, 0)),
    )


def factor_state(groups, rows):
    return (
        hbm(groups, 2, 3, 2, 2, rows, HALF),
        pl.BlockSpec((1, 2, 3, 2, 2, rows, HALF), lambda g: (g, 0, 0, 0, 0, 0, 0)),
    )


def sums(bands, rows, columns, steps=1):
    shape = (bands, steps, 2, 2, rows // bands, columns)
    return hbm(*shape), pl.BlockSpec(shape, lambda g: (0,) * 6)


def halves(bands, rows, columns):
    shape = (bands // 2, 2, 2, rows // bands, columns)
    return hbm(*shape), pl.BlockSpec(shape, lambda g: (0,) * 5)


def fold(keep, got):
    shape = hbm(*keep.shape[1:])
    return pl.pallas_call(
        fold_kernel,
        in_specs=[vmem()] * 2,
        out_specs=[vmem()] * 2,
        out_shape=[shape] * 2,
        compiler_params=compiler_params(8),
        cost_estimate=light(),
        name="fold",
    )(keep, got)


def split(pairs):
    return dict(out_shape=[p[0] for p in pairs], out_specs=[p[1] for p in pairs])


def layer_specs(sources, own):
    rows = sources.shape[3]
    return (
        [pl.BlockSpec((1, 4, 1, rows, HALF), lambda g, h=h: (g, 0, own, 0, h)) for h in range(2)],
        [pl.BlockSpec((1, rows, HALF), lambda g, h=h: (own, 0, h)) for h in range(2)],
    )


def first_edges(freq, sources, slowness):
    groups, _, _, rows, _ = sources.shape
    anywhere = pl.BlockSpec(memory_space=pl.ANY)
    return pl.pallas_call(
        first_kernel,
        in_specs=[smem(), anywhere, anywhere],
        out_specs=[vmem()] * 2,
        out_shape=[hbm(4 * groups + 1, 2, rows, HALF)] * 2,
        scratch_shapes=[
            pltpu.VMEM((2, 2, groups, 4, rows, HALF), jnp.float32),
            plane_scratch(2, rows=rows),
            plane_scratch(2, groups, 2, rows=rows),
            pltpu.SemaphoreType.DMA((2, 2, 2)),
        ],
        compiler_params=compiler_params(8),
        cost_estimate=light(),
        name="first",
    )(freq, in_hbm(sources), in_hbm(slowness))


def edge_layers(sources, slowness):
    layers = sources.shape[2]
    sources, slowness = in_hbm(sources), in_hbm(slowness)
    operands, specs = [], []
    for side in range(2):
        parts = [layer_specs(sources, at if side == 0 else layers - 1 - at) for at in range(3)]
        for what, array in enumerate((sources, slowness)):
            for part in parts:
                operands += [array] * 2
                specs += part[what]
    return operands, specs


def later_edges(freq, sources, slowness, first):
    groups, _, _, rows, _ = sources.shape
    operands, specs = edge_layers(sources, slowness)
    operands = [freq, in_hbm(first)] + operands
    specs = [smem(), pl.BlockSpec(memory_space=pl.ANY)] + specs
    return pl.pallas_call(
        edge_kernel,
        grid=(groups,),
        in_specs=specs,
        **split([sent(groups, rows)] * 2 + [state(groups, rows)]),
        scratch_shapes=[
            plane_scratch(2, 3, 2, rows=rows),
            plane_scratch(2, 2, 3, 2, rows=rows),
            plane_scratch(2, 2, 2, 2, rows=rows),
        ],
        compiler_params=compiler_params(32),
        cost_estimate=light(),
        name="edges",
    )(*operands)


def inner(freq, sources, slowness, second, bands):
    groups, _, layers, rows, columns = sources.shape
    half = [
        pl.BlockSpec((1, 4, layers, rows, HALF), lambda g, h=h: (g, 0, 0, 0, h)) for h in range(2)
    ]
    slow = [pl.BlockSpec((layers, rows, HALF), lambda g, h=h: (0, 0, h)) for h in range(2)]
    sources, slowness = in_hbm(sources), in_hbm(slowness)
    return pl.pallas_call(
        inner_kernel,
        grid=(groups,),
        in_specs=[smem()] + half + slow + [state(groups, rows)[1]],
        **split([sums(bands, rows, columns)] + [state(groups, rows)] * 3),
        scratch_shapes=[
            plane_scratch(layers, 2, rows=rows),
            plane_scratch(2, layers, 2, rows=rows),
            plane_scratch(2, layers, 2, rows=rows),
            plane_scratch(2, layers, 2, rows=rows),
            plane_scratch(2, layers - 4, 2, rows=rows),
            plane_scratch(2, 2, 2, rows=rows),
            plane_scratch(1, 2, 2, rows=rows),
        ],
        compiler_params=compiler_params(40),
        cost_estimate=light(),
        name="inner",
    )(freq, sources, sources, slowness, slowness, in_hbm(second))


def middle(freq, sources, slowness, from_core, from_chip, held, bands):
    groups, _, _, rows, columns = sources.shape
    operands, specs = edge_layers(sources, slowness)
    near = [
        pl.BlockSpec((4, 2, rows, HALF), lambda g: (g, 0, 0, 0)),
        pl.BlockSpec((1, 2, rows, HALF), lambda g: (4 * groups, 0, 0, 0)),
    ]
    return pl.pallas_call(
        middle_kernel,
        grid=(groups,),
        in_specs=[smem()] + specs + near * 2 + [state(groups, rows)[1]] * 4,
        **split(
            [sums(bands, rows, columns)] + [state(groups, rows)] * 3 + [factor_state(groups, rows)]
        ),
        scratch_shapes=[
            plane_scratch(2, 2, 3, 2, rows=rows),
            plane_scratch(2, 2, rows=rows),
            plane_scratch(2, 2, 2, 2, rows=rows),
            plane_scratch(2, 2, 2, rows=rows),
            plane_scratch(2, 2, 2, rows=rows),
            plane_scratch(2, 4, rows=rows),
            plane_scratch(2, rows=rows),
            plane_scratch(2, 2, 2, 2, rows=rows),
            plane_scratch(2, 2, 2, rows=rows),
            plane_scratch(1, 2, 2, rows=rows),
        ],
        compiler_params=compiler_params(40),
        cost_estimate=light(100_000_000),
        name="middle",
    )(
        freq, *operands, from_core, from_core, from_chip, from_chip,
        *[in_hbm(array) for array in held],
    )


def outer(freq, from_core, from_chip, held, bands, rows, columns):
    groups = from_core.shape[1]
    return pl.pallas_call(
        outer_kernel,
        grid=(groups,),
        in_specs=[smem()] + [sent(groups, rows)[1]] * 2 + [state(groups, rows)[1]] * 3
        + [factor_state(groups, rows)[1]],
        **split([halves(bands, rows, columns)] * 4),
        scratch_shapes=[
            plane_scratch(2, 2, 4, rows=rows),
            plane_scratch(2, 2, 2, rows=rows),
            plane_scratch(2, 2, 2, 2, rows=rows),
            plane_scratch(2, 2, 2, rows=rows),
        ],
        compiler_params=compiler_params(32),
        cost_estimate=light(),
        name="outer",
    )(freq, from_core, from_chip, *[in_hbm(array) for array in held])


def route(coverage, own_index):
    lists = coverage[0]
    owner, local = lists // TPD, lists % TPD
    position = jnp.arange(lists.shape[1], dtype=jnp.int32)
    same_owner = owner[:, :, None] == owner[:, None, :]
    earlier = position[None, :] < position[:, None]
    rank = jnp.sum((same_owner & earlier[None]).astype(jnp.int32), axis=2)
    slots = jnp.arange(CAP, dtype=jnp.int32)
    hit = (owner == own_index)[:, :, None] & (rank[:, :, None] == slots[None, None, :])
    pick = jnp.sum(jnp.where(hit, local[:, :, None], 0), axis=1).reshape(-1)
    own_slots = owner * CAP + rank
    return pick, lax.dynamic_index_in_dim(own_slots, own_index, 0, keepdims=False)


def body(sources, slowness, freq_index, coverage):
    groups, _, layers, rows, columns = sources.shape
    bands, members = lax.axis_size("freq"), lax.axis_size("sub")
    own_index = lax.axis_index("sub")
    cores = [(i, i ^ 1) for i in range(members)]
    chips = [(i, i + step) for i in range(members) for step in (2 * (i % 2) - 1,) if 0 <= i + step < members]
    def exchange(to_chip, to_core):
        return lax.ppermute(to_chip, "sub", chips), lax.ppermute(to_core, "sub", cores)

    near = first_edges(freq_index, sources, slowness)
    near_chip, near_core = exchange(*near)
    *edges, second = later_edges(freq_index, sources, slowness, near[0])
    far_chip, far_core = exchange(*edges)
    pick, slots = route(coverage, own_index)

    def spread(chunk):
        return lax.all_to_all(chunk, "freq", split_axis=0, concat_axis=0, tiled=True)

    def spread_next(chunk):
        if chunks:
            chunks[-1], chunk = lax.optimization_barrier((chunks[-1], chunk))
        chunks.append(spread(chunk))

    chunks = []
    chunk, *held = inner(freq_index, sources, slowness, second, bands)
    chunk, near_chip, near_core = lax.optimization_barrier((chunk, near_chip, near_core))
    spread_next(chunk)
    held = [second] + held
    chunk, *held = middle(freq_index, sources, slowness, near_core, near_chip, held, bands)
    spread_next(chunk)
    ends = outer(freq_index, far_core, far_chip, held, bands, rows, columns)
    neighbours = [(i, i ^ 1) for i in range(bands)]
    opposites = [(i, i ^ 2) for i in range(bands)]
    got = [lax.ppermute(send, "freq", neighbours) for send in ends[1::2]]
    chunks[-1], got[0] = lax.optimization_barrier((chunks[-1], got[0]))
    for keep, part in zip(ends[::2], got):
        send, own = fold(keep, part)
        chunks += [own, lax.ppermute(send, "freq", opposites)]
    depth = rows // bands
    precond, outgoing = pl.pallas_call(
        precond_kernel,
        in_specs=[smem()] + [vmem()] * len(chunks),
        out_specs=[vmem()] * 2,
        out_shape=[
            jax.ShapeDtypeStruct((layers, depth, columns), jnp.float32),
            jax.ShapeDtypeStruct((members * CAP, depth, columns), jnp.float32),
        ],
        compiler_params=compiler_params(12),
        name="precond",
    )(pick, *chunks)
    incoming = lax.all_to_all(outgoing, "sub", split_axis=0, concat_axis=0, tiled=True)
    delivered = pl.pallas_call(
        deliver_kernel,
        in_specs=[smem(), vmem()],
        out_specs=vmem(),
        out_shape=jax.ShapeDtypeStruct((1, 1, coverage.shape[2], depth, columns), jnp.float32),
        compiler_params=compiler_params(12),
        name="deliver",
    )(slots, incoming)
    return precond, delivered


def solution(mesh):
    placed = (
        P("freq", None, "sub", None, None),
        P("sub", None, None),
        P("freq"),
        P("freq", None, None),
    )
    return jax.shard_map(
        body,
        mesh=mesh,
        in_specs=placed,
        out_specs=(P("sub", "freq", None), P("freq", "sub", None, None, None)),
        check_vma=False,
    )
```

```python
import functools

import jax
import jax.numpy as jnp
from jax import lax
from jax.experimental import pallas as pl
from jax.experimental.pallas import tpu as pltpu
from jax.sharding import PartitionSpec as P

TPD = 8
CAP = 2
HALF = 128


def masks():
    lane = lax.broadcasted_iota(jnp.int32, (8, HALF), 1)
    row = lax.broadcasted_iota(jnp.int32, (8, HALF), 0)
    return lane == 0, lane == HALF - 1, row == 0, row == 7


def turn(real, imag, coef_real, coef_imag):
    return real * coef_real + imag * coef_imag, imag * coef_real - real * coef_imag


def coefficients(store, slow, scale, factor, nk):
    for k in range(nk):
        for h in range(2):
            sigma = scale * slow(h, k)
            diag = 0.875 - sigma
            inverse = factor / (diag * diag + sigma * sigma)
            store(0, h, k, diag * inverse)
            store(1, h, k, sigma * inverse)


def relax(store, force, near, coef, marks, nk, base=None):
    lane_first, lane_last, row_first, row_last = marks

    def across(c, h, k):
        before, middle, after = [None if layer is None else layer(c, h, k) for layer in near]
        parts = [part for part in (before, after) if part is not None]
        if middle is not None:
            parts.append(middle + middle)
        return functools.reduce(lambda total, part: total + part, parts)

    both = [(c, h) for c in range(2) for h in range(2)]
    top = {at: across(*at, 0) for at in both}
    bottom = {at: across(*at, nk - 1) for at in both}
    here = top
    pair = {at: jnp.where(row_first, 0.0, pltpu.roll(bottom[at], 1, 0)) + top[at] for at in both}
    for k in range(nk):
        if k < nk - 2:
            following = {at: across(*at, k + 1) for at in both}
        elif k == nk - 2:
            following = bottom
        else:
            following = {at: jnp.where(row_last, 0.0, pltpu.roll(top[at], 7, 0)) for at in both}
        terms = []
        for c in range(2):
            depth = []
            for h in range(2):
                later = here[c, h] + following[c, h]
                depth.append(pair[c, h] + later)
                pair[c, h] = later
            left, right = depth
            left_up, right_up = pltpu.roll(left, HALF - 1, 1), pltpu.roll(right, HALF - 1, 1)
            left_down, right_down = pltpu.roll(left, 1, 1), pltpu.roll(right, 1, 1)
            left_sides = jnp.where(lane_last, right_up, left_up) + jnp.where(lane_first, 0.0, left_down)
            right_sides = jnp.where(lane_last, 0.0, right_up) + jnp.where(
                lane_first, left_down, right_down
            )
            for h, (middle, ends) in enumerate(((left, left_sides), (right, right_sides))):
                total = ends + (middle + middle)
                if near[1] is not None:
                    total = total - 8.0 * near[1](c, h, k)
                terms.append(total if force is None else force(c, h, k) + total)
        here = following
        for h in range(2):
            planes = turn(terms[h], terms[2 + h], coef(0, h, k), coef(1, h, k))
            for c in range(2):
                store(c, h, k, planes[c] if base is None else base(c, h, k) + planes[c])


def piece_of(ref, lead):
    return lambda c, h, k: ref[lead + (c, h, pl.ds(8 * k, 8), slice(None))]


def row_piece(refs, lead, offset, tail, nk):
    return lambda c, h, k: refs[h][
        lead + (offset + c,) + tail + (pl.ds(k, 8, stride=nk), slice(None))
    ]


def store_to(*places):
    def store(c, h, k, piece):
        for ref, lead in places:
            ref[lead + (c, h, pl.ds(8 * k, 8), slice(None))] = piece

    return store


def start_layer(store, force, coef, nk):
    for k in range(nk):
        for h in range(2):
            planes = turn(force(0, h, k), force(1, h, k), coef(0, h, k), coef(1, h, k))
            for c in range(2):
                store(c, h, k, planes[c])


def products(last, acc, place, weight, first, nk):
    for side in range(2):
        forward, adjoint = [piece_of(last, (side, pair)) for pair in range(2)]
        for h in range(2):
            for k in range(nk):
                fr, fi = forward(0, h, k), forward(1, h, k)
                ar, ai = adjoint(0, h, k), adjoint(1, h, k)
                terms = (weight * (fr * ar - fi * ai), weight * (fr * fr + fi * fi))
                for number, term in enumerate(terms):
                    at = (place, number, side, h, pl.ds(k, 8, stride=nk), slice(None))
                    acc[at] = jnp.where(first, term, acc[at] + term)


def write_out(out, acc, offset):
    bands, _, _, _, depth, _ = out.shape
    for band in range(bands):
        for place in range(acc.shape[0]):
            for number in range(2):
                for side in range(2):
                    for h in range(2):
                        out[band, offset + place, number, side, :, pl.ds(h * HALF, HALF)] = acc[
                            place, number, side, h, pl.ds(band * depth, depth), :
                        ]


def scale_of(freq, group):
    weight = 1.0 + freq[group].astype(jnp.float32) / 16.0
    return weight, 0.12 * weight


def parity():
    return lax.axis_index("sub") % 2


def paired(side):
    index = lax.axis_index("sub")
    there = index > 0 if side == 0 else index < lax.axis_size("sub") - 1
    return jnp.where(there, 1.0 / 64.0, 0.0)


def first_kernel(indices, sources, slowness, to_chip, to_core, raw, slow, coef, freq, sems, sem):
    groups, _, layers, rows = sources.shape[:4]
    nk = rows // 8
    places = (parity() * (layers - 1), (1 - parity()) * (layers - 1))
    copies = []
    for side, own in enumerate(places):
        for h in range(2):
            lanes = pl.ds(h * HALF, HALF)
            pairs = ((slowness.at[own, :, lanes], slow), (sources.at[:, :, own, :, lanes], raw))
            for number, (ref, held) in enumerate(pairs):
                copies.append(
                    pltpu.make_async_copy(ref, held.at[side, h], sems.at[side, h, number])
                )
    load = pltpu.make_async_copy(indices, freq, sem)
    load.start()
    for copy in copies:
        copy.start()
    load.wait()
    for side, out in enumerate((to_chip, to_core)):
        for copy in copies[4 * side : 4 * side + 4]:
            copy.wait()

        def sigma(h, k):
            return slow[side, h, pl.ds(k, 8, stride=nk), :]

        for h in range(2):
            for k in range(nk):
                out[4 * groups, h, pl.ds(8 * k, 8), :] = sigma(h, k)
        for group in range(groups):
            scale = scale_of(freq, group)[1]
            coefficients(store_to((coef, (side, group))), sigma, scale, 1.0 / 64.0, nk)
            for pair in range(2):
                start_layer(
                    store_from(out, (), 4 * group + 2 * pair),
                    row_piece((raw.at[side, 0], raw.at[side, 1]), (group,), 2 * pair, (), nk),
                    piece_of(coef, (side, group)),
                    nk,
                )


def store_from(ref, lead, offset):
    def store(c, h, k, piece):
        ref[lead + (offset + c, h, pl.ds(8 * k, 8), slice(None))] = piece

    return store


def sent_piece(ref, lead, offset):
    return lambda c, h, k: ref[lead + (offset + c, h, pl.ds(8 * k, 8), slice(None))]


def edge_kernel(freq, _, *refs):
    sides = []
    for side in range(2):
        part = refs[12 * side : 12 * side + 12]
        sides.append([[part[at + 2 * n : at + 2 * n + 2] for n in range(3)] for at in (0, 6)])
    far_chip, far_core, second, coef, one, fields = refs[24:]
    group = pl.program_id(0)
    rows = sides[0][1][0][0].shape[-2]
    nk = rows // 8
    marks = masks()
    scale = scale_of(freq, group)[1]
    chains = [(side, pair) for side in range(2) for pair in range(2)]

    def force(side, pair, at):
        return row_piece(sides[side][0][at], (0,), 2 * pair, (0,), nk)

    for side in range(2):
        for at in range(3):
            slows = sides[side][1][at]
            coefficients(
                store_to((coef, (side, at))),
                lambda h, k, slows=slows: slows[h][0, pl.ds(k, 8, stride=nk), :],
                scale,
                1.0 / 64.0,
                nk,
            )
            for pair in range(2):
                start_layer(
                    store_to((one, (side, pair, at))),
                    force(side, pair, at),
                    piece_of(coef, (side, at)),
                    nk,
                )
    for at in range(2):
        for side, pair in chains:
            near = [piece_of(one, (side, pair, n)) if n >= 0 else None for n in (at - 1, at, at + 1)]
            target = (fields, (side, 0, pair)) if at == 0 else (second, (0, pair, side))
            relax(
                store_to(target), force(side, pair, at), near, piece_of(coef, (side, at)), marks, nk
            )
    for side, pair in chains:
        near = [None, piece_of(fields, (side, 0, pair)), piece_of(second, (0, pair, side))]
        relax(
            store_to((fields, (side, 1, pair))),
            force(side, pair, 0),
            near,
            piece_of(coef, (side, 0)),
            marks,
            nk,
        )
    for out, side in ((far_chip, parity()), (far_core, 1 - parity())):
        for level in range(2):
            for pair in range(2):
                for c in range(2):
                    out[level, 0, 2 * pair + c] = fields[side, level, pair, c]


def inner_kernel(
    freq, src_l, src_r, slow_l, slow_r, second,
    out, two_next, three_near, three_far, coef, one, force, two, three, last, acc,
):
    group = pl.program_id(0)
    groups = pl.num_programs(0)
    layers, rows = src_l.shape[2], src_l.shape[3]
    nk = rows // 8
    marks = masks()
    weight, scale = scale_of(freq, group)
    weight = weight * 4096.0
    sources, slows = (src_l, src_r), (slow_l, slow_r)
    chains = [(side, pair) for side in range(2) for pair in range(2)]

    @pl.loop(0, layers - 2)
    def _(place):
        layer = place + 1
        coefficients(
            store_to((coef, (layer,))),
            lambda h, k: slows[h][layer, pl.ds(k, 8, stride=nk), :],
            scale,
            1.0 / 64.0,
            nk,
        )
        for pair in range(2):
            rows_of = row_piece(sources, (0,), 2 * pair, (layer,), nk)
            keep = store_to((force, (pair, layer)))
            for c in range(2):
                for h in range(2):
                    for k in range(nk):
                        keep(c, h, k, rows_of(c, h, k))
            start_layer(store_to((one, (pair, layer))), rows_of, piece_of(coef, (layer,)), nk)

    def copy_plane(keep, given):
        for c in range(2):
            for h in range(2):
                for k in range(nk):
                    keep(c, h, k, given(c, h, k))

    def layer_at(side, at):
        return at if side == 0 else layers - 1 - at

    def step(target, pair, layer, ref, skip):
        near = [piece_of(ref, (pair, layer + shift - skip)) for shift in (-1, 0, 1)]
        relax(
            store_to(target),
            piece_of(force, (pair, layer)),
            near,
            piece_of(coef, (layer,)),
            marks,
            nk,
        )

    for side, pair in chains:
        copy_plane(
            store_to((two, (pair, layer_at(side, 1)))), piece_of(second, (0, pair, side))
        )

    @pl.loop(0, (layers - 4) // 2)
    def _(turn_at):
        for offset in range(2):
            for pair in range(2):
                layer = 2 + 2 * turn_at + offset
                step((two, (pair, layer)), pair, layer, one, 0)

    @pl.loop(0, (layers - 4) // 2)
    def _(turn_at):
        for offset in range(2):
            for pair in range(2):
                layer = 2 + 2 * turn_at + offset
                step((three, (pair, layer - 2)), pair, layer, two, 0)

    for side, pair in chains:
        step((last, (side, pair)), pair, layers // 2 - 1 + side, three, 2)
        for keep, ref, at in (
            (two_next, two, layer_at(side, 2)),
            (three_near, three, layer_at(side, 2) - 2),
            (three_far, three, layer_at(side, 3) - 2),
        ):
            copy_plane(store_to((keep, (0, pair, side))), piece_of(ref, (pair, at)))
    products(last, acc, 0, weight, group == 0, nk)

    @pl.when(group == groups - 1)
    def _():
        write_out(out, acc, 0)


def middle_kernel(freq, *refs):
    sides = []
    for side in range(2):
        part = refs[12 * side : 12 * side + 12]
        sides.append([[part[at + 2 * n : at + 2 * n + 2] for n in range(3)] for at in (0, 6)])
    core_field, core_slow, chip_field, chip_slow, second, two_next, three_near, three_far = refs[24:32]
    out, base_three, base_next, base_four, factors = refs[32:37]
    force, beyond, one, first_two, first_three, halo, halo_slow, change, last, acc = refs[37:]
    group = pl.program_id(0)
    groups = pl.num_programs(0)
    rows = second.shape[-2]
    nk = rows // 8
    marks = masks()
    weight, scale = scale_of(freq, group)
    weight = weight * 4096.0
    chains = [(side, pair) for side in range(2) for pair in range(2)]
    to_chip, to_core = parity(), 1 - parity()
    halo[to_core] = core_field[...]
    halo[to_chip] = chip_field[...]
    halo_slow[to_core] = core_slow[0]
    halo_slow[to_chip] = chip_slow[0]

    for side in range(2):
        coefficients(
            store_to((beyond, (side,))),
            lambda h, k, side=side: halo_slow[side, h, pl.ds(8 * k, 8), :],
            scale,
            paired(side),
            nk,
        )
        for at in range(3):
            slows = sides[side][1][at]
            coefficients(
                store_to((factors, (0, side, at))),
                lambda h, k, slows=slows: slows[h][0, pl.ds(k, 8, stride=nk), :],
                scale,
                1.0 / 64.0,
                nk,
            )
            for pair in range(2):
                rows_of = row_piece(sides[side][0][at], (0,), 2 * pair, (0,), nk)
                keep = store_to((force, (side, pair, at)))
                for c in range(2):
                    for h in range(2):
                        for k in range(nk):
                            keep(c, h, k, rows_of(c, h, k))
                if at < 2:
                    start_layer(
                        store_to((one, (side, pair, at))),
                        rows_of,
                        piece_of(factors, (0, side, at)),
                        nk,
                    )

    def step(target, side, pair, at, near):
        relax(
            store_to(target),
            piece_of(force, (side, pair, at)),
            near,
            piece_of(factors, (0, side, at)),
            marks,
            nk,
        )

    def held(ref, side, pair):
        return piece_of(ref, (0, pair, side))

    for side, pair in chains:
        near = [sent_piece(halo, (side,), 2 * pair)]
        near += [piece_of(one, (side, pair, at)) for at in range(2)]
        step((first_two, (side, pair)), side, pair, 0, near)
    for side, pair in chains:
        near = [None, None, piece_of(one, (side, pair, 0))]
        relax(store_to((change, (0, side, pair))), None, near, piece_of(beyond, (side,)), marks, nk)
    for side, pair in chains:
        near = [
            piece_of(first_two, (side, pair)),
            held(second, side, pair),
            held(two_next, side, pair),
        ]
        step((first_three, (side, pair)), side, pair, 1, near)
    for side, pair in chains:
        near = [
            None,
            piece_of(change, (0, side, pair)),
            piece_of(first_two, (side, pair)),
        ]
        relax(store_to((change, (1, side, pair))), None, near, piece_of(beyond, (side,)), marks, nk)
    for side, pair in chains:
        three = piece_of(first_three, (side, pair))
        near = [three, held(three_near, side, pair), held(three_far, side, pair)]
        step((last, (side, pair)), side, pair, 2, near)
    products(last, acc, 0, weight, group == 0, nk)
    for side, pair in chains:
        three = piece_of(first_three, (side, pair))
        twos = [piece_of(first_two, (side, pair)), held(second, side, pair)]
        changes = [piece_of(change, (number, side, pair)) for number in range(2)]
        for target, at, near in (
            (base_three, 0, [changes[0], *twos]),
            (base_next, 1, [None, three, held(three_near, side, pair)]),
            (base_four, 0, [changes[1], None, three]),
        ):
            step((target, (0, pair, side)), side, pair, at, near)

    @pl.when(group == groups - 1)
    def _():
        write_out(out, acc, 0)


def write_halves(keep, send, acc, place):
    depth = keep.shape[-2]
    odd = lax.axis_index("freq") % 2
    for out, parity_of in ((keep, odd), (send, 1 - odd)):
        for high in range(2):
            start = pl.multiple_of((2 * high + parity_of) * depth, 8)
            for number in range(2):
                for side in range(2):
                    for h in range(2):
                        out[high, number, side, :, pl.ds(h * HALF, HALF)] = acc[
                            place, number, side, h, pl.ds(start, depth), :
                        ]


def outer_kernel(freq, core, chip, base_three, base_next, base_four, factors, *rest):
    outs, (sent_fields, fresh, last, acc) = rest[:4], rest[4:]
    group = pl.program_id(0)
    groups = pl.num_programs(0)
    rows = base_three.shape[-2]
    nk = rows // 8
    marks = masks()
    weight = scale_of(freq, group)[0] * 4096.0
    chains = [(side, pair) for side in range(2) for pair in range(2)]
    to_chip, to_core = parity(), 1 - parity()
    for number in range(2):
        sent_fields[to_core, number] = core[number, 0]
        sent_fields[to_chip, number] = chip[number, 0]

    def step(target, base, side, pair, at, near):
        relax(
            store_to(target),
            None,
            near,
            piece_of(factors, (0, side, at)),
            marks,
            nk,
            base=piece_of(base, (0, pair, side)),
        )

    for side, pair in chains:
        near = [sent_piece(sent_fields, (side, 0), 2 * pair), None, None]
        step((fresh, (side, pair)), base_three, side, pair, 0, near)
    for side, pair in chains:
        near = [piece_of(fresh, (side, pair)), None, None]
        step((last, (0, side, pair)), base_next, side, pair, 1, near)
    for side, pair in chains:
        near = [sent_piece(sent_fields, (side, 1), 2 * pair), piece_of(fresh, (side, pair)), None]
        step((last, (1, side, pair)), base_four, side, pair, 0, near)
    for place in range(2):
        products(last.at[place], acc, place, weight, group == 0, nk)

    @pl.when(group == groups - 1)
    def _():
        for place in range(2):
            write_halves(*outs[2 * place : 2 * place + 2], acc, place)


def fold_kernel(keep, got, send, own):
    high = lax.axis_index("freq") // 2
    send[...] = keep[1 - high] + got[1 - high]
    own[...] = keep[high] + got[high]


def precond_kernel(pick, *refs):
    chunks, (precond, outgoing) = refs[:-2], refs[-2:]
    layers = precond.shape[0]
    wide = [chunk for chunk in chunks if len(chunk.shape) == 6]
    terms = [
        [functools.partial(lambda chunk, other, at: chunk[other, 0, at[0], at[1]], chunk, other)
         for other in range(chunk.shape[0])]
        for chunk in wide
    ]
    flat = chunks[len(wide) :]
    for place in range(0, len(flat), 2):
        terms.append([lambda at, ref=ref: ref[at[0], at[1]] for ref in flat[place : place + 2]])
    for step, parts in enumerate(terms):
        for side in range(2):
            layer = layers // 2 - 1 - step if side == 0 else layers // 2 + step
            grad, illum = [
                functools.reduce(lambda a, b: a + b, [part((number, side)) for part in parts])
                for number in range(2)
            ]
            precond[layer] = grad / jnp.sqrt(illum + 1.0)

    @pl.loop(0, outgoing.shape[0])
    def _(slot):
        outgoing[slot] = precond[pick[slot]]


def deliver_kernel(slots, incoming, out):
    @pl.loop(0, out.shape[2])
    def _(number):
        out[0, 0, number] = incoming[slots[number]]


def smem():
    return pl.BlockSpec(memory_space=pltpu.SMEM)


def vmem():
    return pl.BlockSpec(memory_space=pltpu.VMEM)


def plane_scratch(*lead, rows):
    return pltpu.VMEM(lead + (2, rows, HALF), jnp.float32)


def compiler_params(mebibytes):
    return pltpu.CompilerParams(vmem_limit_bytes=mebibytes * 1024 * 1024)


def light(size=1000):
    return pl.CostEstimate(flops=1000, bytes_accessed=size, transcendentals=0)


def in_hbm(array):
    return pltpu.with_memory_space_constraint(array, pltpu.HBM)


def hbm(*shape):
    return pltpu.HBM(shape, jnp.float32)


def state(groups, rows):
    return (
        hbm(groups, 2, 2, 2, 2, rows, HALF),
        pl.BlockSpec((1, 2, 2, 2, 2, rows, HALF), lambda g: (g, 0, 0, 0, 0, 0, 0)),
    )


def sent(groups, rows):
    return (
        hbm(2, groups, 4, 2, rows, HALF),
        pl.BlockSpec((2, 1, 4, 2, rows, HALF), lambda g: (0, g, 0, 0, 0, 0)),
    )


def factor_state(groups, rows):
    return (
        hbm(groups, 2, 3, 2, 2, rows, HALF),
        pl.BlockSpec((1, 2, 3, 2, 2, rows, HALF), lambda g: (g, 0, 0, 0, 0, 0, 0)),
    )


def sums(bands, rows, columns, steps=1):
    shape = (bands, steps, 2, 2, rows // bands, columns)
    return hbm(*shape), pl.BlockSpec(shape, lambda g: (0,) * 6)


def halves(bands, rows, columns):
    shape = (bands // 2, 2, 2, rows // bands, columns)
    spec = pl.BlockSpec(shape, lambda g: (0,) * 5)
    return [(jax.ShapeDtypeStruct(shape, jnp.float32), spec), (hbm(*shape), spec)]


def fold(keep, got):
    shape = keep.shape[1:]
    return pl.pallas_call(
        fold_kernel,
        in_specs=[vmem()] * 2,
        out_specs=[vmem()] * 2,
        out_shape=[hbm(*shape), jax.ShapeDtypeStruct(shape, jnp.float32)],
        compiler_params=compiler_params(8),
        cost_estimate=light(),
        name="fold",
    )(keep, got)


def split(pairs):
    return dict(out_shape=[p[0] for p in pairs], out_specs=[p[1] for p in pairs])


def layer_specs(sources, own):
    rows = sources.shape[3]
    return (
        [pl.BlockSpec((1, 4, 1, rows, HALF), lambda g, h=h: (g, 0, own, 0, h)) for h in range(2)],
        [pl.BlockSpec((1, rows, HALF), lambda g, h=h: (own, 0, h)) for h in range(2)],
    )


def first_edges(freq, sources, slowness):
    groups, _, _, rows, _ = sources.shape
    anywhere = pl.BlockSpec(memory_space=pl.ANY)
    return pl.pallas_call(
        first_kernel,
        in_specs=[anywhere] * 3,
        out_specs=[vmem()] * 2,
        out_shape=[hbm(4 * groups + 1, 2, rows, HALF)] * 2,
        scratch_shapes=[
            pltpu.VMEM((2, 2, groups, 4, rows, HALF), jnp.float32),
            plane_scratch(2, rows=rows),
            plane_scratch(2, groups, 2, rows=rows),
            pltpu.SMEM((groups,), jnp.int32),
            pltpu.SemaphoreType.DMA((2, 2, 2)),
            pltpu.SemaphoreType.DMA,
        ],
        compiler_params=compiler_params(8),
        cost_estimate=light(),
        name="first",
    )(in_hbm(freq), in_hbm(sources), in_hbm(slowness))


def edge_layers(sources, slowness):
    layers = sources.shape[2]
    sources, slowness = in_hbm(sources), in_hbm(slowness)
    operands, specs = [], []
    for side in range(2):
        parts = [layer_specs(sources, at if side == 0 else layers - 1 - at) for at in range(3)]
        for what, array in enumerate((sources, slowness)):
            for part in parts:
                operands += [array] * 2
                specs += part[what]
    return operands, specs


def later_edges(freq, sources, slowness, first):
    groups, _, _, rows, _ = sources.shape
    operands, specs = edge_layers(sources, slowness)
    operands = [freq, in_hbm(first)] + operands
    specs = [smem(), pl.BlockSpec(memory_space=pl.ANY)] + specs
    return pl.pallas_call(
        edge_kernel,
        grid=(groups,),
        in_specs=specs,
        **split([sent(groups, rows)] * 2 + [state(groups, rows)]),
        scratch_shapes=[
            plane_scratch(2, 3, 2, rows=rows),
            plane_scratch(2, 2, 3, 2, rows=rows),
            plane_scratch(2, 2, 2, 2, rows=rows),
        ],
        compiler_params=compiler_params(32),
        cost_estimate=light(),
        name="edges",
    )(*operands)


def inner(freq, sources, slowness, second, bands):
    groups, _, layers, rows, columns = sources.shape
    half = [
        pl.BlockSpec((1, 4, layers, rows, HALF), lambda g, h=h: (g, 0, 0, 0, h)) for h in range(2)
    ]
    slow = [pl.BlockSpec((layers, rows, HALF), lambda g, h=h: (0, 0, h)) for h in range(2)]
    sources, slowness = in_hbm(sources), in_hbm(slowness)
    return pl.pallas_call(
        inner_kernel,
        grid=(groups,),
        in_specs=[smem()] + half + slow + [state(groups, rows)[1]],
        **split([sums(bands, rows, columns)] + [state(groups, rows)] * 3),
        scratch_shapes=[
            plane_scratch(layers, 2, rows=rows),
            plane_scratch(2, layers, 2, rows=rows),
            plane_scratch(2, layers, 2, rows=rows),
            plane_scratch(2, layers, 2, rows=rows),
            plane_scratch(2, layers - 4, 2, rows=rows),
            plane_scratch(2, 2, 2, rows=rows),
            plane_scratch(1, 2, 2, rows=rows),
        ],
        compiler_params=compiler_params(40),
        cost_estimate=light(),
        name="inner",
    )(freq, sources, sources, slowness, slowness, in_hbm(second))


def middle(freq, sources, slowness, from_core, from_chip, held, bands):
    groups, _, _, rows, columns = sources.shape
    operands, specs = edge_layers(sources, slowness)
    near = [
        pl.BlockSpec((4, 2, rows, HALF), lambda g: (g, 0, 0, 0)),
        pl.BlockSpec((1, 2, rows, HALF), lambda g: (4 * groups, 0, 0, 0)),
    ]
    return pl.pallas_call(
        middle_kernel,
        grid=(groups,),
        in_specs=[smem()] + specs + near * 2 + [state(groups, rows)[1]] * 4,
        **split(
            [sums(bands, rows, columns)] + [state(groups, rows)] * 3 + [factor_state(groups, rows)]
        ),
        scratch_shapes=[
            plane_scratch(2, 2, 3, 2, rows=rows),
            plane_scratch(2, 2, rows=rows),
            plane_scratch(2, 2, 2, 2, rows=rows),
            plane_scratch(2, 2, 2, rows=rows),
            plane_scratch(2, 2, 2, rows=rows),
            plane_scratch(2, 4, rows=rows),
            plane_scratch(2, rows=rows),
            plane_scratch(2, 2, 2, 2, rows=rows),
            plane_scratch(2, 2, 2, rows=rows),
            plane_scratch(1, 2, 2, rows=rows),
        ],
        compiler_params=compiler_params(40),
        cost_estimate=light(100_000_000),
        name="middle",
    )(
        freq, *operands, from_core, from_core, from_chip, from_chip,
        *[in_hbm(array) for array in held],
    )


def outer(freq, from_core, from_chip, held, bands, rows, columns):
    groups = from_core.shape[1]
    return pl.pallas_call(
        outer_kernel,
        grid=(groups,),
        in_specs=[smem()] + [sent(groups, rows)[1]] * 2 + [state(groups, rows)[1]] * 3
        + [factor_state(groups, rows)[1]],
        **split(halves(bands, rows, columns) * 2),
        scratch_shapes=[
            plane_scratch(2, 2, 4, rows=rows),
            plane_scratch(2, 2, 2, rows=rows),
            plane_scratch(2, 2, 2, 2, rows=rows),
            plane_scratch(2, 2, 2, rows=rows),
        ],
        compiler_params=compiler_params(32),
        cost_estimate=light(),
        name="outer",
    )(freq, from_core, from_chip, *[in_hbm(array) for array in held])


def route(coverage, own_index):
    lists = coverage[0]
    owner, local = lists // TPD, lists % TPD
    position = jnp.arange(lists.shape[1], dtype=jnp.int32)
    same_owner = owner[:, :, None] == owner[:, None, :]
    earlier = position[None, :] < position[:, None]
    rank = jnp.sum((same_owner & earlier[None]).astype(jnp.int32), axis=2)
    slots = jnp.arange(CAP, dtype=jnp.int32)
    hit = (owner == own_index)[:, :, None] & (rank[:, :, None] == slots[None, None, :])
    pick = jnp.sum(jnp.where(hit, local[:, :, None], 0), axis=1).reshape(-1)
    own_slots = owner * CAP + rank
    return pick, lax.dynamic_index_in_dim(own_slots, own_index, 0, keepdims=False)


def body(sources, slowness, freq_index, coverage):
    groups, _, layers, rows, columns = sources.shape
    bands, members = lax.axis_size("freq"), lax.axis_size("sub")
    own_index = lax.axis_index("sub")
    cores = [(i, i ^ 1) for i in range(members)]
    chips = [(i, i + step) for i in range(members) for step in (2 * (i % 2) - 1,) if 0 <= i + step < members]
    def exchange(to_chip, to_core):
        return lax.ppermute(to_chip, "sub", chips), lax.ppermute(to_core, "sub", cores)

    near = first_edges(freq_index, sources, slowness)
    near_chip, near_core = exchange(*near)
    *edges, second = later_edges(freq_index, sources, slowness, near[0])
    far_chip, far_core = exchange(*edges)
    pick, slots = route(coverage, own_index)

    def spread(chunk):
        return lax.all_to_all(chunk, "freq", split_axis=0, concat_axis=0, tiled=True)

    def spread_next(chunk):
        if chunks:
            chunks[-1], chunk = lax.optimization_barrier((chunks[-1], chunk))
        chunks.append(spread(chunk))

    chunks = []
    chunk, *held = inner(freq_index, sources, slowness, second, bands)
    chunk, near_chip, near_core = lax.optimization_barrier((chunk, near_chip, near_core))
    spread_next(chunk)
    held = [second] + held
    chunk, *held = middle(freq_index, sources, slowness, near_core, near_chip, held, bands)
    spread_next(chunk)
    ends = outer(freq_index, far_core, far_chip, held, bands, rows, columns)
    neighbours = [(i, i ^ 1) for i in range(bands)]
    opposites = [(i, i ^ 2) for i in range(bands)]
    got = [lax.ppermute(send, "freq", neighbours) for send in ends[1::2]]
    chunks[-1], got[0] = lax.optimization_barrier((chunks[-1], got[0]))
    for keep, part in zip(ends[::2], got):
        send, own = fold(keep, part)
        chunks += [own, lax.ppermute(send, "freq", opposites)]
    depth = rows // bands
    precond, outgoing = pl.pallas_call(
        precond_kernel,
        in_specs=[smem()] + [vmem()] * len(chunks),
        out_specs=[vmem()] * 2,
        out_shape=[
            jax.ShapeDtypeStruct((layers, depth, columns), jnp.float32),
            jax.ShapeDtypeStruct((members * CAP, depth, columns), jnp.float32),
        ],
        compiler_params=compiler_params(12),
        name="precond",
    )(pick, *chunks)
    incoming = lax.all_to_all(outgoing, "sub", split_axis=0, concat_axis=0, tiled=True)
    delivered = pl.pallas_call(
        deliver_kernel,
        in_specs=[smem(), vmem()],
        out_specs=vmem(),
        out_shape=jax.ShapeDtypeStruct((1, 1, coverage.shape[2], depth, columns), jnp.float32),
        compiler_params=compiler_params(12),
        name="deliver",
    )(slots, incoming)
    return precond, delivered


def solution(mesh):
    placed = (
        P("freq", None, "sub", None, None),
        P("sub", None, None),
        P("freq"),
        P("freq", None, None),
    )
    return jax.shard_map(
        body,
        mesh=mesh,
        in_specs=placed,
        out_specs=(P("sub", "freq", None), P("freq", "sub", None, None, None)),
        check_vma=False,
    )
```

```python
import functools

import jax
import jax.numpy as jnp
from jax import lax
from jax.experimental import pallas as pl
from jax.experimental.pallas import tpu as pltpu
from jax.sharding import PartitionSpec as P

TPD = 8
CAP = 2
HALF = 128


def masks():
    lane = lax.broadcasted_iota(jnp.int32, (8, HALF), 1)
    row = lax.broadcasted_iota(jnp.int32, (8, HALF), 0)
    return lane == 0, lane == HALF - 1, row == 0, row == 7


def turn(real, imag, coef_real, coef_imag):
    return real * coef_real + imag * coef_imag, imag * coef_real - real * coef_imag


def coefficients(store, slow, scale, factor, nk):
    for k in range(nk):
        for h in range(2):
            sigma = scale * slow(h, k)
            diag = 0.875 - sigma
            inverse = factor / (diag * diag + sigma * sigma)
            store(0, h, k, diag * inverse)
            store(1, h, k, sigma * inverse)


def relax(store, force, near, coef, marks, nk, base=None):
    lane_first, lane_last, row_first, row_last = marks

    def across(c, h, k):
        before, middle, after = [None if layer is None else layer(c, h, k) for layer in near]
        parts = [part for part in (before, after) if part is not None]
        if middle is not None:
            parts.append(middle + middle)
        return functools.reduce(lambda total, part: total + part, parts)

    both = [(c, h) for c in range(2) for h in range(2)]
    top = {at: across(*at, 0) for at in both}
    bottom = {at: across(*at, nk - 1) for at in both}
    here = top
    pair = {at: jnp.where(row_first, 0.0, pltpu.roll(bottom[at], 1, 0)) + top[at] for at in both}
    for k in range(nk):
        if k < nk - 2:
            following = {at: across(*at, k + 1) for at in both}
        elif k == nk - 2:
            following = bottom
        else:
            following = {at: jnp.where(row_last, 0.0, pltpu.roll(top[at], 7, 0)) for at in both}
        terms = []
        for c in range(2):
            depth = []
            for h in range(2):
                later = here[c, h] + following[c, h]
                depth.append(pair[c, h] + later)
                pair[c, h] = later
            left, right = depth
            left_up, right_up = pltpu.roll(left, HALF - 1, 1), pltpu.roll(right, HALF - 1, 1)
            left_down, right_down = pltpu.roll(left, 1, 1), pltpu.roll(right, 1, 1)
            left_sides = jnp.where(lane_last, right_up, left_up) + jnp.where(lane_first, 0.0, left_down)
            right_sides = jnp.where(lane_last, 0.0, right_up) + jnp.where(
                lane_first, left_down, right_down
            )
            for h, (middle, ends) in enumerate(((left, left_sides), (right, right_sides))):
                total = ends + (middle + middle)
                if near[1] is not None:
                    total = total - 8.0 * near[1](c, h, k)
                terms.append(total if force is None else force(c, h, k) + total)
        here = following
        for h in range(2):
            planes = turn(terms[h], terms[2 + h], coef(0, h, k), coef(1, h, k))
            for c in range(2):
                store(c, h, k, planes[c] if base is None else base(c, h, k) + planes[c])


def piece_of(ref, lead):
    return lambda c, h, k: ref[lead + (c, h, pl.ds(8 * k, 8), slice(None))]


def row_piece(refs, lead, offset, tail, nk):
    return lambda c, h, k: refs[h][
        lead + (offset + c,) + tail + (pl.ds(k, 8, stride=nk), slice(None))
    ]


def store_to(*places):
    def store(c, h, k, piece):
        for ref, lead in places:
            ref[lead + (c, h, pl.ds(8 * k, 8), slice(None))] = piece

    return store


def start_layer(store, force, coef, nk):
    for k in range(nk):
        for h in range(2):
            planes = turn(force(0, h, k), force(1, h, k), coef(0, h, k), coef(1, h, k))
            for c in range(2):
                store(c, h, k, planes[c])


def products(last, acc, place, weight, first, nk):
    for side in range(2):
        forward, adjoint = [piece_of(last, (side, pair)) for pair in range(2)]
        for h in range(2):
            for k in range(nk):
                fr, fi = forward(0, h, k), forward(1, h, k)
                ar, ai = adjoint(0, h, k), adjoint(1, h, k)
                terms = (weight * (fr * ar - fi * ai), weight * (fr * fr + fi * fi))
                for number, term in enumerate(terms):
                    at = (place, number, side, h, pl.ds(k, 8, stride=nk), slice(None))
                    acc[at] = jnp.where(first, term, acc[at] + term)


def write_out(out, acc, offset):
    bands, _, _, _, depth, _ = out.shape
    for band in range(bands):
        for place in range(acc.shape[0]):
            for number in range(2):
                for side in range(2):
                    for h in range(2):
                        out[band, offset + place, number, side, :, pl.ds(h * HALF, HALF)] = acc[
                            place, number, side, h, pl.ds(band * depth, depth), :
                        ]


def scale_of(freq, group):
    weight = 1.0 + freq[group].astype(jnp.float32) / 16.0
    return weight, 0.12 * weight


def parity():
    return lax.axis_index("sub") % 2


def paired(side):
    index = lax.axis_index("sub")
    there = index > 0 if side == 0 else index < lax.axis_size("sub") - 1
    return jnp.where(there, 1.0 / 64.0, 0.0)


def first_kernel(indices, sources, slowness, to_chip, to_core, raw, slow, coef, freq, sems, sem):
    groups, _, layers, rows = sources.shape[:4]
    nk = rows // 8
    places = (parity() * (layers - 1), (1 - parity()) * (layers - 1))
    copies = []
    for side, own in enumerate(places):
        for h in range(2):
            lanes = pl.ds(h * HALF, HALF)
            pairs = ((slowness.at[own, :, lanes], slow), (sources.at[:, :, own, :, lanes], raw))
            for number, (ref, held) in enumerate(pairs):
                copies.append(
                    pltpu.make_async_copy(ref, held.at[side, h], sems.at[side, h, number])
                )
    load = pltpu.make_async_copy(indices, freq, sem)
    load.start()
    for copy in copies:
        copy.start()
    load.wait()
    for side, out in enumerate((to_chip, to_core)):
        for copy in copies[4 * side : 4 * side + 4]:
            copy.wait()

        def sigma(h, k):
            return slow[side, h, pl.ds(k, 8, stride=nk), :]

        for h in range(2):
            for k in range(nk):
                out[4 * groups, h, pl.ds(8 * k, 8), :] = sigma(h, k)
        for group in range(groups):
            scale = scale_of(freq, group)[1]
            coefficients(store_to((coef, (side, group))), sigma, scale, 1.0 / 64.0, nk)
            for pair in range(2):
                start_layer(
                    store_from(out, (), 4 * group + 2 * pair),
                    row_piece((raw.at[side, 0], raw.at[side, 1]), (group,), 2 * pair, (), nk),
                    piece_of(coef, (side, group)),
                    nk,
                )


def store_from(ref, lead, offset):
    def store(c, h, k, piece):
        ref[lead + (offset + c, h, pl.ds(8 * k, 8), slice(None))] = piece

    return store


def sent_piece(ref, lead, offset):
    return lambda c, h, k: ref[lead + (offset + c, h, pl.ds(8 * k, 8), slice(None))]


def edge_kernel(freq, _, *refs):
    sides = []
    for side in range(2):
        part = refs[12 * side : 12 * side + 12]
        sides.append([[part[at + 2 * n : at + 2 * n + 2] for n in range(3)] for at in (0, 6)])
    far_chip, far_core, second, coef, one, fields = refs[24:]
    group = pl.program_id(0)
    rows = sides[0][1][0][0].shape[-2]
    nk = rows // 8
    marks = masks()
    scale = scale_of(freq, group)[1]
    chains = [(side, pair) for side in range(2) for pair in range(2)]

    def force(side, pair, at):
        return row_piece(sides[side][0][at], (0,), 2 * pair, (0,), nk)

    for side in range(2):
        for at in range(3):
            slows = sides[side][1][at]
            coefficients(
                store_to((coef, (side, at))),
                lambda h, k, slows=slows: slows[h][0, pl.ds(k, 8, stride=nk), :],
                scale,
                1.0 / 64.0,
                nk,
            )
            for pair in range(2):
                start_layer(
                    store_to((one, (side, pair, at))),
                    force(side, pair, at),
                    piece_of(coef, (side, at)),
                    nk,
                )
    for at in range(2):
        for side, pair in chains:
            near = [piece_of(one, (side, pair, n)) if n >= 0 else None for n in (at - 1, at, at + 1)]
            target = (fields, (side, 0, pair)) if at == 0 else (second, (0, pair, side))
            relax(
                store_to(target), force(side, pair, at), near, piece_of(coef, (side, at)), marks, nk
            )
    for side, pair in chains:
        near = [None, piece_of(fields, (side, 0, pair)), piece_of(second, (0, pair, side))]
        relax(
            store_to((fields, (side, 1, pair))),
            force(side, pair, 0),
            near,
            piece_of(coef, (side, 0)),
            marks,
            nk,
        )
    for out, side in ((far_chip, parity()), (far_core, 1 - parity())):
        for level in range(2):
            for pair in range(2):
                for c in range(2):
                    out[level, 0, 2 * pair + c] = fields[side, level, pair, c]


def inner_kernel(
    freq, src_l, src_r, slow_l, slow_r, second,
    out, two_next, three_near, three_far, coef, one, force, two, three, last, acc,
):
    group = pl.program_id(0)
    groups = pl.num_programs(0)
    layers, rows = src_l.shape[2], src_l.shape[3]
    nk = rows // 8
    marks = masks()
    weight, scale = scale_of(freq, group)
    weight = weight * 4096.0
    sources, slows = (src_l, src_r), (slow_l, slow_r)
    chains = [(side, pair) for side in range(2) for pair in range(2)]

    @pl.loop(0, layers - 2)
    def _(place):
        layer = place + 1
        coefficients(
            store_to((coef, (layer,))),
            lambda h, k: slows[h][layer, pl.ds(k, 8, stride=nk), :],
            scale,
            1.0 / 64.0,
            nk,
        )
        for pair in range(2):
            rows_of = row_piece(sources, (0,), 2 * pair, (layer,), nk)
            keep = store_to((force, (pair, layer)))
            for c in range(2):
                for h in range(2):
                    for k in range(nk):
                        keep(c, h, k, rows_of(c, h, k))
            start_layer(store_to((one, (pair, layer))), rows_of, piece_of(coef, (layer,)), nk)

    def copy_plane(keep, given):
        for c in range(2):
            for h in range(2):
                for k in range(nk):
                    keep(c, h, k, given(c, h, k))

    def layer_at(side, at):
        return at if side == 0 else layers - 1 - at

    def step(target, pair, layer, ref, skip):
        near = [piece_of(ref, (pair, layer + shift - skip)) for shift in (-1, 0, 1)]
        relax(
            store_to(target),
            piece_of(force, (pair, layer)),
            near,
            piece_of(coef, (layer,)),
            marks,
            nk,
        )

    for side, pair in chains:
        copy_plane(
            store_to((two, (pair, layer_at(side, 1)))), piece_of(second, (0, pair, side))
        )

    @pl.loop(0, (layers - 4) // 2)
    def _(turn_at):
        for offset in range(2):
            for pair in range(2):
                layer = 2 + 2 * turn_at + offset
                step((two, (pair, layer)), pair, layer, one, 0)

    @pl.loop(0, (layers - 4) // 2)
    def _(turn_at):
        for offset in range(2):
            for pair in range(2):
                layer = 2 + 2 * turn_at + offset
                step((three, (pair, layer - 2)), pair, layer, two, 0)

    for side, pair in chains:
        step((last, (side, pair)), pair, layers // 2 - 1 + side, three, 2)
        for keep, ref, at in (
            (two_next, two, layer_at(side, 2)),
            (three_near, three, layer_at(side, 2) - 2),
            (three_far, three, layer_at(side, 3) - 2),
        ):
            copy_plane(store_to((keep, (0, pair, side))), piece_of(ref, (pair, at)))
    products(last, acc, 0, weight, group == 0, nk)

    @pl.when(group == groups - 1)
    def _():
        write_out(out, acc, 0)


def middle_kernel(freq, *refs):
    sides = []
    for side in range(2):
        part = refs[12 * side : 12 * side + 12]
        sides.append([[part[at + 2 * n : at + 2 * n + 2] for n in range(3)] for at in (0, 6)])
    core_field, core_slow, chip_field, chip_slow, second, two_next, three_near, three_far = refs[24:32]
    out, base_three, base_next, base_four, factors = refs[32:37]
    force, beyond, one, first_two, first_three, halo, halo_slow, change, last, acc = refs[37:]
    group = pl.program_id(0)
    groups = pl.num_programs(0)
    rows = second.shape[-2]
    nk = rows // 8
    marks = masks()
    weight, scale = scale_of(freq, group)
    weight = weight * 4096.0
    chains = [(side, pair) for side in range(2) for pair in range(2)]
    to_chip, to_core = parity(), 1 - parity()
    halo[to_core] = core_field[...]
    halo[to_chip] = chip_field[...]
    halo_slow[to_core] = core_slow[0]
    halo_slow[to_chip] = chip_slow[0]

    for side in range(2):
        coefficients(
            store_to((beyond, (side,))),
            lambda h, k, side=side: halo_slow[side, h, pl.ds(8 * k, 8), :],
            scale,
            paired(side),
            nk,
        )
        for at in range(3):
            slows = sides[side][1][at]
            coefficients(
                store_to((factors, (0, side, at))),
                lambda h, k, slows=slows: slows[h][0, pl.ds(k, 8, stride=nk), :],
                scale,
                1.0 / 64.0,
                nk,
            )
            for pair in range(2):
                rows_of = row_piece(sides[side][0][at], (0,), 2 * pair, (0,), nk)
                keep = store_to((force, (side, pair, at)))
                for c in range(2):
                    for h in range(2):
                        for k in range(nk):
                            keep(c, h, k, rows_of(c, h, k))
                if at < 2:
                    start_layer(
                        store_to((one, (side, pair, at))),
                        rows_of,
                        piece_of(factors, (0, side, at)),
                        nk,
                    )

    def step(target, side, pair, at, near):
        relax(
            store_to(target),
            piece_of(force, (side, pair, at)),
            near,
            piece_of(factors, (0, side, at)),
            marks,
            nk,
        )

    def held(ref, side, pair):
        return piece_of(ref, (0, pair, side))

    for side, pair in chains:
        near = [sent_piece(halo, (side,), 2 * pair)]
        near += [piece_of(one, (side, pair, at)) for at in range(2)]
        step((first_two, (side, pair)), side, pair, 0, near)
    for side, pair in chains:
        near = [None, None, piece_of(one, (side, pair, 0))]
        relax(store_to((change, (0, side, pair))), None, near, piece_of(beyond, (side,)), marks, nk)
    for side, pair in chains:
        near = [
            piece_of(first_two, (side, pair)),
            held(second, side, pair),
            held(two_next, side, pair),
        ]
        step((first_three, (side, pair)), side, pair, 1, near)
    for side, pair in chains:
        near = [
            None,
            piece_of(change, (0, side, pair)),
            piece_of(first_two, (side, pair)),
        ]
        relax(store_to((change, (1, side, pair))), None, near, piece_of(beyond, (side,)), marks, nk)
    for side, pair in chains:
        three = piece_of(first_three, (side, pair))
        near = [three, held(three_near, side, pair), held(three_far, side, pair)]
        step((last, (side, pair)), side, pair, 2, near)
    products(last, acc, 0, weight, group == 0, nk)
    for side, pair in chains:
        three = piece_of(first_three, (side, pair))
        twos = [piece_of(first_two, (side, pair)), held(second, side, pair)]
        changes = [piece_of(change, (number, side, pair)) for number in range(2)]
        for target, at, near in (
            (base_three, 0, [changes[0], *twos]),
            (base_next, 1, [None, three, held(three_near, side, pair)]),
            (base_four, 0, [changes[1], None, three]),
        ):
            step((target, (0, pair, side)), side, pair, at, near)

    @pl.when(group == groups - 1)
    def _():
        write_out(out, acc, 0)


def write_halves(keep, send, acc, place):
    depth = keep.shape[-2]
    odd = lax.axis_index("freq") % 2
    for out, parity_of in ((keep, odd), (send, 1 - odd)):
        for high in range(2):
            start = pl.multiple_of((2 * high + parity_of) * depth, 8)
            for number in range(2):
                for side in range(2):
                    for h in range(2):
                        out[high, number, side, :, pl.ds(h * HALF, HALF)] = acc[
                            place, number, side, h, pl.ds(start, depth), :
                        ]


def outer_kernel(freq, core, chip, base_three, base_next, base_four, factors, *rest):
    outs, (sent_fields, fresh, last, acc) = rest[:4], rest[4:]
    group = pl.program_id(0)
    groups = pl.num_programs(0)
    rows = base_three.shape[-2]
    nk = rows // 8
    marks = masks()
    weight = scale_of(freq, group)[0] * 4096.0
    chains = [(side, pair) for side in range(2) for pair in range(2)]
    to_chip, to_core = parity(), 1 - parity()
    for number in range(2):
        sent_fields[to_core, number] = core[number, 0]
        sent_fields[to_chip, number] = chip[number, 0]

    def step(target, base, side, pair, at, near):
        relax(
            store_to(target),
            None,
            near,
            piece_of(factors, (0, side, at)),
            marks,
            nk,
            base=piece_of(base, (0, pair, side)),
        )

    for side, pair in chains:
        near = [sent_piece(sent_fields, (side, 0), 2 * pair), None, None]
        step((fresh, (side, pair)), base_three, side, pair, 0, near)
    for side, pair in chains:
        near = [piece_of(fresh, (side, pair)), None, None]
        step((last, (0, side, pair)), base_next, side, pair, 1, near)
    for side, pair in chains:
        near = [sent_piece(sent_fields, (side, 1), 2 * pair), piece_of(fresh, (side, pair)), None]
        step((last, (1, side, pair)), base_four, side, pair, 0, near)
    for place in range(2):
        products(last.at[place], acc, place, weight, group == 0, nk)

    @pl.when(group == groups - 1)
    def _():
        for place in range(2):
            write_halves(*outs[2 * place : 2 * place + 2], acc, place)


def fold_kernel(keep, got, send, own):
    high = lax.axis_index("freq") // 2
    send[...] = keep[1 - high] + got[1 - high]
    own[...] = keep[high] + got[high]


def precond_kernel(pick, *refs):
    chunks, (precond, outgoing) = refs[:-2], refs[-2:]
    layers = precond.shape[0]
    wide = [chunk for chunk in chunks if len(chunk.shape) == 6]
    terms = [
        [functools.partial(lambda chunk, other, at: chunk[other, 0, at[0], at[1]], chunk, other)
         for other in range(chunk.shape[0])]
        for chunk in wide
    ]
    flat = chunks[len(wide) :]
    for place in range(0, len(flat), 2):
        terms.append([lambda at, ref=ref: ref[at[0], at[1]] for ref in flat[place : place + 2]])
    for step, parts in enumerate(terms):
        for side in range(2):
            layer = layers // 2 - 1 - step if side == 0 else layers // 2 + step
            grad, illum = [
                functools.reduce(lambda a, b: a + b, [part((number, side)) for part in parts])
                for number in range(2)
            ]
            precond[layer] = grad / jnp.sqrt(illum + 1.0)

    @pl.loop(0, outgoing.shape[0])
    def _(slot):
        outgoing[slot] = precond[pick[slot]]


def deliver_kernel(slots, incoming, out):
    @pl.loop(0, out.shape[2])
    def _(number):
        out[0, 0, number] = incoming[slots[number]]


def smem():
    return pl.BlockSpec(memory_space=pltpu.SMEM)


def vmem():
    return pl.BlockSpec(memory_space=pltpu.VMEM)


def plane_scratch(*lead, rows):
    return pltpu.VMEM(lead + (2, rows, HALF), jnp.float32)


def compiler_params(mebibytes):
    return pltpu.CompilerParams(vmem_limit_bytes=mebibytes * 1024 * 1024)


def light(size=1000):
    return pl.CostEstimate(flops=1000, bytes_accessed=size, transcendentals=0)


def in_hbm(array):
    return pltpu.with_memory_space_constraint(array, pltpu.HBM)


def hbm(*shape):
    return pltpu.HBM(shape, jnp.float32)


def state(groups, rows):
    return (
        hbm(groups, 2, 2, 2, 2, rows, HALF),
        pl.BlockSpec((1, 2, 2, 2, 2, rows, HALF), lambda g: (g, 0, 0, 0, 0, 0, 0)),
    )


def sent(groups, rows):
    return (
        hbm(2, groups, 4, 2, rows, HALF),
        pl.BlockSpec((2, 1, 4, 2, rows, HALF), lambda g: (0, g, 0, 0, 0, 0)),
    )


def factor_state(groups, rows):
    return (
        hbm(groups, 2, 3, 2, 2, rows, HALF),
        pl.BlockSpec((1, 2, 3, 2, 2, rows, HALF), lambda g: (g, 0, 0, 0, 0, 0, 0)),
    )


def sums(bands, rows, columns, steps=1):
    shape = (bands, steps, 2, 2, rows // bands, columns)
    return hbm(*shape), pl.BlockSpec(shape, lambda g: (0,) * 6)


def halves(bands, rows, columns):
    shape = (bands // 2, 2, 2, rows // bands, columns)
    spec = pl.BlockSpec(shape, lambda g: (0,) * 5)
    return [(jax.ShapeDtypeStruct(shape, jnp.float32), spec)] * 2


def fold(keep, got):
    shape = keep.shape[1:]
    return pl.pallas_call(
        fold_kernel,
        in_specs=[vmem()] * 2,
        out_specs=[vmem()] * 2,
        out_shape=[jax.ShapeDtypeStruct(shape, jnp.float32)] * 2,
        compiler_params=compiler_params(8),
        cost_estimate=light(),
        name="fold",
    )(keep, got)


def split(pairs):
    return dict(out_shape=[p[0] for p in pairs], out_specs=[p[1] for p in pairs])


def layer_specs(sources, own):
    rows = sources.shape[3]
    return (
        [pl.BlockSpec((1, 4, 1, rows, HALF), lambda g, h=h: (g, 0, own, 0, h)) for h in range(2)],
        [pl.BlockSpec((1, rows, HALF), lambda g, h=h: (own, 0, h)) for h in range(2)],
    )


def first_edges(freq, sources, slowness):
    groups, _, _, rows, _ = sources.shape
    anywhere = pl.BlockSpec(memory_space=pl.ANY)
    return pl.pallas_call(
        first_kernel,
        in_specs=[anywhere] * 3,
        out_specs=[vmem()] * 2,
        out_shape=[jax.ShapeDtypeStruct((4 * groups + 1, 2, rows, HALF), jnp.float32)] * 2,
        scratch_shapes=[
            pltpu.VMEM((2, 2, groups, 4, rows, HALF), jnp.float32),
            plane_scratch(2, rows=rows),
            plane_scratch(2, groups, 2, rows=rows),
            pltpu.SMEM((groups,), jnp.int32),
            pltpu.SemaphoreType.DMA((2, 2, 2)),
            pltpu.SemaphoreType.DMA,
        ],
        compiler_params=compiler_params(8),
        cost_estimate=light(),
        name="first",
    )(in_hbm(freq), in_hbm(sources), in_hbm(slowness))


def edge_layers(sources, slowness):
    layers = sources.shape[2]
    sources, slowness = in_hbm(sources), in_hbm(slowness)
    operands, specs = [], []
    for side in range(2):
        parts = [layer_specs(sources, at if side == 0 else layers - 1 - at) for at in range(3)]
        for what, array in enumerate((sources, slowness)):
            for part in parts:
                operands += [array] * 2
                specs += part[what]
    return operands, specs


def later_edges(freq, sources, slowness, first):
    groups, _, _, rows, _ = sources.shape
    operands, specs = edge_layers(sources, slowness)
    operands = [freq, first] + operands
    specs = [smem(), pl.BlockSpec(memory_space=pl.ANY)] + specs
    return pl.pallas_call(
        edge_kernel,
        grid=(groups,),
        in_specs=specs,
        **split([sent(groups, rows)] * 2 + [state(groups, rows)]),
        scratch_shapes=[
            plane_scratch(2, 3, 2, rows=rows),
            plane_scratch(2, 2, 3, 2, rows=rows),
            plane_scratch(2, 2, 2, 2, rows=rows),
        ],
        compiler_params=compiler_params(32),
        cost_estimate=light(),
        name="edges",
    )(*operands)


def inner(freq, sources, slowness, second, bands):
    groups, _, layers, rows, columns = sources.shape
    half = [
        pl.BlockSpec((1, 4, layers, rows, HALF), lambda g, h=h: (g, 0, 0, 0, h)) for h in range(2)
    ]
    slow = [pl.BlockSpec((layers, rows, HALF), lambda g, h=h: (0, 0, h)) for h in range(2)]
    sources, slowness = in_hbm(sources), in_hbm(slowness)
    return pl.pallas_call(
        inner_kernel,
        grid=(groups,),
        in_specs=[smem()] + half + slow + [state(groups, rows)[1]],
        **split([sums(bands, rows, columns)] + [state(groups, rows)] * 3),
        scratch_shapes=[
            plane_scratch(layers, 2, rows=rows),
            plane_scratch(2, layers, 2, rows=rows),
            plane_scratch(2, layers, 2, rows=rows),
            plane_scratch(2, layers, 2, rows=rows),
            plane_scratch(2, layers - 4, 2, rows=rows),
            plane_scratch(2, 2, 2, rows=rows),
            plane_scratch(1, 2, 2, rows=rows),
        ],
        compiler_params=compiler_params(40),
        cost_estimate=light(),
        name="inner",
    )(freq, sources, sources, slowness, slowness, in_hbm(second))


def middle(freq, sources, slowness, from_core, from_chip, held, bands):
    groups, _, _, rows, columns = sources.shape
    operands, specs = edge_layers(sources, slowness)
    near = [
        pl.BlockSpec((4, 2, rows, HALF), lambda g: (g, 0, 0, 0)),
        pl.BlockSpec((1, 2, rows, HALF), lambda g: (4 * groups, 0, 0, 0)),
    ]
    return pl.pallas_call(
        middle_kernel,
        grid=(groups,),
        in_specs=[smem()] + specs + near * 2 + [state(groups, rows)[1]] * 4,
        **split(
            [sums(bands, rows, columns)] + [state(groups, rows)] * 3 + [factor_state(groups, rows)]
        ),
        scratch_shapes=[
            plane_scratch(2, 2, 3, 2, rows=rows),
            plane_scratch(2, 2, rows=rows),
            plane_scratch(2, 2, 2, 2, rows=rows),
            plane_scratch(2, 2, 2, rows=rows),
            plane_scratch(2, 2, 2, rows=rows),
            plane_scratch(2, 4, rows=rows),
            plane_scratch(2, rows=rows),
            plane_scratch(2, 2, 2, 2, rows=rows),
            plane_scratch(2, 2, 2, rows=rows),
            plane_scratch(1, 2, 2, rows=rows),
        ],
        compiler_params=compiler_params(40),
        cost_estimate=light(100_000_000),
        name="middle",
    )(
        freq, *operands, from_core, from_core, from_chip, from_chip,
        *[in_hbm(array) for array in held],
    )


def outer(freq, from_core, from_chip, held, bands, rows, columns):
    groups = from_core.shape[1]
    return pl.pallas_call(
        outer_kernel,
        grid=(groups,),
        in_specs=[smem()] + [sent(groups, rows)[1]] * 2 + [state(groups, rows)[1]] * 3
        + [factor_state(groups, rows)[1]],
        **split(halves(bands, rows, columns) * 2),
        scratch_shapes=[
            plane_scratch(2, 2, 4, rows=rows),
            plane_scratch(2, 2, 2, rows=rows),
            plane_scratch(2, 2, 2, 2, rows=rows),
            plane_scratch(2, 2, 2, rows=rows),
        ],
        compiler_params=compiler_params(32),
        cost_estimate=light(),
        name="outer",
    )(freq, from_core, from_chip, *[in_hbm(array) for array in held])


def route(coverage, own_index):
    lists = coverage[0]
    owner, local = lists // TPD, lists % TPD
    position = jnp.arange(lists.shape[1], dtype=jnp.int32)
    same_owner = owner[:, :, None] == owner[:, None, :]
    earlier = position[None, :] < position[:, None]
    rank = jnp.sum((same_owner & earlier[None]).astype(jnp.int32), axis=2)
    slots = jnp.arange(CAP, dtype=jnp.int32)
    hit = (owner == own_index)[:, :, None] & (rank[:, :, None] == slots[None, None, :])
    pick = jnp.sum(jnp.where(hit, local[:, :, None], 0), axis=1).reshape(-1)
    own_slots = owner * CAP + rank
    return pick, lax.dynamic_index_in_dim(own_slots, own_index, 0, keepdims=False)


def body(sources, slowness, freq_index, coverage):
    groups, _, layers, rows, columns = sources.shape
    bands, members = lax.axis_size("freq"), lax.axis_size("sub")
    own_index = lax.axis_index("sub")
    cores = [(i, i ^ 1) for i in range(members)]
    chips = [(i, i + step) for i in range(members) for step in (2 * (i % 2) - 1,) if 0 <= i + step < members]
    def exchange(to_chip, to_core):
        return lax.ppermute(to_chip, "sub", chips), lax.ppermute(to_core, "sub", cores)

    near = first_edges(freq_index, sources, slowness)
    near_chip, near_core = exchange(*near)
    *edges, second = later_edges(freq_index, sources, slowness, near[0])
    far_chip, far_core = exchange(*edges)
    pick, slots = route(coverage, own_index)

    def spread(chunk):
        return lax.all_to_all(chunk, "freq", split_axis=0, concat_axis=0, tiled=True)

    def spread_next(chunk):
        if chunks:
            chunks[-1], chunk = lax.optimization_barrier((chunks[-1], chunk))
        chunks.append(spread(chunk))

    chunks = []
    chunk, *held = inner(freq_index, sources, slowness, second, bands)
    chunk, near_chip, near_core = lax.optimization_barrier((chunk, near_chip, near_core))
    spread_next(chunk)
    held = [second] + held
    chunk, *held = middle(freq_index, sources, slowness, near_core, near_chip, held, bands)
    spread_next(chunk)
    ends = outer(freq_index, far_core, far_chip, held, bands, rows, columns)
    neighbours = [(i, i ^ 1) for i in range(bands)]
    opposites = [(i, i ^ 2) for i in range(bands)]
    got = [lax.ppermute(send, "freq", neighbours) for send in ends[1::2]]
    chunks[-1], got[0] = lax.optimization_barrier((chunks[-1], got[0]))
    for keep, part in zip(ends[::2], got):
        send, own = fold(keep, part)
        chunks += [own, lax.ppermute(send, "freq", opposites)]
    depth = rows // bands
    precond, outgoing = pl.pallas_call(
        precond_kernel,
        in_specs=[smem()] + [vmem()] * len(chunks),
        out_specs=[vmem()] * 2,
        out_shape=[
            jax.ShapeDtypeStruct((layers, depth, columns), jnp.float32),
            jax.ShapeDtypeStruct((members * CAP, depth, columns), jnp.float32),
        ],
        compiler_params=compiler_params(12),
        name="precond",
    )(pick, *chunks)
    incoming = lax.all_to_all(outgoing, "sub", split_axis=0, concat_axis=0, tiled=True)
    delivered = pl.pallas_call(
        deliver_kernel,
        in_specs=[smem(), vmem()],
        out_specs=vmem(),
        out_shape=jax.ShapeDtypeStruct((1, 1, coverage.shape[2], depth, columns), jnp.float32),
        compiler_params=compiler_params(12),
        name="deliver",
    )(slots, incoming)
    return precond, delivered


def solution(mesh):
    placed = (
        P("freq", None, "sub", None, None),
        P("sub", None, None),
        P("freq"),
        P("freq", None, None),
    )
    return jax.shard_map(
        body,
        mesh=mesh,
        in_specs=placed,
        out_specs=(P("sub", "freq", None), P("freq", "sub", None, None, None)),
        check_vma=False,
    )
```
